128 devices in a mesh: leaf: 128 (over z, y, x, core).
Axes of the slice: x: 4, y: 4, z: 4, core: 2. Of those that a mesh axis runs over, the one named last changes fastest.
Arguments:
- points: float32 [16, 524288], P(None, 'leaf'), may hold values from -6 to 6
- charges: float32 [16, 524288], P(None, 'leaf'), may hold values from -1.2 to 1.2
- leaf_basis: float32 [64, 524288], P(None, 'leaf'), may hold values from -0.5 to 0.5
- local_transfer: float32 [7936, 4096], P('leaf'), may hold values from -0.625 to 0.625
- local_anchors: float32 [8064, 1024], P('leaf'), may hold values from -6 to 6
- local_lists: int32 [8064, 8], P('leaf'), may hold values from -1 to 4095, as said below
- near_blocks: int32 [4096, 8], P('leaf'), may hold values from -1 to 4095, as said below
- top_transfer: float32 [254, 4096], replicated, may hold values from -0.625 to 0.625
- top_anchors: float32 [127, 1024], replicated, may hold values from -6 to 6
- top_lists: int32 [127, 8], replicated, may hold values from -1 to 63, as said below
Outputs:
- potential: float32 [16, 524288], P(None, 'leaf')
The draws below stay inside these ranges and needn't reach their ends.
Inputs may be any that keep to these rules, and one draw needn't show every extreme that they name: `near_blocks`: entry 0 of row t is t itself; the other entries of a row are distinct leaves u != t with |u - t| <= 16, or -1 for no block. `local_lists`: the entries of a row are distinct; each is -1 (none) or a cluster p of the row's level with 2 <= |p - c| <= 6, where c is the row's cluster. `top_lists`: the entries of a row are distinct; each is -1 (none) or a cluster p of the row's level with 2 <= |p - c| <= 6, where c is the row's cluster.
All inputs are finite; a program needn't handle non-finite values.
Results may differ from the reference program's by a relative error of at most 0.0003.
Values sent between devices are 32-bit elements; how exact they have to be, the bound alone decides.
No kernel may reach another device: no remote copies, remote signals or barrier semaphores. Data moves between devices by JAX's collectives and lax.ppermute only.
A program may use at most 128 MiB of HBM per device.

```python
import jax
import jax.numpy as jnp
from jax import lax

DIM = 16
RHS = 16
LEAF = 128
RANK = 64
LEAVES_DEV = 32
NEAR = 8
NREACH = 16
ILIST = 8
REACH = 6
POINTS = 524288
LEAVES = 4096
LOCAL_CLUSTERS = 8064
LOCAL_CHILDREN = 7936
TOP_CLUSTERS = 127
TOP_CHILDREN = 254
N_LEAF = 128


def pick_offsets(key, row_count, candidates, chosen):
    number = candidates.shape[0]
    scores = jax.random.randint(key, (row_count, number), 0, 1 << 20) * number + jnp.arange(number, dtype=jnp.int32)[None, :]
    ranking = jnp.argsort(scores, axis=1, stable=True)[:, :chosen]
    return jnp.take(candidates, ranking)


def list_partners(key, clusters, totals):
    stretch = jnp.arange(2, REACH + 1, dtype=jnp.int32)
    candidates = jnp.concatenate([-stretch[::-1], stretch])
    offsets = pick_offsets(key, clusters.shape[0], candidates, ILIST)
    partner = clusters[:, None] + offsets
    inside = (partner >= 0) & (partner < totals[:, None])
    return jnp.where(inside, partner, -1).astype(jnp.int32)


def draw_local_lists(key, part):
    key = jax.random.fold_in(key, 11)
    per_device = 2 * LEAVES_DEV - 1
    devices = LOCAL_CLUSTERS // per_device
    local_depth = LEAVES_DEV.bit_length() - 1
    cluster_parts = []
    total_parts = []
    for height in range(local_depth + 1):
        number = LEAVES_DEV >> height
        device_ids = jnp.arange(devices, dtype=jnp.int32)[:, None]
        cluster_parts.append(device_ids * number + jnp.arange(number, dtype=jnp.int32)[None, :])
        total_parts.append(jnp.full((devices, number), devices * number, jnp.int32))
    clusters = jnp.concatenate(cluster_parts, axis=1).reshape(-1)
    totals = jnp.concatenate(total_parts, axis=1).reshape(-1)
    return list_partners(key, clusters, totals)


def draw_top_lists(key, part):
    key = jax.random.fold_in(key, 37)
    devices = TOP_CLUSTERS + 1
    top_depth = devices.bit_length() - 1
    cluster_parts = []
    total_parts = []
    for height in range(1, top_depth + 1):
        number = devices >> height
        cluster_parts.append(jnp.arange(number, dtype=jnp.int32))
        total_parts.append(jnp.full((number,), number, jnp.int32))
    clusters = jnp.concatenate(cluster_parts)
    totals = jnp.concatenate(total_parts)
    return list_partners(key, clusters, totals)


def draw_near_blocks(key, part):
    key = jax.random.fold_in(key, 23)
    stretch = jnp.arange(1, NREACH + 1, dtype=jnp.int32)
    candidates = jnp.concatenate([-stretch[::-1], stretch])
    offsets = pick_offsets(key, LEAVES, candidates, NEAR - 1)
    leaves = jnp.arange(LEAVES, dtype=jnp.int32)
    partner = leaves[:, None] + offsets
    inside = (partner >= 0) & (partner < LEAVES)
    partner = jnp.where(inside, partner, -1)
    return jnp.concatenate([leaves[:, None], partner], axis=1).astype(jnp.int32)


def steps_of(rng, dims, cuts, least, largest):
    def one(axis_at, shards_of):
        steps = jax.random.uniform(jax.random.fold_in(jax.random.fold_in(rng, 6), axis_at), (shards_of,), jnp.float32, least / len(cuts), largest / len(cuts))
        return jnp.repeat(jnp.exp(steps), dims[axis_at] // shards_of).reshape((-1,) + (1,) * (len(dims) - axis_at - 1))

    level = one(*cuts[0])
    for cut in cuts[1:]:
        level = level * one(*cut)
    return level


def gaussian(stream_key, shape, deviation, limit, cuts=(), kind=jnp.bfloat16):
    result = deviation * jax.random.normal(stream_key, shape, jnp.float32)
    if cuts:
        result = result * steps_of(stream_key, shape, cuts, -0.22, 0.18)
    return jnp.clip(result, -limit, limit).astype(kind)


def setup_inputs(seed: int = 0) -> dict:
    seeds = jax.random.split(jax.random.key(seed), 11)
    return {
        "points": gaussian(seeds[0], (DIM, POINTS), 1.0, 6.0, ((1, 128),), jnp.float32),
        "charges": gaussian(seeds[1], (RHS, POINTS), 0.2, 1.2, ((1, 128),), jnp.float32),
        "leaf_basis": gaussian(seeds[2], (RANK, POINTS), LEAF ** -0.5, 0.5, ((1, 128),), jnp.float32),
        "local_transfer": gaussian(seeds[3], (LOCAL_CHILDREN, RANK * RANK), (3 * RANK // 2) ** -0.5, 0.625, ((0, 128),), jnp.float32),
        "local_anchors": gaussian(seeds[4], (LOCAL_CLUSTERS, RANK * DIM), 1.0, 6.0, ((0, 128),), jnp.float32),
        "local_lists": draw_local_lists(jax.random.fold_in(seeds[10], 71), 0),
        "near_blocks": draw_near_blocks(jax.random.fold_in(seeds[10], 71), 0),
        "top_transfer": gaussian(seeds[7], (TOP_CHILDREN, RANK * RANK), (3 * RANK // 2) ** -0.5, 0.625, (), jnp.float32),
        "top_anchors": gaussian(seeds[8], (TOP_CLUSTERS, RANK * DIM), 1.0, 6.0, (), jnp.float32),
        "top_lists": draw_top_lists(jax.random.fold_in(seeds[10], 71), 0),
    }


length_scale = 3.0
highest = lax.Precision.HIGHEST

def matern_block(row_points, column_points):
    cross = jnp.einsum('...ad,...bd->...ab', row_points, column_points, precision=highest)
    row_norms = lax.optimization_barrier(jnp.sum(row_points * row_points, axis=-1))[..., :, None]
    column_norms = lax.optimization_barrier(jnp.sum(column_points * column_points, axis=-1))[..., None, :]
    squared = jnp.maximum(row_norms + column_norms - 2.0 * cross, 0.0)
    scaled = jnp.sqrt(3.0 * squared) / length_scale
    return (1.0 + scaled) * jnp.exp(-scaled)

def far_field(own_anchors, lists, source_moments, source_anchors, first_index):
    clusters = lists.shape[0]
    block_size = min(clusters, 128)
    usable = lists >= 0
    located = jnp.clip(lists - first_index, 0, source_moments.shape[0] - 1)

    def one_block(inputs):
        anchors_block, located_block, usable_block = inputs
        partner_moments = jnp.where(usable_block[:, :, None, None], jnp.take(source_moments, located_block, axis=0), 0.0)
        partner_anchors = jnp.take(source_anchors, located_block, axis=0)
        own_block = jnp.broadcast_to(anchors_block[:, None], partner_anchors.shape)
        kernel = matern_block(own_block, partner_anchors)
        return jnp.einsum('cnab,cnbs->cas', kernel, partner_moments, precision=highest)
    blocks = clusters // block_size
    results = lax.map(one_block, (own_anchors.reshape((blocks, block_size) + own_anchors.shape[1:]), located.reshape(blocks, block_size, -1), usable.reshape(blocks, block_size, -1)))
    return results.reshape((clusters,) + results.shape[2:])

def near_field(target_leaves, source_leaves, source_charges, near_blocks, first_index):
    leaf_count = target_leaves.shape[0]
    block_size = min(leaf_count, 16)
    usable = near_blocks >= 0
    located = jnp.clip(near_blocks - first_index, 0, source_leaves.shape[0] - 1)

    def one_block(inputs):
        targets, located_block, usable_block = inputs
        partner_points = jnp.take(source_leaves, located_block, axis=0)
        partner_charges = jnp.where(usable_block[:, :, None, None], jnp.take(source_charges, located_block, axis=0), 0.0)
        own_block = jnp.broadcast_to(targets[:, None], partner_points.shape)
        kernel = matern_block(own_block, partner_points)
        return jnp.einsum('bnpq,bnqs->bps', kernel, partner_charges, precision=highest)
    blocks = leaf_count // block_size
    results = lax.map(one_block, (target_leaves.reshape((blocks, block_size) + target_leaves.shape[1:]), located.reshape(blocks, block_size, -1), usable.reshape(blocks, block_size, -1)))
    return results.reshape((leaf_count,) + results.shape[2:])

def level_rows(values, devices, per_device, first_row, number):
    shaped = values.reshape((devices, per_device) + values.shape[1:])
    picked = shaped[:, first_row:first_row + number]
    return picked.reshape((devices * number,) + values.shape[1:])

def upward(transfer, moments):
    lifted = jnp.einsum('cab,cas->cbs', transfer, moments, precision=highest)
    return lifted[0::2] + lifted[1::2]

def downward(transfer, parents):
    return jnp.einsum('cab,cbs->cas', transfer, jnp.repeat(parents, 2, axis=0), precision=highest)

def reference(points, charges, leaf_basis, local_transfer, local_anchors, local_lists, near_blocks, top_transfer, top_anchors, top_lists):
    devices = N_LEAF
    local_depth = LEAVES_DEV.bit_length() - 1
    top_depth = devices.bit_length() - 1
    per_clusters = 2 * LEAVES_DEV - 1
    per_children = 2 * LEAVES_DEV - 2
    anchors_by_level = []
    lists_by_level = []
    transfer_by_level = []
    for height in range(local_depth + 1):
        number = LEAVES_DEV >> height
        first_row = 2 * LEAVES_DEV - 2 * number
        anchors_by_level.append(level_rows(local_anchors, devices, per_clusters, first_row, number).reshape(-1, RANK, DIM))
        lists_by_level.append(level_rows(local_lists, devices, per_clusters, first_row, number))
        if height < local_depth:
            transfer_by_level.append(level_rows(local_transfer, devices, per_children, first_row, number).reshape(-1, RANK, RANK))
    for height in range(top_depth):
        number = devices >> height
        first_row = 2 * devices - 2 * number
        transfer_by_level.append(top_transfer[first_row:first_row + number].reshape(-1, RANK, RANK))
    for height in range(1, top_depth + 1):
        number = devices >> height
        first_row = devices - (devices >> height - 1)
        anchors_by_level.append(top_anchors[first_row:first_row + number].reshape(-1, RANK, DIM))
        lists_by_level.append(top_lists[first_row:first_row + number])
    basis_leaves = leaf_basis.reshape(RANK, LEAVES, LEAF)
    charge_leaves = charges.reshape(RHS, LEAVES, LEAF)
    moments = [jnp.einsum('rtp,stp->trs', basis_leaves, charge_leaves, precision=highest)]
    for transfer in transfer_by_level:
        moments.append(upward(transfer, moments[-1]))
    far_terms = []
    for height in range(len(moments)):
        far_terms.append(far_field(anchors_by_level[height], lists_by_level[height], moments[height], anchors_by_level[height], 0))
    expansion = far_terms[-1]
    for height in range(len(transfer_by_level) - 1, -1, -1):
        expansion = far_terms[height] + downward(transfer_by_level[height], expansion)
    far_points = jnp.einsum('rtp,trs->stp', basis_leaves, expansion, precision=highest).reshape(RHS, POINTS)
    point_leaves = points.reshape(DIM, LEAVES, LEAF).transpose(1, 2, 0)
    near_term = near_field(point_leaves, point_leaves, charge_leaves.transpose(1, 2, 0), near_blocks, 0)
    near_points = near_term.transpose(2, 0, 1).reshape(RHS, POINTS)
    return near_points + far_points
```

```python
import math

import jax
import jax.numpy as jnp
import numpy as np
from jax import lax
from jax.experimental import pallas as pl
from jax.experimental.pallas import tpu as pltpu
from jax.sharding import PartitionSpec as P

DIM = 16
RHS = 16
LEAF = 128
RANK = 64
LEAVES_DEV = 32
NREACH = 16
REACH = 6
DEVICES = 128
TOP = 7
SHARED = 6
SLOTS = 4

bf16 = jnp.bfloat16
f32 = jnp.float32
SCALE = math.log2(math.e) / math.sqrt(3.0)
LN2 = math.log(2.0)
TINY = 1e-30

COLUMN = [0, 2048, 3072, 3584, 3840, 3968]
ROW = [0, 32, 48, 56, 60]
RIM = [0, 384, 768, 1152, 1408, 1536]
RIM_WIDTH = 1664
LOW_PIECES = [(0, 384), (2048, 2432), (3072, 3456), (3584, 4096)]
HIGH_PIECES = [(1664, 2048), (2688, 3072), (3200, 4096)]
VMEM = pl.BlockSpec(memory_space=pltpu.VMEM)
SMEM = pl.BlockSpec(memory_space=pltpu.SMEM)


def relevant(first, second, level):
    return 2 <= abs((first >> level) - (second >> level)) <= REACH


def slot_tables():
    sent = np.full((DEVICES, DEVICES, SLOTS), TOP, np.int32)
    held = np.zeros((DEVICES, SHARED, DEVICES), np.int32)
    for first in range(DEVICES):
        for second in range(DEVICES):
            levels = [level for level in range(SHARED) if relevant(first, second, level)]
            for slot, level in enumerate(levels):
                sent[first, second, slot] = level
                held[first, level, second] = slot
            sent[first, second, SLOTS - 1] = SHARED
    return np.concatenate([sent.reshape(DEVICES, -1), held.reshape(DEVICES, -1)], axis=1)


SENT = DEVICES * SLOTS


def split(x):
    high = x.astype(bf16)
    return high, (x - high.astype(f32)).astype(bf16)


def lanes(*parts):
    return jnp.concatenate(parts, axis=1)


def rows(*parts):
    return jnp.concatenate(parts, axis=0)


def dot(a, b):
    return jnp.dot(a, b, preferred_element_type=f32)


def dot_nt(a, b):
    return lax.dot_general(a, b, (((1,), (1,)), ((), ())), preferred_element_type=f32)


def narrow(x):
    high, low = split(x)
    return rows(lanes(high, high), lanes(low, low))


def folded(x):
    return x[:16] + x[16:]


def sides(x):
    x = x * SCALE
    high = x.astype(bf16).astype(f32)
    low = (x - high).astype(bf16).astype(f32)
    norm = jnp.sum(high * (high + 2.0 * low), axis=0, keepdims=True)
    norm_high = norm.astype(bf16).astype(f32)
    norm_middle = (norm - norm_high).astype(bf16).astype(f32)
    norm_low = norm - norm_high - norm_middle
    row = lax.broadcasted_iota(jnp.int32, x.shape, 0)
    parts = jnp.where(row % 3 == 0, norm_high, jnp.where(row % 3 == 1, norm_middle, norm_low))
    return high, low, parts, row


def source_side(x):
    high, low, parts, row = sides(x)
    tail = jnp.where(row < 3, 1.0, jnp.where(row < 6, parts, 0.0))
    return rows(high, high, low, tail)


def target_sides(x):
    high, low, parts, row = sides(x)
    tail = jnp.where(row < 3, parts, jnp.where(row < 6, 1.0, 0.0))
    factors = rows(-2.0 * high, -2.0 * low, -2.0 * high, tail)
    first = rows(factors, jnp.zeros_like(factors)).T
    return first.astype(bf16), pltpu.roll(first, RANK, 1).astype(bf16)


def matern(squared):
    squared = jnp.maximum(squared, TINY)
    distance = squared * lax.rsqrt(squared)
    return (1.0 + LN2 * distance) * jnp.exp2(-distance)


def pick(parts):
    lane = lax.broadcasted_iota(jnp.int32, parts[0].shape, 1)
    result = parts[3]
    for j in (2, 1, 0):
        result = jnp.where(lane < 32 * (j + 1), parts[j], result)
    return result


def interact(targets, sources, weights):
    kernel = matern(dot(targets, sources))
    high, low = split(kernel)
    size = kernel.shape[0]
    result = dot(rows(high, low), weights)
    quarter = size // 4
    return pick(
        [
            result[quarter * j : quarter * (j + 1)]
            + result[size + quarter * j : size + quarter * (j + 1)]
            for j in range(4)
        ]
    )


def weight_turns(slabs):
    parts = []
    for slab in slabs:
        high = slab.astype(bf16).astype(f32)
        parts += [high, slab - high]
    columns = rows(*parts).T
    return [
        (columns if turn == 0 else pltpu.roll(columns, 32 * turn, 1)).astype(bf16)
        for turn in range(4)
    ]


def halves(first, second):
    lane = lax.broadcasted_iota(jnp.int32, first.shape, 1)
    return jnp.where(lane < RANK, first, second)


def moments_kernel(
    tables, basis, charges, transfer, path, moments, low_rim, high_rim, outgoing, blocks
):
    def two_leaves(q, carry):
        parts = []
        for leaf in range(2):
            columns = pl.ds(pl.multiple_of(q * 256 + leaf * 128, 128), 128)
            high, low = split(basis[:, columns])
            parts.append(folded(dot_nt(narrow(charges[:, columns]), lanes(high, low))))
        moments[:, pl.ds(pl.multiple_of(q * 128, 128), 128)] = lanes(*parts)
        return carry

    lax.fori_loop(0, LEAVES_DEV // 2, two_leaves, 0, unroll=8)

    def lifted(slab, matrices):
        high, low = split(matrices)
        return folded(dot(narrow(slab), rows(high, low)))

    for height in range(5):
        number = LEAVES_DEV >> height
        parents = []
        for q in range(number // 2):
            start = (ROW[height] + 2 * q) * RANK
            slab = moments[:, COLUMN[height] + 128 * q : COLUMN[height] + 128 * (q + 1)]
            parents.append(lifted(slab, transfer[start : start + 128, :]))
        if height == 4:
            parents.append(jnp.zeros((16, RANK), f32))
        for q in range(len(parents) // 2):
            start = COLUMN[height + 1] + 128 * q
            moments[:, start : start + 128] = lanes(parents[2 * q], parents[2 * q + 1])

    for rim, pieces in ((low_rim, LOW_PIECES), (high_rim, HIGH_PIECES)):
        start = 0
        for first, last in pieces:
            rim[:, start : start + last - first] = moments[:, first:last]
            start += last - first

    value = moments[:, COLUMN[5] : COLUMN[5] + RANK]
    for level in range(SHARED + 1):
        blocks[level] = lanes(value[:8], value[8:])
        if level < SHARED:
            value = lifted(value, path[RANK * level : RANK * (level + 1), :])
    blocks[TOP] = jnp.zeros((8, 128), f32)

    def one_device(other, carry):
        for slot in range(SLOTS - 1):
            outgoing[other, 8 * slot : 8 * (slot + 1), :] = blocks[tables[other * SLOTS + slot]]
        outgoing[other, 8 * (SLOTS - 1) : 8 * SLOTS, :] = blocks[SHARED]
        return carry

    lax.fori_loop(0, DEVICES, one_device, 0, unroll=8)


def moments_call(tables, basis, charges, transfer, path):
    shape = jax.ShapeDtypeStruct
    return pl.pallas_call(
        moments_kernel,
        out_shape=(
            shape((16, 4096), f32),
            shape((16, RIM_WIDTH), f32),
            shape((16, RIM_WIDTH), f32),
            shape((DEVICES, 8 * SLOTS, 128), f32),
        ),
        in_specs=[SMEM, VMEM, VMEM, VMEM, VMEM],
        out_specs=(VMEM, VMEM, VMEM, VMEM),
        scratch_shapes=[pltpu.VMEM((8, 8, 128), f32)],
        compiler_params=pltpu.CompilerParams(vmem_limit_bytes=48 * 2**20),
        cost_estimate=pl.CostEstimate(flops=10**9, bytes_accessed=2**22, transcendentals=0),
        name="moments",
    )(tables, basis, charges, transfer, path)


def near_kernel(device, near_blocks, points, charges, low, high, out, factors, weights):
    def prepare(point_ref, charge_ref, charge_row, first):
        def four_leaves(i, carry):
            columns = pl.ds(pl.multiple_of(i * 512, 512), 512)
            side = source_side(point_ref[:DIM, columns]).astype(bf16)
            charge = charge_ref[charge_row : charge_row + RHS, columns]
            slabs = []
            for m in range(4):
                factors[(first + i) * 4 + m] = side[:, 128 * m : 128 * (m + 1)]
                slabs.append(charge[:, 128 * m : 128 * (m + 1)])
            for turn, value in enumerate(weight_turns(slabs)):
                weights[turn, first + i] = value
            return carry

        return four_leaves

    lax.fori_loop(0, 4, prepare(low, low, DIM, 0), 0, unroll=2)
    lax.fori_loop(0, 8, prepare(points, charges, 0, 4), 0, unroll=2)
    lax.fori_loop(0, 4, prepare(high, high, DIM, 12), 0, unroll=2)
    factors[64] = jnp.zeros((64, 128), bf16)
    for turn in range(4):
        weights[turn, 16] = jnp.zeros((128, 128), bf16)
    first_leaf = device[0] * LEAVES_DEV - NREACH

    def one_leaf(t, carry):
        columns = pl.ds(pl.multiple_of(t * 128, 128), 128)
        front, back = target_sides(points[:, columns])
        empty = jnp.zeros_like(front)
        targets = rows(
            lanes(front, empty), lanes(back, empty), lanes(empty, front), lanes(empty, back)
        )
        located = []
        for j in range(8):
            block = near_blocks[t, j]
            inside = jnp.minimum(jnp.maximum(block - first_leaf, 0), 63)
            located.append(jnp.where(block < 0, 64, inside))
        sources = rows(
            *[lanes(factors[located[2 * j]], factors[located[2 * j + 1]]) for j in range(4)]
        )
        weight = rows(
            *[
                pick([weights[(j - located[2 * j + h]) & 3, located[2 * j + h] >> 2] for j in range(4)])
                for h in range(2)
            ]
        )
        total = interact(targets, sources, weight).T
        out[:, columns] = sum(total[16 * g : 16 * (g + 1)] for g in range(8))
        return carry

    lax.fori_loop(0, LEAVES_DEV, one_leaf, 0, unroll=8)


def near_call(device, near_blocks, points, charges, low, high):
    return pl.pallas_call(
        near_kernel,
        out_shape=jax.ShapeDtypeStruct((RHS, LEAVES_DEV * LEAF), f32),
        in_specs=[SMEM, SMEM, VMEM, VMEM, VMEM, VMEM],
        out_specs=VMEM,
        scratch_shapes=[
            pltpu.VMEM((65, 64, 128), bf16),
            pltpu.VMEM((4, 17, 128, 128), bf16),
        ],
        compiler_params=pltpu.CompilerParams(vmem_limit_bytes=48 * 2**20),
        cost_estimate=pl.CostEstimate(flops=10**10, bytes_accessed=2**22, transcendentals=0),
        name="near",
    )(device, near_blocks, points, charges, low, high)


def prepare_factors(anchors, factors, groups):
    def four_slabs(i, carry):
        side = source_side(anchors[:, pl.ds(pl.multiple_of(i * 512, 512), 512)])
        for m in range(4):
            slab = side[:, 128 * m : 128 * (m + 1)]
            turned = pltpu.roll(slab, RANK, 1)
            factors[(i * 4 + m) * 2] = halves(slab, turned).astype(bf16)
            factors[(i * 4 + m) * 2 + 1] = halves(turned, slab).astype(bf16)
        return carry

    lax.fori_loop(0, groups, four_slabs, 0, unroll=2)


def prepare_weights(moments, weights, groups):
    def four_slabs(i, carry):
        value = moments[:, pl.ds(pl.multiple_of(i * 512, 512), 512)]
        turns = weight_turns([value[:, 128 * m : 128 * (m + 1)] for m in range(4)])
        for turn in range(4):
            weights[turn, i, 0] = turns[turn][:RANK]
            weights[turn, i, 1] = turns[turn][RANK:]
        return carry

    lax.fori_loop(0, groups, four_slabs, 0, unroll=2)


def two_targets(anchors):
    front, back = target_sides(anchors)
    empty = jnp.zeros((RANK, 128), bf16)
    return rows(
        lanes(front[:RANK], empty),
        lanes(back[:RANK], empty),
        lanes(empty, front[RANK:]),
        lanes(empty, back[RANK:]),
    )


def four_sources(factors, located):
    return lanes(
        halves(factors[located[0]], factors[located[1]]),
        halves(factors[located[2]], factors[located[3]]),
    )


def placed(weights, index, slot):
    pair = index >> 1
    return weights[(slot - pair) & 3, pair >> 2, index & 1]


def two_clusters(anchors, factors, weights, located):
    sources = rows(*[four_sources(factors, located[4 * slot : 4 * slot + 4]) for slot in range(4)])
    weight = rows(
        *[pick([placed(weights, located[4 * slot + m], slot) for slot in range(4)]) for m in range(4)]
    )
    return cluster_sums(interact(two_targets(anchors), sources, weight))


def cluster_sums(total):
    total = total.T
    return lanes(
        total[:16] + total[16:32] + total[32:48] + total[48:64],
        total[64:80] + total[80:96] + total[96:112] + total[112:],
    )


def locate(entry, first, last, base, empty):
    inside = jnp.minimum(jnp.maximum(entry - first, 0), last)
    return jnp.where(entry < 0, empty, base + inside)


FINE_BASE = [0, 44, 72]
FINE_EMPTY = 92


def fine_kernel(
    device,
    lists,
    anchors,
    moments,
    low_anchors,
    high_anchors,
    low_moments,
    high_moments,
    far,
    held_anchors,
    held_moments,
    factors,
    weights,
):
    start = 0
    for height in range(3):
        width = (LEAVES_DEV >> height) * RANK
        rim = slice(RIM[height], RIM[height] + REACH * RANK)
        own = slice(COLUMN[height], COLUMN[height] + width)
        for held, parts in (
            (
                held_anchors,
                (low_anchors[2 * DIM : 3 * DIM, rim], anchors[:, own], high_anchors[2 * DIM : 3 * DIM, rim]),
            ),
            (held_moments, (low_moments[:, rim], moments[:, own], high_moments[:, rim])),
        ):
            at = start
            for part in parts:
                held[:, at : at + part.shape[1]] = part
                at += part.shape[1]
        start = at
    held_anchors[:, start:] = jnp.zeros((DIM, 48 * 128 - start), f32)
    held_moments[:, start:] = jnp.zeros((DIM, 48 * 128 - start), f32)
    prepare_factors(held_anchors, factors, 12)
    prepare_weights(held_moments, weights, 12)

    for height in range(3):
        number = LEAVES_DEV >> height

        def one_pair(q, carry, height=height, number=number):
            first = device[0] * number - REACH
            located = []
            for cluster in range(2):
                for j in range(8):
                    entry = lists[2 * LEAVES_DEV - 2 * number + 2 * q + cluster, j]
                    located.append(
                        locate(entry, first, number + 2 * REACH - 1, FINE_BASE[height], FINE_EMPTY)
                    )
            columns = pl.ds(pl.multiple_of(COLUMN[height] + q * 128, 128), 128)
            far[:, columns] = two_clusters(anchors[:, columns], factors, weights, located)
            return carry

        lax.fori_loop(0, number // 2, one_pair, 0, unroll=4)


def fine_call(device, lists, anchors, moments, low, high, low_moments, high_moments):
    return pl.pallas_call(
        fine_kernel,
        out_shape=jax.ShapeDtypeStruct((RHS, 56 * RANK), f32),
        in_specs=[SMEM, SMEM] + [VMEM] * 6,
        out_specs=VMEM,
        scratch_shapes=[
            pltpu.VMEM((DIM, 48 * 128), f32),
            pltpu.VMEM((RHS, 48 * 128), f32),
            pltpu.VMEM((96, 64, 128), bf16),
            pltpu.VMEM((4, 12, 2, 64, 128), bf16),
        ],
        compiler_params=pltpu.CompilerParams(vmem_limit_bytes=48 * 2**20),
        cost_estimate=pl.CostEstimate(flops=5 * 10**9, bytes_accessed=2**22, transcendentals=0),
        name="fine",
    )(device, lists, anchors, moments, low, high, low_moments, high_moments)


COARSE_EMPTY = 30


def coarse_kernel(
    device,
    tables,
    lists,
    top_lists,
    anchors,
    moments,
    low_anchors,
    high_anchors,
    low_moments,
    high_moments,
    low_second,
    high_second,
    low_third,
    high_third,
    incoming,
    top_anchors,
    path,
    transfer,
    basis,
    far,
    near,
    out,
    held_anchors,
    held_moments,
    factors,
    weights,
    expansion,
):
    me = device[0]
    a = slice(0, DIM)
    m = slice(DIM, 2 * DIM)
    e = slice(2 * DIM, 3 * DIM)

    def at(column):
        return slice(column, column + 128)

    slabs = [
        (low_second[a, at(0)], low_second[m, at(0)]),
        (low_anchors[e, at(1152)], low_moments[:, at(1152)]),
        (low_anchors[e, at(1280)], low_moments[:, at(1280)]),
        (anchors[:, at(3584)], moments[:, at(3584)]),
        (anchors[:, at(3712)], moments[:, at(3712)]),
        (high_anchors[e, at(1152)], high_moments[:, at(1152)]),
        (high_anchors[e, at(1280)], high_moments[:, at(1280)]),
        (high_second[a, at(0)], high_second[m, at(0)]),
        (low_third[a, at(0)], low_third[m, at(0)]),
        (low_second[a, at(128)], low_second[m, at(128)]),
        (low_anchors[e, at(1408)], low_moments[:, at(1408)]),
        (anchors[:, at(3840)], moments[:, at(3840)]),
        (high_anchors[e, at(1408)], high_moments[:, at(1408)]),
        (high_second[a, at(128)], high_second[m, at(128)]),
        (high_third[a, at(0)], high_third[m, at(0)]),
        (low_third[a, at(256)], None),
        (low_third[a, at(128)], None),
        (low_second[a, at(256)], None),
        (low_anchors[e, at(1536)], None),
        (anchors[:, at(3968)], None),
        (high_anchors[e, at(1536)], None),
        (high_second[a, at(256)], None),
        (high_third[a, at(128)], None),
        (high_third[a, at(256)], None),
    ]
    for index, (anchor_slab, moment_slab) in enumerate(slabs):
        held_anchors[:, at(128 * index)] = anchor_slab
        if moment_slab is not None:
            held_moments[:, at(128 * index)] = moment_slab
    held_moments[:, at(128 * 15)] = jnp.zeros((RHS, 128), f32)
    prepare_factors(held_anchors, factors, 6)
    prepare_weights(held_moments, weights, 4)

    def local_pair(height, q, base):
        number = LEAVES_DEV >> height
        located = []
        for cluster in range(2):
            for j in range(8):
                entry = lists[2 * LEAVES_DEV - 2 * number + 2 * q + cluster, j]
                located.append(
                    locate(entry, me * number - REACH, number + 2 * REACH - 1, base, COARSE_EMPTY)
                )
        return two_clusters(
            anchors[:, at(COLUMN[height] + 128 * q)], factors, weights, located
        )

    far_third = [local_pair(3, q, 0) for q in range(2)]
    far_fourth = local_pair(4, 0, 16)

    lane = lax.broadcasted_iota(jnp.int32, (8, 128), 1)

    def two_blocks(first, second):
        return rows(
            jnp.where(lane < RANK, first, pltpu.roll(second, RANK, 1)),
            jnp.where(lane < RANK, pltpu.roll(first, RANK, 1), second),
        )

    def lifted(slab, matrices):
        high, low = split(matrices)
        return folded(dot(narrow(slab), rows(high, low)))

    sixth = [
        jnp.sum(incoming[64 * c : 64 * (c + 1), 8 * (SLOTS - 1) : 8 * SLOTS, :], axis=0)
        for c in range(2)
    ]
    seventh = lifted(two_blocks(*sixth), path[RANK * 7 : RANK * 9, :])
    seventh = lanes(seventh[:8], seventh[8:])

    entries = [[lists[62, j] for j in range(8)]]
    for level in range(1, TOP + 1):
        row = DEVICES - (DEVICES >> (level - 1)) + (me >> level)
        entries.append([top_lists[row, j] for j in range(8)])

    def block(level, entry):
        if level == TOP:
            return jnp.where(entry == 0, seventh, 0.0)
        if level == SHARED:
            return jnp.where(entry == 0, sixth[0], jnp.where(entry == 1, sixth[1], 0.0))
        first = jnp.maximum(entry, 0) << level

        def add(i, total):
            slot = tables[SENT + level * DEVICES + first + i]
            return total + incoming[first + i, pl.ds(pl.multiple_of(slot * 8, 8), 8), :]

        count = jnp.where(entry < 0, 0, 1 << level)
        return lax.fori_loop(0, count, add, jnp.zeros((8, 128), f32))

    far_chain = []
    for unit in range(4):
        pairs = []
        for level in (2 * unit, 2 * unit + 1):
            held = [block(level, entry) for entry in entries[level]]
            pairs += [two_blocks(held[2 * j], held[2 * j + 1]) for j in range(4)]
        weight = []
        for h in range(2):
            parts = []
            for slot in range(4):
                high = pairs[2 * slot + h].astype(bf16).astype(f32)
                parts += [high, pairs[2 * slot + h] - high]
            weight.append(rows(*parts).T.astype(bf16))
        own = top_anchors[:, at(128 * unit)]
        sources = []
        for level in (2 * unit, 2 * unit + 1):
            for h in range(2):
                if level == 0:
                    located = []
                    for j in range(4):
                        shift = entries[0][4 * h + j] - me + REACH
                        shift = jnp.minimum(jnp.maximum(shift, 0), 2 * REACH)
                        place = shift + sum(
                            (shift >= edge).astype(jnp.int32) for edge in (1, 6, 7, 8)
                        )
                        located.append(30 + place)
                    sources.append(four_sources(factors, located))
                else:
                    start = 512 * level + 256 * h
                    sources.append(source_side(top_anchors[:, start : start + 256]).astype(bf16))
        if unit == 0:
            own = halves(anchors[:, at(COLUMN[5])], own)
        result = cluster_sums(interact(two_targets(own), rows(*sources), rows(*weight)))
        far_chain += [result[:, :RANK], result[:, RANK:]]

    def pushed(value, matrices):
        high, low = split(matrices)
        return folded(dot_nt(narrow(value), lanes(high, low)))

    value = far_chain[TOP]
    for level in range(TOP - 1, -1, -1):
        value = far_chain[level] + pushed(value, path[RANK * level : RANK * (level + 1), :])

    def children(parent, height, q):
        start = (ROW[height] + 2 * q) * RANK
        return pushed(parent, transfer[start : start + 128, :])

    upper = [far_fourth + children(value, 4, 0)]
    for height in (3, 2, 1, 0):
        lower = []
        for q, slab in enumerate(upper):
            for side in range(2):
                parent = slab[:, RANK * side : RANK * (side + 1)]
                index = 2 * q + side
                if height == 3:
                    own = far_third[index]
                else:
                    own = far[:, at(COLUMN[height] + 128 * index)]
                lower.append(own + children(parent, height, index))
        upper = lower
    for q, slab in enumerate(upper):
        expansion[:, at(128 * q)] = slab

    def two_leaves(q, carry):
        slab = expansion[:, pl.ds(pl.multiple_of(q * 128, 128), 128)]
        for leaf in range(2):
            columns = pl.ds(pl.multiple_of(q * 256 + leaf * 128, 128), 128)
            high, low = split(basis[:, columns])
            own = slab[:, RANK * leaf : RANK * (leaf + 1)]
            out[:, columns] = near[:, columns] + folded(dot(narrow(own), rows(high, low)))
        return carry

    lax.fori_loop(0, LEAVES_DEV // 2, two_leaves, 0, unroll=8)


def coarse_call(*arguments):
    return pl.pallas_call(
        coarse_kernel,
        out_shape=jax.ShapeDtypeStruct((RHS, LEAVES_DEV * LEAF), f32),
        in_specs=[SMEM] * 4 + [VMEM] * 17,
        out_specs=VMEM,
        scratch_shapes=[
            pltpu.VMEM((DIM, 24 * 128), f32),
            pltpu.VMEM((RHS, 16 * 128), f32),
            pltpu.VMEM((48, 64, 128), bf16),
            pltpu.VMEM((4, 4, 2, 64, 128), bf16),
            pltpu.VMEM((RHS, 2048), f32),
        ],
        compiler_params=pltpu.CompilerParams(vmem_limit_bytes=48 * 2**20),
        cost_estimate=pl.CostEstimate(flops=10**9, bytes_accessed=2**23, transcendentals=0),
        name="coarse",
    )(*arguments)


def shifted(value, by):
    return lax.ppermute(value, "leaf", [(i, (i + by) % DEVICES) for i in range(DEVICES)])


def as_columns(anchor_rows):
    return anchor_rows.reshape(-1, DIM).T


def pieces(array, parts):
    return jnp.concatenate([array[:, first:last] for first, last in parts], axis=1)


def on_device(
    points,
    charges,
    leaf_basis,
    local_transfer,
    local_anchors,
    local_lists,
    near_blocks,
    top_transfer,
    top_anchors,
    top_lists,
):
    index = lax.axis_index("leaf")
    device = index.reshape(1)
    half = NREACH * LEAF
    anchors = as_columns(jnp.pad(local_anchors, ((0, 1), (0, 0))))

    def rim(columns, parts):
        held = jnp.pad(pieces(anchors, parts), ((0, 0), (0, half - RIM_WIDTH)))
        return jnp.concatenate([points[:, columns], charges[:, columns], held], axis=0)

    low = shifted(rim(slice(half, None), HIGH_PIECES), 1)
    high = shifted(rim(slice(0, half), LOW_PIECES), -1)

    tables = lax.dynamic_index_in_dim(jnp.asarray(slot_tables()), index, 0, keepdims=False)
    levels = jnp.arange(TOP, dtype=jnp.int32)
    own_rows = 2 * DEVICES - (2 * DEVICES >> levels) + (index >> levels)
    path_rows = jnp.concatenate([own_rows, jnp.array([252, 253], jnp.int32)])
    path = jnp.take(top_transfer, path_rows, axis=0, mode="clip").reshape(-1, RANK)
    transfer = local_transfer.reshape(-1, RANK)
    moments, low_rim, high_rim, outgoing = moments_call(
        tables, leaf_basis, charges, transfer, path
    )
    incoming = lax.all_to_all(outgoing, "leaf", 0, 0)
    low_moments = shifted(high_rim, 1)
    high_moments = shifted(low_rim, -1)

    upper = levels + 1
    first_rows = DEVICES - (DEVICES >> (upper - 1))
    chain_rows = first_rows + (index >> upper)
    chain_lists = jnp.take(top_lists, chain_rows, axis=0, mode="clip")
    partner_rows = first_rows[:, None] + jnp.maximum(chain_lists, 0)
    wanted = jnp.concatenate([chain_rows[:1], chain_rows, partner_rows.reshape(-1)])
    chain_anchors = as_columns(jnp.take(top_anchors, wanted, axis=0, mode="clip"))

    def roots(array):
        return array[2 * DIM :, RIM[5] : RIM[5] + RANK]

    own_root = anchors[:, COLUMN[5] : COLUMN[5] + RANK]

    def second(columns, root_pair):
        held = jnp.concatenate([anchors[:, columns], anchors[:, 3840:3968]] + root_pair, axis=1)
        sent = jnp.concatenate([moments[:, columns], moments[:, 3840:4096]], axis=1)
        return jnp.concatenate([held, sent], axis=0)

    low_second = shifted(second(slice(3712, 3840), [roots(low), own_root]), 2)
    high_second = shifted(second(slice(3584, 3712), [own_root, roots(high)]), -2)

    near = near_call(device, near_blocks, points, charges, low, high)

    def third(parts):
        held = jnp.concatenate([anchors[:, 3840:3968]] + parts + [own_root], axis=1)
        sent = jnp.concatenate([moments[:, 3840:4096], moments[:, 3968:4096]], axis=1)
        return jnp.concatenate([held, sent], axis=0)

    near, low_second, high_second = lax.optimization_barrier((near, low_second, high_second))
    low_roots = low_second[:DIM, 256:384]
    high_roots = high_second[:DIM, 256:384]
    low_third = shifted(third([low_roots[:, RANK:], roots(low), low_roots[:, :RANK]]), 3)
    high_third = shifted(third([roots(high), high_roots[:, :RANK], high_roots[:, RANK:]]), -3)
    far = fine_call(device, local_lists, anchors, moments, low, high, low_moments, high_moments)
    return coarse_call(
        device,
        tables,
        local_lists,
        top_lists,
        anchors,
        moments,
        low,
        high,
        low_moments,
        high_moments,
        low_second,
        high_second,
        low_third,
        high_third,
        incoming,
        chain_anchors,
        path,
        transfer,
        leaf_basis,
        far,
        near,
    )


def solution(mesh):
    in_specs = (
        P(None, "leaf"),
        P(None, "leaf"),
        P(None, "leaf"),
        P("leaf", None),
        P("leaf", None),
        P("leaf", None),
        P("leaf", None),
        P(),
        P(),
        P(),
    )
    out_specs = P(None, "leaf")
    return jax.shard_map(
        on_device, mesh=mesh, in_specs=in_specs, out_specs=out_specs, check_vma=False
    )
```

```python
import math

import jax
import jax.numpy as jnp
import numpy as np
from jax import lax
from jax.experimental import pallas as pl
from jax.experimental.pallas import tpu as pltpu
from jax.sharding import PartitionSpec as P

DIM = 16
RHS = 16
LEAF = 128
RANK = 64
LEAVES_DEV = 32
NREACH = 16
REACH = 6
DEVICES = 128
TOP = 7
SHARED = 6
SLOTS = 4
NOTHING = 7
ANCHORS = 8
FORMED = (-6, -5, 5, 6)
LOCAL = 62
MATRICES = LOCAL + 13

bf16 = jnp.bfloat16
f32 = jnp.float32
SCALE = math.log2(math.e) / math.sqrt(3.0)
LN2 = math.log(2.0)
TINY = 1e-30

COLUMN = [0, 2048, 3072, 3584, 3840, 3968]
ROW = [0, 32, 48, 56, 60]
RIM = [0, 384, 768, 1152, 1408, 1536]
RIM_WIDTH = 1664
LOW_PIECES = [(0, 384), (2048, 2432), (3072, 3456), (3584, 4096)]
HIGH_PIECES = [(1664, 2048), (2688, 3072), (3200, 4096)]
VMEM_LIMIT = 60 * 2**20
VMEM = pl.BlockSpec(memory_space=pltpu.VMEM)
SMEM = pl.BlockSpec(memory_space=pltpu.SMEM)
HBM = pl.BlockSpec(memory_space=pltpu.HBM)


def relevant(first, second, level):
    return 2 <= abs((first >> level) - (second >> level)) <= REACH


def slot_tables():
    sent = np.full((DEVICES, DEVICES, SLOTS), NOTHING, np.int32)
    held = np.zeros((DEVICES, SHARED + 1, DEVICES), np.int32)
    for first in range(DEVICES):
        for second in range(DEVICES):
            levels = [level for level in range(SHARED) if relevant(first, second, level)]
            if levels and levels[0] == 0:
                if len(levels) == 3:
                    levels.pop()
                    held[first, 2, second] = SLOTS + FORMED.index(second - first)
                levels.append(ANCHORS)
            for slot, level in enumerate(levels):
                sent[first, second, slot] = level
                held[first, SHARED if level == ANCHORS else level, second] = slot
            sent[first, second, SLOTS - 1] = SHARED
    tables = np.concatenate([sent.reshape(DEVICES, -1), held.reshape(DEVICES, -1)], axis=1)
    return tables.reshape(DEVICES, -1, 128)


SENT = DEVICES * SLOTS
TABLE = (SENT + (SHARED + 1) * DEVICES) // 128


def started(semaphores, *pairs):
    copies = []
    for index, (source, target) in enumerate(pairs):
        copy = pltpu.make_async_copy(source, target, semaphores.at[index])
        copy.start()
        copies.append(copy)
    return copies


def split(x):
    high = x.astype(bf16)
    return high, (x - high.astype(f32)).astype(bf16)


def lanes(*parts):
    return jnp.concatenate(parts, axis=1)


def rows(*parts):
    return jnp.concatenate(parts, axis=0)


def dot(a, b):
    return jnp.dot(a, b, preferred_element_type=f32)


def dot_nt(a, b):
    return lax.dot_general(a, b, (((1,), (1,)), ((), ())), preferred_element_type=f32)


def narrow(x):
    high, low = split(x)
    return rows(lanes(high, high), lanes(low, low))


def folded(x):
    return x[:16] + x[16:]


def sides(x):
    x = x * SCALE
    high = x.astype(bf16).astype(f32)
    low = (x - high).astype(bf16).astype(f32)
    norm = jnp.sum(high * (high + 2.0 * low), axis=0, keepdims=True)
    norm_high = norm.astype(bf16).astype(f32)
    norm_middle = (norm - norm_high).astype(bf16).astype(f32)
    norm_low = norm - norm_high - norm_middle
    row = lax.broadcasted_iota(jnp.int32, x.shape, 0)
    parts = jnp.where(row % 3 == 0, norm_high, jnp.where(row % 3 == 1, norm_middle, norm_low))
    return high, low, parts, row


def source_side(x):
    high, low, parts, row = sides(x)
    tail = jnp.where(row < 3, 1.0, jnp.where(row < 6, parts, 0.0))
    return rows(high, high, low, tail)


def target_sides(x):
    high, low, parts, row = sides(x)
    tail = jnp.where(row < 3, parts, jnp.where(row < 6, 1.0, 0.0))
    factors = rows(-2.0 * high, -2.0 * low, -2.0 * high, tail)
    first = rows(factors, jnp.zeros_like(factors)).T
    return first.astype(bf16), pltpu.roll(first, RANK, 1).astype(bf16)


def matern(squared):
    squared = jnp.maximum(squared, TINY)
    distance = squared * lax.rsqrt(squared)
    return (1.0 + LN2 * distance) * jnp.exp2(-distance)


def pick(parts):
    lane = lax.broadcasted_iota(jnp.int32, parts[0].shape, 1)
    result = parts[3]
    for j in (2, 1, 0):
        result = jnp.where(lane < 32 * (j + 1), parts[j], result)
    return result


def interact(targets, sources, weights):
    kernel = matern(dot(targets, sources))
    high, low = split(kernel)
    size = kernel.shape[0]
    result = dot(rows(high, low), weights)
    quarter = size // 4
    return pick(
        [
            result[quarter * j : quarter * (j + 1)]
            + result[size + quarter * j : size + quarter * (j + 1)]
            for j in range(4)
        ]
    )


def weight_turns(slabs):
    parts = []
    for slab in slabs:
        high = slab.astype(bf16).astype(f32)
        parts += [high, slab - high]
    columns = rows(*parts).T
    return [
        (columns if turn == 0 else pltpu.roll(columns, 32 * turn, 1)).astype(bf16)
        for turn in range(4)
    ]


def halves(first, second):
    lane = lax.broadcasted_iota(jnp.int32, first.shape, 1)
    return jnp.where(lane < RANK, first, second)


def regrouped(load, staged, count, width):
    for c in range(count):
        value = load(c)
        for i in range(width):
            staged[8 * i + c : 8 * i + c + 1, :] = value[:, 128 * i : 128 * (i + 1)]


def tile(staged, c, width):
    return staged[pl.ds(c, width, stride=8), :]


def store_matrix(staged, c, matrices, index):
    value = tile(staged, c, 32)
    matrices[pl.ds(RANK * index, 32, stride=2), :] = value[:, :RANK]
    matrices[pl.ds(RANK * index + 1, 32, stride=2), :] = value[:, RANK:]


def eight_anchors(tiles):
    group = lax.broadcasted_iota(jnp.int32, (8, 128), 1) // 16
    for bit in (1, 2, 4):
        turned = list(tiles)
        for p in range(8):
            if p & bit == 0:
                first, second = tiles[p], tiles[p | bit]
                turned[p] = jnp.where(group & bit == 0, first, pltpu.roll(second, 16 * bit, 1))
                turned[p | bit] = jnp.where(
                    group & bit == 0, pltpu.roll(first, 128 - 16 * bit, 1), second
                )
        tiles = turned
    held = rows(*tiles).T
    slabs = [lanes(held[32 * q : 32 * q + 16], held[32 * q + 16 : 32 * q + 32]) for q in range(4)]
    value = rows(*slabs)
    high = value.astype(bf16)
    rest = value - high.astype(f32)
    middle = rest.astype(bf16)
    low = (rest - middle.astype(f32)).astype(bf16)
    row = lax.broadcasted_iota(jnp.int32, (128, 128), 0)
    column = lax.broadcasted_iota(jnp.int32, (128, 128), 1)
    order = (row & RANK) + 8 * (row & 7) + ((row & 63) >> 3)
    order = jnp.where(order == column, 1.0, 0.0).astype(bf16)
    value = dot(rows(high, middle, low), order)
    value = value[:64] + (value[64:128] + value[128:])
    return [value[16 * q : 16 * (q + 1)] for q in range(4)]


def lifted(slab, matrices):
    high, low = split(matrices)
    return folded(dot(narrow(slab), rows(high, low)))


def as_block(value):
    return lanes(value[:8], value[8:])


def moments_kernel(
    device,
    tables_hbm,
    basis_hbm,
    charges_hbm,
    transfer_hbm,
    anchors_hbm,
    top_hbm,
    moments_out,
    anchors_out,
    inner_out,
    outer_out,
    third,
    outgoing_out,
    matrices_out,
    tables,
    basis,
    charges,
    transfer,
    anchor_rows,
    top_transfer,
    moments,
    anchors,
    inner,
    outer,
    outgoing,
    matrices,
    blocks,
    staged,
    staged_anchors,
    semaphores,
):
    me = device[0]
    quarters = [slice(1024 * i, 1024 * (i + 1)) for i in range(4)]
    loads = started(
        semaphores,
        (charges_hbm, charges),
        *[(basis_hbm.at[:, part], basis.at[:, part]) for part in quarters],
        (transfer_hbm, transfer),
        (top_hbm, top_transfer),
        (anchors_hbm, anchor_rows),
        (tables_hbm.at[me], tables),
    )
    loads[0].wait()

    def two_leaves(q, carry):
        parts = []
        for leaf in range(2):
            columns = pl.ds(pl.multiple_of(q * 256 + leaf * 128, 128), 128)
            high, low = split(basis[:, columns])
            parts.append(folded(dot_nt(narrow(charges[:, columns]), lanes(high, low))))
        moments[:, pl.ds(pl.multiple_of(q * 128, 128), 128)] = lanes(*parts)
        return carry

    for part in range(4):
        loads[1 + part].wait()
        lax.fori_loop(4 * part, 4 * part + 4, two_leaves, 0, unroll=4)

    loads[5].wait()
    for group in range(8):
        count = min(8, LOCAL - 8 * group)
        for i in range(32):
            staged[group % 2, 8 * i : 8 * i + count, :] = transfer[
                8 * group : 8 * group + count, 128 * i : 128 * (i + 1)
            ]
        for c in range(count):
            store_matrix(staged.at[group % 2], c, matrices, 8 * group + c)
    loads[6].wait()
    chain = [2 * DEVICES - (2 * DEVICES >> level) + (me >> level) for level in range(TOP)]
    chain += [252, 253]
    for shift in FORMED:
        other = jnp.minimum(jnp.maximum(me + shift, 0), DEVICES - 1)
        chain.append(DEVICES + (other >> 1))
    for group in range(2):
        part = chain[8 * group : 8 * group + 8]
        regrouped(lambda c: top_transfer[pl.ds(part[c], 1), :], staged.at[group], len(part), 32)
        for c in range(len(part)):
            store_matrix(staged.at[group], c, matrices, LOCAL + 8 * group + c)
    stores = started(semaphores.at[9:], (matrices, matrices_out))

    loads[7].wait()
    for group in range(8):
        count = min(8, 63 - 8 * group)
        for i in range(8):
            staged_anchors[group % 2, 8 * i : 8 * i + count, :] = anchor_rows[
                8 * group : 8 * group + count, 128 * i : 128 * (i + 1)
            ]
        tiles = [tile(staged_anchors.at[group % 2], c, 8) for c in range(count)]
        tiles += [jnp.zeros((8, 128), f32)] * (8 - count)
        for q, slab in enumerate(eight_anchors(tiles)):
            anchors[:, 512 * group + 128 * q : 512 * group + 128 * (q + 1)] = slab

    for height in range(5):
        number = LEAVES_DEV >> height
        parents = []
        for q in range(number // 2):
            start = (ROW[height] + 2 * q) * RANK
            slab = moments[:, COLUMN[height] + 128 * q : COLUMN[height] + 128 * (q + 1)]
            parents.append(lifted(slab, matrices[start : start + 128, :]))
        if height == 4:
            parents.append(jnp.zeros((16, RANK), f32))
        for q in range(len(parents) // 2):
            start = COLUMN[height + 1] + 128 * q
            moments[:, start : start + 128] = lanes(parents[2 * q], parents[2 * q + 1])

    even = (me & 1) == 0

    def fill(low_rim, high_rim):
        for row, value in ((slice(0, DIM), anchors), (slice(DIM, 2 * DIM), moments)):
            for rim, parts in ((low_rim, LOW_PIECES), (high_rim, HIGH_PIECES)):
                start = 0
                for first, last in parts:
                    rim[row, start : start + last - first] = value[:, first:last]
                    start += last - first

    @pl.when(even)
    def _():
        fill(outer, inner)

    @pl.when(jnp.logical_not(even))
    def _():
        fill(inner, outer)

    third[:DIM, :] = anchors[:, 3840:3968]
    third[DIM:, :] = moments[:, 3840:3968]
    stores += started(
        semaphores.at[10:],
        (inner, inner_out),
        (outer, outer_out),
        (moments, moments_out),
        (anchors, anchors_out),
    )

    value = moments[:, COLUMN[5] : COLUMN[5] + RANK]
    for level in range(SHARED + 1):
        blocks[level] = as_block(value)
        if level < SHARED:
            start = RANK * (LOCAL + level)
            value = lifted(value, matrices[start : start + RANK, :])
    blocks[NOTHING] = jnp.zeros((8, 128), f32)
    blocks[ANCHORS] = as_block(anchors[:, COLUMN[5] : COLUMN[5] + RANK])

    def one_device(other, carry):
        for slot in range(SLOTS - 1):
            kind = tables[other // 32, (other % 32) * SLOTS + slot]
            outgoing[other, 8 * slot : 8 * (slot + 1), :] = blocks[kind]
        outgoing[other, 8 * (SLOTS - 1) : 8 * SLOTS, :] = blocks[SHARED]
        return carry

    loads[8].wait()
    for part in range(4):
        lax.fori_loop(32 * part, 32 * part + 32, one_device, 0, unroll=8)
        own = slice(32 * part, 32 * part + 32)
        stores += started(semaphores.at[14 + part :], (outgoing.at[own], outgoing_out.at[own]))
    for copy in stores:
        copy.wait()


def moments_call(*arguments):
    shape = jax.ShapeDtypeStruct
    return pl.pallas_call(
        moments_kernel,
        out_shape=(
            shape((16, 4096), f32),
            shape((16, 4096), f32),
            shape((32, RIM_WIDTH), f32),
            shape((32, RIM_WIDTH), f32),
            shape((32, 128), f32),
            shape((DEVICES, 8 * SLOTS, 128), f32),
            shape((MATRICES * RANK, RANK), f32),
        ),
        in_specs=[SMEM] + [HBM] * 6,
        out_specs=(HBM, HBM, HBM, HBM, VMEM, HBM, HBM),
        scratch_shapes=[
            pltpu.SMEM((TABLE, 128), jnp.int32),
            pltpu.VMEM((RANK, 4096), f32),
            pltpu.VMEM((RHS, 4096), f32),
            pltpu.VMEM((LOCAL, RANK * RANK), f32),
            pltpu.VMEM((63, RANK * DIM), f32),
            pltpu.VMEM((254, RANK * RANK), f32),
            pltpu.VMEM((RHS, 4096), f32),
            pltpu.VMEM((DIM, 4096), f32),
            pltpu.VMEM((32, RIM_WIDTH), f32),
            pltpu.VMEM((32, RIM_WIDTH), f32),
            pltpu.VMEM((DEVICES, 8 * SLOTS, 128), f32),
            pltpu.VMEM((MATRICES * RANK, RANK), f32),
            pltpu.VMEM((9, 8, 128), f32),
            pltpu.VMEM((2, 256, 128), f32),
            pltpu.VMEM((2, 64, 128), f32),
            pltpu.SemaphoreType.DMA((18,)),
        ],
        compiler_params=pltpu.CompilerParams(vmem_limit_bytes=VMEM_LIMIT),
        cost_estimate=pl.CostEstimate(flops=10**9, bytes_accessed=2**22, transcendentals=0),
        name="moments",
    )(*arguments)


def near_kernel(
    device,
    near_blocks,
    points_hbm,
    charges_hbm,
    inner_hbm,
    outer_hbm,
    out_hbm,
    points,
    charges,
    inner,
    outer,
    out,
    factors,
    weights,
    semaphores,
):
    me = device[0]
    loads = started(
        semaphores,
        (points_hbm, points),
        (charges_hbm, charges),
        (inner_hbm, inner),
        (outer_hbm, outer),
    )

    def prepare(point_ref, charge_ref, charge_row, first):
        def four_leaves(i, carry):
            columns = pl.ds(pl.multiple_of(i * 512, 512), 512)
            side = source_side(point_ref[:DIM, columns]).astype(bf16)
            charge = charge_ref[charge_row : charge_row + RHS, columns]
            slabs = []
            for m in range(4):
                factors[(first + i) * 4 + m] = side[:, 128 * m : 128 * (m + 1)]
                slabs.append(charge[:, 128 * m : 128 * (m + 1)])
            for turn, value in enumerate(weight_turns(slabs)):
                weights[turn, first + i] = value
            return carry

        return four_leaves

    loads[0].wait()
    loads[1].wait()
    lax.fori_loop(0, 8, prepare(points, charges, 0, 4), 0, unroll=2)
    side = (me & 1) * 12
    loads[2].wait()
    lax.fori_loop(0, 4, prepare(inner, inner, DIM, 12 - side), 0, unroll=2)
    loads[3].wait()
    lax.fori_loop(0, 4, prepare(outer, outer, DIM, side), 0, unroll=2)
    factors[64] = jnp.zeros((64, 128), bf16)
    for turn in range(4):
        weights[turn, 16] = jnp.zeros((128, 128), bf16)
    first_leaf = me * LEAVES_DEV - NREACH

    def one_leaf(t, carry):
        columns = pl.ds(pl.multiple_of(t * 128, 128), 128)
        front, back = target_sides(points[:, columns])
        empty = jnp.zeros_like(front)
        targets = rows(
            lanes(front, empty), lanes(back, empty), lanes(empty, front), lanes(empty, back)
        )
        located = []
        for j in range(8):
            block = near_blocks[t, j]
            inside = jnp.minimum(jnp.maximum(block - first_leaf, 0), 63)
            located.append(jnp.where(block < 0, 64, inside))
        sources = rows(
            *[lanes(factors[located[2 * j]], factors[located[2 * j + 1]]) for j in range(4)]
        )
        weight = rows(
            *[
                pick([weights[(j - located[2 * j + h]) & 3, located[2 * j + h] >> 2] for j in range(4)])
                for h in range(2)
            ]
        )
        total = interact(targets, sources, weight).T
        out[:, columns] = sum(total[16 * g : 16 * (g + 1)] for g in range(8))
        return carry

    stores = []
    for part in range(2):
        lax.fori_loop(16 * part, 16 * part + 16, one_leaf, 0, unroll=8)
        own = slice(2048 * part, 2048 * part + 2048)
        stores += started(semaphores.at[4 + part :], (out.at[:, own], out_hbm.at[:, own]))
    for copy in stores:
        copy.wait()


def near_call(*arguments):
    return pl.pallas_call(
        near_kernel,
        out_shape=jax.ShapeDtypeStruct((RHS, LEAVES_DEV * LEAF), f32),
        in_specs=[SMEM, SMEM] + [HBM] * 4,
        out_specs=HBM,
        scratch_shapes=[
            pltpu.VMEM((DIM, LEAVES_DEV * LEAF), f32),
            pltpu.VMEM((RHS, LEAVES_DEV * LEAF), f32),
            pltpu.VMEM((DIM + RHS, NREACH * LEAF), f32),
            pltpu.VMEM((DIM + RHS, NREACH * LEAF), f32),
            pltpu.VMEM((RHS, LEAVES_DEV * LEAF), f32),
            pltpu.VMEM((65, 64, 128), bf16),
            pltpu.VMEM((4, 17, 128, 128), bf16),
            pltpu.SemaphoreType.DMA((6,)),
        ],
        compiler_params=pltpu.CompilerParams(vmem_limit_bytes=VMEM_LIMIT),
        cost_estimate=pl.CostEstimate(flops=10**10, bytes_accessed=2**22, transcendentals=0),
        name="near",
    )(*arguments)


def prepare_factors(anchors, factors, groups):
    def four_slabs(i, carry):
        side = source_side(anchors[:, pl.ds(pl.multiple_of(i * 512, 512), 512)])
        for m in range(4):
            slab = side[:, 128 * m : 128 * (m + 1)]
            turned = pltpu.roll(slab, RANK, 1)
            factors[(i * 4 + m) * 2] = halves(slab, turned).astype(bf16)
            factors[(i * 4 + m) * 2 + 1] = halves(turned, slab).astype(bf16)
        return carry

    lax.fori_loop(0, groups, four_slabs, 0, unroll=2)


def prepare_weights(moments, weights, groups):
    def four_slabs(i, carry):
        value = moments[:, pl.ds(pl.multiple_of(i * 512, 512), 512)]
        turns = weight_turns([value[:, 128 * m : 128 * (m + 1)] for m in range(4)])
        for turn in range(4):
            weights[turn, i, 0] = turns[turn][:RANK]
            weights[turn, i, 1] = turns[turn][RANK:]
        return carry

    lax.fori_loop(0, groups, four_slabs, 0, unroll=2)


def two_targets(anchors):
    front, back = target_sides(anchors)
    empty = jnp.zeros((RANK, 128), bf16)
    return rows(
        lanes(front[:RANK], empty),
        lanes(back[:RANK], empty),
        lanes(empty, front[RANK:]),
        lanes(empty, back[RANK:]),
    )


def four_sources(factors, located):
    return lanes(
        halves(factors[located[0]], factors[located[1]]),
        halves(factors[located[2]], factors[located[3]]),
    )


def placed(weights, index, slot):
    pair = index >> 1
    return weights[(slot - pair) & 3, pair >> 2, index & 1]


def two_clusters(anchors, factors, weights, located):
    sources = rows(*[four_sources(factors, located[4 * slot : 4 * slot + 4]) for slot in range(4)])
    weight = rows(
        *[pick([placed(weights, located[4 * slot + m], slot) for slot in range(4)]) for m in range(4)]
    )
    return cluster_sums(interact(two_targets(anchors), sources, weight))


def cluster_sums(total):
    total = total.T
    return lanes(
        total[:16] + total[16:32] + total[32:48] + total[48:64],
        total[64:80] + total[80:96] + total[96:112] + total[112:],
    )


def locate(entry, first, last, base, empty):
    inside = jnp.minimum(jnp.maximum(entry - first, 0), last)
    return jnp.where(entry < 0, empty, base + inside)


FINE_BASE = [0, 44, 72]
FINE_EMPTY = 92


def fine_kernel(
    device,
    lists,
    anchors_hbm,
    moments_hbm,
    inner_hbm,
    outer_hbm,
    far_hbm,
    anchors,
    moments,
    inner,
    outer,
    far,
    held_anchors,
    held_moments,
    factors,
    weights,
    semaphores,
):
    me = device[0]
    loads = started(
        semaphores,
        (anchors_hbm, anchors),
        (moments_hbm, moments),
        (inner_hbm, inner),
        (outer_hbm, outer),
    )
    for copy in loads:
        copy.wait()
    odd = (me & 1) == 1
    start = 0
    for height in range(3):
        width = (LEAVES_DEV >> height) * RANK
        wide = REACH * RANK
        rim = slice(RIM[height], RIM[height] + wide)
        own = slice(COLUMN[height], COLUMN[height] + width)
        far_end = start + wide + width
        for held, whole, row in (
            (held_anchors, anchors, slice(0, DIM)),
            (held_moments, moments, slice(DIM, 2 * DIM)),
        ):
            held[:, start + wide : far_end] = whole[:, own]
            inner_at = pl.multiple_of(jnp.where(odd, start, far_end), 128)
            outer_at = pl.multiple_of(jnp.where(odd, far_end, start), 128)
            held[:, pl.ds(inner_at, wide)] = inner[row, rim]
            held[:, pl.ds(outer_at, wide)] = outer[row, rim]
        start = far_end + wide
    held_anchors[:, start:] = jnp.zeros((DIM, 48 * 128 - start), f32)
    held_moments[:, start:] = jnp.zeros((DIM, 48 * 128 - start), f32)
    prepare_factors(held_anchors, factors, 12)
    prepare_weights(held_moments, weights, 12)

    for height in range(3):
        number = LEAVES_DEV >> height

        def one_pair(q, carry, height=height, number=number):
            first = me * number - REACH
            located = []
            for cluster in range(2):
                for j in range(8):
                    entry = lists[2 * LEAVES_DEV - 2 * number + 2 * q + cluster, j]
                    located.append(
                        locate(entry, first, number + 2 * REACH - 1, FINE_BASE[height], FINE_EMPTY)
                    )
            columns = pl.ds(pl.multiple_of(COLUMN[height] + q * 128, 128), 128)
            far[:, columns] = two_clusters(anchors[:, columns], factors, weights, located)
            return carry

        lax.fori_loop(0, number // 2, one_pair, 0, unroll=4)
    for copy in started(semaphores, (far, far_hbm)):
        copy.wait()


def fine_call(*arguments):
    return pl.pallas_call(
        fine_kernel,
        out_shape=jax.ShapeDtypeStruct((RHS, 56 * RANK), f32),
        in_specs=[SMEM, SMEM] + [HBM] * 4,
        out_specs=HBM,
        scratch_shapes=[
            pltpu.VMEM((DIM, 4096), f32),
            pltpu.VMEM((RHS, 4096), f32),
            pltpu.VMEM((32, RIM_WIDTH), f32),
            pltpu.VMEM((32, 2048), f32),
            pltpu.VMEM((RHS, 56 * RANK), f32),
            pltpu.VMEM((DIM, 48 * 128), f32),
            pltpu.VMEM((RHS, 48 * 128), f32),
            pltpu.VMEM((96, 64, 128), bf16),
            pltpu.VMEM((4, 12, 2, 64, 128), bf16),
            pltpu.SemaphoreType.DMA((4,)),
        ],
        compiler_params=pltpu.CompilerParams(vmem_limit_bytes=VMEM_LIMIT),
        cost_estimate=pl.CostEstimate(flops=5 * 10**9, bytes_accessed=2**22, transcendentals=0),
        name="fine",
    )(*arguments)


COARSE_EMPTY = 30


def coarse_kernel(
    device,
    lists,
    top_lists,
    tables_hbm,
    anchors_hbm,
    moments_hbm,
    inner_hbm,
    outer_hbm,
    beyond_hbm,
    third_hbm,
    top_hbm,
    incoming_hbm,
    matrices_hbm,
    far_hbm,
    basis_hbm,
    near_hbm,
    out_hbm,
    tables,
    anchors,
    moments,
    inner,
    outer,
    beyond,
    third,
    top_anchors,
    incoming,
    matrices,
    far,
    basis,
    near,
    out,
    held_anchors,
    held_moments,
    factors,
    weights,
    expansion,
    staged,
    formed,
    semaphores,
):
    me = device[0]
    loads = started(
        semaphores,
        (anchors_hbm, anchors),
        (moments_hbm, moments),
        (inner_hbm.at[:, 1152:], inner),
        (outer_hbm.at[:, 1152:], outer),
        (beyond_hbm, beyond),
        (third_hbm, third),
        (top_hbm, top_anchors),
        (tables_hbm.at[me], tables),
        (incoming_hbm, incoming),
        (matrices_hbm, matrices),
        (far_hbm, far),
        (basis_hbm, basis),
        (near_hbm, near),
    )
    for copy in loads[:6]:
        copy.wait()
    odd = (me & 1) == 1

    def at(column):
        return slice(column, column + 128)

    def place(on_inner, source, column, low_place, high_place):
        below = odd if on_inner else jnp.logical_not(odd)
        target = pl.multiple_of(jnp.where(below, low_place, high_place) * 128, 128)
        held_anchors[:, pl.ds(target, 128)] = source[:DIM, column]
        held_moments[:, pl.ds(target, 128)] = source[DIM:, column]

    def nearest(on_inner, column):
        below = odd if on_inner else jnp.logical_not(odd)
        return pl.ds(pl.multiple_of(column + jnp.where(below, 128, 0), 128), 128)

    for on_inner, source in ((True, inner), (False, outer)):
        place(on_inner, source, at(0), 1, 5)
        place(on_inner, source, at(128), 2, 6)
        place(on_inner, source, at(256), 10, 12)
    place(False, outer, nearest(False, 512), 0, 7)
    place(False, outer, at(768), 9, 13)
    place(False, third, at(0), 8, 14)
    place(True, beyond, nearest(True, 0), 0, 7)
    place(True, beyond, at(256), 9, 13)
    place(True, beyond, at(768), 8, 14)
    for index, column in ((3, 3584), (4, 3712), (11, 3840)):
        held_anchors[:, at(128 * index)] = anchors[:, at(column)]
        held_moments[:, at(128 * index)] = moments[:, at(column)]
    held_anchors[:, at(128 * 15)] = jnp.zeros((DIM, 128), f32)
    held_moments[:, at(128 * 15)] = jnp.zeros((RHS, 128), f32)
    prepare_factors(held_anchors, factors, 4)
    prepare_weights(held_moments, weights, 4)

    def local_pair(height, q, base):
        number = LEAVES_DEV >> height
        located = []
        for cluster in range(2):
            for j in range(8):
                entry = lists[2 * LEAVES_DEV - 2 * number + 2 * q + cluster, j]
                located.append(
                    locate(entry, me * number - REACH, number + 2 * REACH - 1, base, COARSE_EMPTY)
                )
        return two_clusters(
            anchors[:, at(COLUMN[height] + 128 * q)], factors, weights, located
        )

    far_third = [local_pair(3, q, 0) for q in range(2)]
    far_fourth = local_pair(4, 0, 16)

    loads[8].wait()
    loads[9].wait()
    loads[7].wait()

    lane = lax.broadcasted_iota(jnp.int32, (8, 128), 1)

    def two_blocks(first, second):
        return rows(
            jnp.where(lane < RANK, first, pltpu.roll(second, RANK, 1)),
            jnp.where(lane < RANK, pltpu.roll(first, RANK, 1), second),
        )

    sixth = [
        jnp.sum(incoming[64 * c : 64 * (c + 1), 8 * (SLOTS - 1) : 8 * SLOTS, :], axis=0)
        for c in range(2)
    ]
    seventh = lifted(two_blocks(*sixth), matrices[RANK * (LOCAL + 7) : RANK * (LOCAL + 9), :])
    seventh = as_block(seventh)

    def held(kind, other):
        slot = tables[SENT // 128 + kind, other]
        return slot, incoming[other, pl.ds(pl.multiple_of((slot & 3) * 8, 8), 8), :]

    for index, shift in enumerate(FORMED):
        other = jnp.minimum(jnp.maximum(me + shift, 0), DEVICES - 1)
        value = two_blocks(held(1, other)[1], jnp.zeros((8, 128), f32))[:, :RANK]
        start = RANK * (LOCAL + 9 + index)
        formed[index] = as_block(lifted(value, matrices[start : start + RANK, :]))

    entries = [[lists[62, j] for j in range(8)]]
    for level in range(1, TOP + 1):
        row = DEVICES - (DEVICES >> (level - 1)) + (me >> level)
        entries.append([top_lists[row, j] for j in range(8)])

    def block(level, entry):
        if level == TOP:
            return jnp.where(entry == 0, seventh, 0.0)
        if level == SHARED:
            return jnp.where(entry == 0, sixth[0], jnp.where(entry == 1, sixth[1], 0.0))
        first = jnp.maximum(entry, 0) << level

        def add(i, total):
            slot, value = held(level, first + i)
            if level == 2:
                value = jnp.where(slot < SLOTS, value, formed[slot & 3])
            return total + value

        count = jnp.where(entry < 0, 0, 1 << level)
        return lax.fori_loop(0, count, add, jnp.zeros((8, 128), f32))

    wanted = [0] + [DEVICES - (DEVICES >> (level - 1)) + (me >> level) for level in range(1, TOP + 1)]
    for level in range(1, TOP + 1):
        first = DEVICES - (DEVICES >> (level - 1))
        wanted += [first + jnp.maximum(entry, 0) for entry in entries[level]]
    columns = []
    loads[6].wait()
    for group in range(8):
        part = wanted[8 * group : 8 * group + 8]
        regrouped(lambda c: top_anchors[pl.ds(part[c], 1), :], staged.at[group % 2], 8, 8)
        columns += eight_anchors([tile(staged.at[group % 2], c, 8) for c in range(8)])

    far_chain = []
    for unit in range(4):
        pairs = []
        for level in (2 * unit, 2 * unit + 1):
            sums = [block(level, entry) for entry in entries[level]]
            pairs += [two_blocks(sums[2 * j], sums[2 * j + 1]) for j in range(4)]
        weight = []
        for h in range(2):
            parts = []
            for slot in range(4):
                high = pairs[2 * slot + h].astype(bf16).astype(f32)
                parts += [high, pairs[2 * slot + h] - high]
            weight.append(rows(*parts).T.astype(bf16))
        own = columns[unit]
        sources = []
        for level in (2 * unit, 2 * unit + 1):
            for h in range(2):
                if level == 0:
                    found = [
                        held(SHARED, jnp.maximum(entry, 0))[1] for entry in entries[0][4 * h : 4 * h + 4]
                    ]
                    pair = lanes(two_blocks(found[0], found[1]), two_blocks(found[2], found[3]))
                else:
                    pair = lanes(*columns[4 * level + 2 * h : 4 * level + 2 * h + 2])
                sources.append(source_side(pair).astype(bf16))
        if unit == 0:
            own = halves(anchors[:, at(COLUMN[5])], own)
        result = cluster_sums(interact(two_targets(own), rows(*sources), rows(*weight)))
        far_chain += [result[:, :RANK], result[:, RANK:]]

    def pushed(value, matrix):
        high, low = split(matrix)
        return folded(dot_nt(narrow(value), lanes(high, low)))

    value = far_chain[TOP]
    for level in range(TOP - 1, -1, -1):
        value = far_chain[level] + pushed(value, matrices[RANK * (LOCAL + level) : RANK * (LOCAL + level + 1), :])

    def children(parent, height, q):
        start = (ROW[height] + 2 * q) * RANK
        return pushed(parent, matrices[start : start + 128, :])

    loads[10].wait()
    upper = [far_fourth + children(value, 4, 0)]
    for height in (3, 2, 1, 0):
        lower = []
        for q, slab in enumerate(upper):
            for side in range(2):
                parent = slab[:, RANK * side : RANK * (side + 1)]
                index = 2 * q + side
                if height == 3:
                    own = far_third[index]
                else:
                    own = far[:, at(COLUMN[height] + 128 * index)]
                lower.append(own + children(parent, height, index))
        upper = lower
    for q, slab in enumerate(upper):
        expansion[:, at(128 * q)] = slab

    def two_leaves(q, carry):
        slab = expansion[:, pl.ds(pl.multiple_of(q * 128, 128), 128)]
        for leaf in range(2):
            columns = pl.ds(pl.multiple_of(q * 256 + leaf * 128, 128), 128)
            high, low = split(basis[:, columns])
            own = slab[:, RANK * leaf : RANK * (leaf + 1)]
            out[:, columns] = near[:, columns] + folded(dot(narrow(own), rows(high, low)))
        return carry

    loads[11].wait()
    loads[12].wait()
    stores = []
    for part in range(2):
        lax.fori_loop(8 * part, 8 * part + 8, two_leaves, 0, unroll=8)
        own = slice(2048 * part, 2048 * part + 2048)
        stores += started(semaphores.at[13 + part :], (out.at[:, own], out_hbm.at[:, own]))
    for copy in stores:
        copy.wait()


def coarse_call(*arguments):
    return pl.pallas_call(
        coarse_kernel,
        out_shape=jax.ShapeDtypeStruct((RHS, LEAVES_DEV * LEAF), f32),
        in_specs=[SMEM] * 3 + [HBM] * 13,
        out_specs=HBM,
        scratch_shapes=[
            pltpu.SMEM((TABLE, 128), jnp.int32),
            pltpu.VMEM((DIM, 4096), f32),
            pltpu.VMEM((RHS, 4096), f32),
            pltpu.VMEM((32, 512), f32),
            pltpu.VMEM((32, 896), f32),
            pltpu.VMEM((32, 896), f32),
            pltpu.VMEM((32, 128), f32),
            pltpu.VMEM((127, RANK * DIM), f32),
            pltpu.VMEM((DEVICES, 8 * SLOTS, 128), f32),
            pltpu.VMEM((MATRICES * RANK, RANK), f32),
            pltpu.VMEM((RHS, 56 * RANK), f32),
            pltpu.VMEM((RANK, 4096), f32),
            pltpu.VMEM((RHS, 4096), f32),
            pltpu.VMEM((RHS, 4096), f32),
            pltpu.VMEM((DIM, 16 * 128), f32),
            pltpu.VMEM((RHS, 16 * 128), f32),
            pltpu.VMEM((32, 64, 128), bf16),
            pltpu.VMEM((4, 4, 2, 64, 128), bf16),
            pltpu.VMEM((RHS, 2048), f32),
            pltpu.VMEM((2, 64, 128), f32),
            pltpu.VMEM((4, 8, 128), f32),
            pltpu.SemaphoreType.DMA((15,)),
        ],
        compiler_params=pltpu.CompilerParams(vmem_limit_bytes=VMEM_LIMIT),
        cost_estimate=pl.CostEstimate(flops=10**9, bytes_accessed=2**23, transcendentals=0),
        name="coarse",
    )(*arguments)


def exchanged(value, mate):
    pairs = []
    for device in range(DEVICES):
        other = mate(device)
        pairs.append((device, other if 0 <= other < DEVICES else device))
    return lax.ppermute(value, "leaf", pairs)


def inner_mate(device):
    return device + 1 if device % 2 == 0 else device - 1


def outer_mate(device):
    return device - 1 if device % 2 == 0 else device + 1


def third_mate(device):
    return device - 3 if device % 2 == 0 else device + 3


def on_device(
    points,
    charges,
    leaf_basis,
    local_transfer,
    local_anchors,
    local_lists,
    near_blocks,
    top_transfer,
    top_anchors,
    top_lists,
):
    index = lax.axis_index("leaf")
    device = index.reshape(1)
    half = NREACH * LEAF
    lower = (index & 1) * half

    def edge(start):
        return jnp.concatenate(
            [lax.dynamic_slice_in_dim(array, start, half, 1) for array in (points, charges)], axis=0
        )

    inner_edge, outer_edge, device = lax.optimization_barrier(
        (edge(half - lower), edge(lower), device)
    )
    inner_leaves = exchanged(inner_edge, inner_mate)
    outer_leaves = exchanged(outer_edge, outer_mate)

    tables = jnp.asarray(slot_tables())
    moments, anchors, inner_rim, outer_rim, third, outgoing, matrices = moments_call(
        device, tables, leaf_basis, charges, local_transfer, local_anchors, top_transfer
    )
    outgoing, inner_leaves, outer_leaves = lax.optimization_barrier(
        (outgoing, inner_leaves, outer_leaves)
    )
    inner = exchanged(inner_rim, inner_mate)
    incoming = lax.all_to_all(outgoing, "leaf", 0, 0)
    outer = exchanged(
        jnp.concatenate([outer_rim, inner[:, RIM[3] : RIM[5]]], axis=1), outer_mate
    )
    third = exchanged(third, third_mate)
    near = near_call(device, near_blocks, points, charges, inner_leaves, outer_leaves)
    near, outer = lax.optimization_barrier((near, outer))
    beyond = exchanged(outer[:, RIM[3] :], inner_mate)
    far = fine_call(device, local_lists, anchors, moments, inner, outer)
    return coarse_call(
        device,
        local_lists,
        top_lists,
        tables,
        anchors,
        moments,
        inner,
        outer,
        beyond,
        third,
        top_anchors,
        incoming,
        matrices,
        far,
        leaf_basis,
        near,
    )


def solution(mesh):
    in_specs = (
        P(None, "leaf"),
        P(None, "leaf"),
        P(None, "leaf"),
        P("leaf", None),
        P("leaf", None),
        P("leaf", None),
        P("leaf", None),
        P(),
        P(),
        P(),
    )
    out_specs = P(None, "leaf")
    return jax.shard_map(
        on_device, mesh=mesh, in_specs=in_specs, out_specs=out_specs, check_vma=False
    )
```

```python
import math

import jax
import jax.numpy as jnp
import numpy as np
from jax import lax
from jax.experimental import pallas as pl
from jax.experimental.pallas import tpu as pltpu
from jax.sharding import PartitionSpec as P

DIM = 16
RHS = 16
LEAF = 128
RANK = 64
LEAVES_DEV = 32
NREACH = 16
REACH = 6
DEVICES = 128
TOP = 7
SHARED = 6
SLOTS = 3
SUMMIT_ROW = 124
NOTHING = 7
ANCHORS = 8
FORMED = (-6, -5, 5, 6)
LOCAL = 62
MATRICES = LOCAL + 13

bf16 = jnp.bfloat16
f32 = jnp.float32
SCALE = math.log2(math.e) / math.sqrt(3.0)
LN2 = math.log(2.0)
TINY = 1e-30

COLUMN = [0, 2048, 3072, 3584, 3840, 3968]
ROW = [0, 32, 48, 56, 60]
RIM = [0, 384, 768, 1152, 1408, 1536]
RIM_WIDTH = 1664
LOW_PIECES = [(0, 384), (2048, 2432), (3072, 3456), (3584, 4096)]
HIGH_PIECES = [(1664, 2048), (2688, 3072), (3200, 4096)]
VMEM_LIMIT = 60 * 2**20
VMEM = pl.BlockSpec(memory_space=pltpu.VMEM)
SMEM = pl.BlockSpec(memory_space=pltpu.SMEM)
HBM = pl.BlockSpec(memory_space=pltpu.HBM)


def relevant(first, second, level):
    return 2 <= abs((first >> level) - (second >> level)) <= REACH


def slot_tables():
    sent = np.full((DEVICES, SLOTS, DEVICES), NOTHING, np.int32)
    held = np.zeros((DEVICES, SHARED + 1, DEVICES), np.int32)
    for first in range(DEVICES):
        for second in range(DEVICES):
            levels = [level for level in range(SHARED) if relevant(first, second, level)]
            if levels and levels[0] == 0:
                if len(levels) == 3:
                    levels.pop()
                    held[first, 2, second] = 4 + FORMED.index(second - first)
                levels.append(ANCHORS)
            for slot, level in enumerate(levels):
                sent[first, slot, second] = level
                held[first, SHARED if level == ANCHORS else level, second] = slot
    return np.concatenate([sent, held], axis=1)


TABLE = SLOTS + SHARED + 1


def started(semaphores, *pairs):
    copies = []
    for index, (source, target) in enumerate(pairs):
        copy = pltpu.make_async_copy(source, target, semaphores.at[index])
        copy.start()
        copies.append(copy)
    return copies


def split(x):
    high = x.astype(bf16)
    return high, (x - high.astype(f32)).astype(bf16)


def lanes(*parts):
    return jnp.concatenate(parts, axis=1)


def rows(*parts):
    return jnp.concatenate(parts, axis=0)


def dot(a, b):
    return jnp.dot(a, b, preferred_element_type=f32)


def dot_nt(a, b):
    return lax.dot_general(a, b, (((1,), (1,)), ((), ())), preferred_element_type=f32)


def narrow(x):
    high, low = split(x)
    return rows(lanes(high, high), lanes(low, low))


def folded(x):
    return x[:16] + x[16:]


def sides(x):
    x = x * SCALE
    high = x.astype(bf16).astype(f32)
    low = (x - high).astype(bf16).astype(f32)
    norm = jnp.sum(high * (high + 2.0 * low), axis=0, keepdims=True)
    norm_high = norm.astype(bf16).astype(f32)
    norm_middle = (norm - norm_high).astype(bf16).astype(f32)
    norm_low = norm - norm_high - norm_middle
    row = lax.broadcasted_iota(jnp.int32, x.shape, 0)
    parts = jnp.where(row % 3 == 0, norm_high, jnp.where(row % 3 == 1, norm_middle, norm_low))
    return high, low, parts, row


def source_side(x):
    high, low, parts, row = sides(x)
    tail = jnp.where(row < 3, 1.0, jnp.where(row < 6, parts, 0.0))
    return rows(high, high, low, tail)


def target_sides(x):
    high, low, parts, row = sides(x)
    tail = jnp.where(row < 3, parts, jnp.where(row < 6, 1.0, 0.0))
    factors = rows(-2.0 * high, -2.0 * low, -2.0 * high, tail)
    first = rows(factors, jnp.zeros_like(factors)).T
    return first.astype(bf16), pltpu.roll(first, RANK, 1).astype(bf16)


def matern(squared):
    squared = jnp.maximum(squared, TINY)
    distance = squared * lax.rsqrt(squared)
    return (1.0 + LN2 * distance) * jnp.exp2(-distance)


def pick(parts):
    lane = lax.broadcasted_iota(jnp.int32, parts[0].shape, 1)
    result = parts[3]
    for j in (2, 1, 0):
        result = jnp.where(lane < 32 * (j + 1), parts[j], result)
    return result


def interact(targets, sources, weights):
    kernel = matern(dot(targets, sources))
    high, low = split(kernel)
    size = kernel.shape[0]
    result = dot(rows(high, low), weights)
    quarter = size // 4
    return pick(
        [
            result[quarter * j : quarter * (j + 1)]
            + result[size + quarter * j : size + quarter * (j + 1)]
            for j in range(4)
        ]
    )


def weight_turns(slabs):
    parts = []
    for slab in slabs:
        high = slab.astype(bf16).astype(f32)
        parts += [high, slab - high]
    columns = rows(*parts).T
    return [
        (columns if turn == 0 else pltpu.roll(columns, 32 * turn, 1)).astype(bf16)
        for turn in range(4)
    ]


def halves(first, second):
    lane = lax.broadcasted_iota(jnp.int32, first.shape, 1)
    return jnp.where(lane < RANK, first, second)


def regrouped(load, staged, count, width):
    for c in range(count):
        value = load(c)
        for i in range(width):
            staged[8 * i + c : 8 * i + c + 1, :] = value[:, 128 * i : 128 * (i + 1)]


def tile(staged, c, width):
    return staged[pl.ds(c, width, stride=8), :]


def store_matrix(staged, c, matrices, index):
    value = tile(staged, c, 32)
    matrices[pl.ds(RANK * index, 32, stride=2), :] = value[:, :RANK]
    matrices[pl.ds(RANK * index + 1, 32, stride=2), :] = value[:, RANK:]


def eight_anchors(tiles):
    group = lax.broadcasted_iota(jnp.int32, (8, 128), 1) // 16
    for bit in (1, 2, 4):
        turned = list(tiles)
        for p in range(8):
            if p & bit == 0:
                first, second = tiles[p], tiles[p | bit]
                turned[p] = jnp.where(group & bit == 0, first, pltpu.roll(second, 16 * bit, 1))
                turned[p | bit] = jnp.where(
                    group & bit == 0, pltpu.roll(first, 128 - 16 * bit, 1), second
                )
        tiles = turned
    held = rows(*tiles).T
    slabs = [lanes(held[32 * q : 32 * q + 16], held[32 * q + 16 : 32 * q + 32]) for q in range(4)]
    value = rows(*slabs)
    high = value.astype(bf16)
    rest = value - high.astype(f32)
    middle = rest.astype(bf16)
    low = (rest - middle.astype(f32)).astype(bf16)
    row = lax.broadcasted_iota(jnp.int32, (128, 128), 0)
    column = lax.broadcasted_iota(jnp.int32, (128, 128), 1)
    order = (row & RANK) + 8 * (row & 7) + ((row & 63) >> 3)
    order = jnp.where(order == column, 1.0, 0.0).astype(bf16)
    value = dot(rows(high, middle, low), order)
    value = value[:64] + (value[64:128] + value[128:])
    return [value[16 * q : 16 * (q + 1)] for q in range(4)]


def lifted(slab, matrices):
    high, low = split(matrices)
    return folded(dot(narrow(slab), rows(high, low)))


def as_block(value):
    return lanes(value[:8], value[8:])


def moments_kernel(
    device,
    tables_hbm,
    basis_hbm,
    charges_hbm,
    transfer_hbm,
    anchors_hbm,
    top_hbm,
    moments_out,
    anchors_out,
    inner_out,
    outer_out,
    third,
    summit,
    outgoing_out,
    matrices_out,
    tables,
    basis,
    charges,
    transfer,
    anchor_rows,
    top_transfer,
    moments,
    anchors,
    inner,
    outer,
    outgoing,
    matrices,
    blocks,
    staged,
    staged_anchors,
    semaphores,
):
    me = device[0]
    quarters = [slice(1024 * i, 1024 * (i + 1)) for i in range(4)]
    loads = started(
        semaphores,
        (charges_hbm, charges),
        *[(basis_hbm.at[:, part], basis.at[:, part]) for part in quarters],
        (transfer_hbm, transfer),
        (anchors_hbm, anchor_rows),
        (tables_hbm.at[me], tables),
    )
    chain = [2 * DEVICES - (2 * DEVICES >> level) + (me >> level) for level in range(TOP)]
    chain += [252, 253]
    for shift in FORMED:
        other = jnp.minimum(jnp.maximum(me + shift, 0), DEVICES - 1)
        chain.append(DEVICES + (other >> 1))
    chain_loads = started(
        semaphores.at[18:],
        *[
            (top_hbm.at[pl.ds(row, 1), :], top_transfer.at[pl.ds(index, 1), :])
            for index, row in enumerate(chain)
        ],
    )
    loads[0].wait()

    def two_leaves(q, carry):
        parts = []
        for leaf in range(2):
            columns = pl.ds(pl.multiple_of(q * 256 + leaf * 128, 128), 128)
            high, low = split(basis[:, columns])
            parts.append(folded(dot_nt(narrow(charges[:, columns]), lanes(high, low))))
        moments[:, pl.ds(pl.multiple_of(q * 128, 128), 128)] = lanes(*parts)
        return carry

    for part in range(4):
        loads[1 + part].wait()
        lax.fori_loop(4 * part, 4 * part + 4, two_leaves, 0, unroll=4)

    loads[5].wait()
    for group in range(8):
        count = min(8, LOCAL - 8 * group)
        for i in range(32):
            staged[group % 2, 8 * i : 8 * i + count, :] = transfer[
                8 * group : 8 * group + count, 128 * i : 128 * (i + 1)
            ]
        for c in range(count):
            store_matrix(staged.at[group % 2], c, matrices, 8 * group + c)
    for copy in chain_loads:
        copy.wait()
    for group in range(2):
        count = min(8, 13 - 8 * group)
        for i in range(32):
            staged[group, 8 * i : 8 * i + count, :] = top_transfer[
                8 * group : 8 * group + count, 128 * i : 128 * (i + 1)
            ]
        for c in range(count):
            store_matrix(staged.at[group], c, matrices, LOCAL + 8 * group + c)
    stores = started(semaphores.at[9:], (matrices, matrices_out))

    loads[6].wait()
    for group in range(8):
        count = min(8, 63 - 8 * group)
        for i in range(8):
            staged_anchors[group % 2, 8 * i : 8 * i + count, :] = anchor_rows[
                8 * group : 8 * group + count, 128 * i : 128 * (i + 1)
            ]
        tiles = [tile(staged_anchors.at[group % 2], c, 8) for c in range(count)]
        tiles += [jnp.zeros((8, 128), f32)] * (8 - count)
        for q, slab in enumerate(eight_anchors(tiles)):
            anchors[:, 512 * group + 128 * q : 512 * group + 128 * (q + 1)] = slab

    for height in range(5):
        number = LEAVES_DEV >> height
        parents = []
        for q in range(number // 2):
            start = (ROW[height] + 2 * q) * RANK
            slab = moments[:, COLUMN[height] + 128 * q : COLUMN[height] + 128 * (q + 1)]
            parents.append(lifted(slab, matrices[start : start + 128, :]))
        if height == 4:
            parents.append(jnp.zeros((16, RANK), f32))
        for q in range(len(parents) // 2):
            start = COLUMN[height + 1] + 128 * q
            moments[:, start : start + 128] = lanes(parents[2 * q], parents[2 * q + 1])

    even = (me & 1) == 0

    def fill(low_rim, high_rim):
        for row, value in ((slice(0, DIM), anchors), (slice(DIM, 2 * DIM), moments)):
            for rim, parts in ((low_rim, LOW_PIECES), (high_rim, HIGH_PIECES)):
                start = 0
                for first, last in parts:
                    rim[row, start : start + last - first] = value[:, first:last]
                    start += last - first

    @pl.when(even)
    def _():
        fill(outer, inner)

    @pl.when(jnp.logical_not(even))
    def _():
        fill(inner, outer)

    third[:DIM, :] = anchors[:, 3840:3968]
    third[DIM:, :] = moments[:, 3840:3968]
    stores += started(
        semaphores.at[10:],
        (inner, inner_out),
        (outer, outer_out),
        (moments, moments_out),
        (anchors, anchors_out),
    )

    value = moments[:, COLUMN[5] : COLUMN[5] + RANK]
    for level in range(SHARED + 1):
        blocks[level] = as_block(value)
        if level < SHARED:
            start = RANK * (LOCAL + level)
            value = lifted(value, matrices[start : start + RANK, :])
    blocks[NOTHING] = jnp.zeros((8, 128), f32)
    for half in range(2):
        summit[half] = jnp.where(me >> SHARED == half, blocks[SHARED], 0.0)
    blocks[ANCHORS] = as_block(anchors[:, COLUMN[5] : COLUMN[5] + RANK])

    def one_device(other, carry):
        for slot in range(SLOTS):
            outgoing[other, 8 * slot : 8 * (slot + 1), :] = blocks[tables[slot, other]]
        return carry

    loads[7].wait()
    for part in range(4):
        lax.fori_loop(32 * part, 32 * part + 32, one_device, 0, unroll=8)
        own = slice(32 * part, 32 * part + 32)
        stores += started(semaphores.at[14 + part :], (outgoing.at[own], outgoing_out.at[own]))
    for copy in stores:
        copy.wait()


def moments_call(*arguments):
    shape = jax.ShapeDtypeStruct
    return pl.pallas_call(
        moments_kernel,
        out_shape=(
            shape((16, 4096), f32),
            shape((16, 4096), f32),
            shape((32, RIM_WIDTH), f32),
            shape((32, RIM_WIDTH), f32),
            shape((32, 128), f32),
            shape((2, 8, 128), f32),
            shape((DEVICES, 8 * SLOTS, 128), f32),
            shape((MATRICES * RANK, RANK), f32),
        ),
        in_specs=[SMEM] + [HBM] * 6,
        out_specs=(HBM, HBM, HBM, HBM, VMEM, VMEM, HBM, HBM),
        scratch_shapes=[
            pltpu.SMEM((TABLE, 128), jnp.int32),
            pltpu.VMEM((RANK, 4096), f32),
            pltpu.VMEM((RHS, 4096), f32),
            pltpu.VMEM((LOCAL, RANK * RANK), f32),
            pltpu.VMEM((63, RANK * DIM), f32),
            pltpu.VMEM((16, RANK * RANK), f32),
            pltpu.VMEM((RHS, 4096), f32),
            pltpu.VMEM((DIM, 4096), f32),
            pltpu.VMEM((32, RIM_WIDTH), f32),
            pltpu.VMEM((32, RIM_WIDTH), f32),
            pltpu.VMEM((DEVICES, 8 * SLOTS, 128), f32),
            pltpu.VMEM((MATRICES * RANK, RANK), f32),
            pltpu.VMEM((9, 8, 128), f32),
            pltpu.VMEM((2, 256, 128), f32),
            pltpu.VMEM((2, 64, 128), f32),
            pltpu.SemaphoreType.DMA((31,)),
        ],
        compiler_params=pltpu.CompilerParams(vmem_limit_bytes=VMEM_LIMIT),
        cost_estimate=pl.CostEstimate(flops=10**9, bytes_accessed=2**22, transcendentals=0),
        name="moments",
    )(*arguments)


def near_kernel(
    device,
    near_blocks,
    points_hbm,
    charges_hbm,
    inner_hbm,
    outer_hbm,
    out_hbm,
    points,
    charges,
    inner,
    outer,
    out,
    factors,
    weights,
    semaphores,
):
    me = device[0]
    loads = started(
        semaphores,
        (points_hbm, points),
        (charges_hbm, charges),
        (inner_hbm, inner),
        (outer_hbm, outer),
    )

    def prepare(point_ref, charge_ref, charge_row, first):
        def four_leaves(i, carry):
            columns = pl.ds(pl.multiple_of(i * 512, 512), 512)
            side = source_side(point_ref[:DIM, columns]).astype(bf16)
            charge = charge_ref[charge_row : charge_row + RHS, columns]
            slabs = []
            for m in range(4):
                factors[(first + i) * 4 + m] = side[:, 128 * m : 128 * (m + 1)]
                slabs.append(charge[:, 128 * m : 128 * (m + 1)])
            for turn, value in enumerate(weight_turns(slabs)):
                weights[turn, first + i] = value
            return carry

        return four_leaves

    loads[0].wait()
    loads[1].wait()
    lax.fori_loop(0, 8, prepare(points, charges, 0, 4), 0, unroll=8)
    side = (me & 1) * 12
    loads[2].wait()
    lax.fori_loop(0, 4, prepare(inner, inner, DIM, 12 - side), 0, unroll=4)
    loads[3].wait()
    lax.fori_loop(0, 4, prepare(outer, outer, DIM, side), 0, unroll=4)
    factors[64] = jnp.zeros((64, 128), bf16)
    for turn in range(4):
        weights[turn, 16] = jnp.zeros((128, 128), bf16)
    first_leaf = me * LEAVES_DEV - NREACH

    def one_leaf(t, carry):
        columns = pl.ds(pl.multiple_of(t * 128, 128), 128)
        front, back = target_sides(points[:, columns])
        empty = jnp.zeros_like(front)
        targets = rows(
            lanes(front, empty), lanes(back, empty), lanes(empty, front), lanes(empty, back)
        )
        located = []
        for j in range(8):
            block = near_blocks[j, t]
            inside = jnp.minimum(jnp.maximum(block - first_leaf, 0), 63)
            located.append(jnp.where(block < 0, 64, inside))
        sources = rows(
            *[lanes(factors[located[2 * j]], factors[located[2 * j + 1]]) for j in range(4)]
        )
        weight = rows(
            *[
                pick([weights[(j - located[2 * j + h]) & 3, located[2 * j + h] >> 2] for j in range(4)])
                for h in range(2)
            ]
        )
        total = interact(targets, sources, weight).T
        out[:, columns] = sum(total[16 * g : 16 * (g + 1)] for g in range(8))
        return carry

    stores = []
    for part in range(2):
        lax.fori_loop(16 * part, 16 * part + 16, one_leaf, 0, unroll=16)
        own = slice(2048 * part, 2048 * part + 2048)
        stores += started(semaphores.at[4 + part :], (out.at[:, own], out_hbm.at[:, own]))
    for copy in stores:
        copy.wait()


def near_call(*arguments):
    return pl.pallas_call(
        near_kernel,
        out_shape=jax.ShapeDtypeStruct((RHS, LEAVES_DEV * LEAF), f32),
        in_specs=[SMEM, SMEM] + [HBM] * 4,
        out_specs=HBM,
        scratch_shapes=[
            pltpu.VMEM((DIM, LEAVES_DEV * LEAF), f32),
            pltpu.VMEM((RHS, LEAVES_DEV * LEAF), f32),
            pltpu.VMEM((DIM + RHS, NREACH * LEAF), f32),
            pltpu.VMEM((DIM + RHS, NREACH * LEAF), f32),
            pltpu.VMEM((RHS, LEAVES_DEV * LEAF), f32),
            pltpu.VMEM((65, 64, 128), bf16),
            pltpu.VMEM((4, 17, 128, 128), bf16),
            pltpu.SemaphoreType.DMA((6,)),
        ],
        compiler_params=pltpu.CompilerParams(vmem_limit_bytes=VMEM_LIMIT),
        cost_estimate=pl.CostEstimate(flops=10**10, bytes_accessed=2**22, transcendentals=0),
        name="near",
    )(*arguments)


def prepare_factors(anchors, factors, groups):
    def four_slabs(i, carry):
        side = source_side(anchors[:, pl.ds(pl.multiple_of(i * 512, 512), 512)])
        for m in range(4):
            slab = side[:, 128 * m : 128 * (m + 1)]
            turned = pltpu.roll(slab, RANK, 1)
            factors[(i * 4 + m) * 2] = halves(slab, turned).astype(bf16)
            factors[(i * 4 + m) * 2 + 1] = halves(turned, slab).astype(bf16)
        return carry

    lax.fori_loop(0, groups, four_slabs, 0, unroll=True)


def prepare_weights(moments, weights, groups):
    def four_slabs(i, carry):
        value = moments[:, pl.ds(pl.multiple_of(i * 512, 512), 512)]
        turns = weight_turns([value[:, 128 * m : 128 * (m + 1)] for m in range(4)])
        for turn in range(4):
            weights[turn, i, 0] = turns[turn][:RANK]
            weights[turn, i, 1] = turns[turn][RANK:]
        return carry

    lax.fori_loop(0, groups, four_slabs, 0, unroll=True)


def two_targets(anchors):
    front, back = target_sides(anchors)
    empty = jnp.zeros((RANK, 128), bf16)
    return rows(
        lanes(front[:RANK], empty),
        lanes(back[:RANK], empty),
        lanes(empty, front[RANK:]),
        lanes(empty, back[RANK:]),
    )


def four_sources(factors, located):
    return lanes(
        halves(factors[located[0]], factors[located[1]]),
        halves(factors[located[2]], factors[located[3]]),
    )


def placed(weights, index, slot):
    pair = index >> 1
    return weights[(slot - pair) & 3, pair >> 2, index & 1]


def two_clusters(anchors, factors, weights, located):
    sources = rows(*[four_sources(factors, located[4 * slot : 4 * slot + 4]) for slot in range(4)])
    weight = rows(
        *[pick([placed(weights, located[4 * slot + m], slot) for slot in range(4)]) for m in range(4)]
    )
    return cluster_sums(interact(two_targets(anchors), sources, weight))


def cluster_sums(total):
    total = total.T
    return lanes(
        total[:16] + total[16:32] + total[32:48] + total[48:64],
        total[64:80] + total[80:96] + total[96:112] + total[112:],
    )


def locate(entry, first, last, base, empty):
    inside = jnp.minimum(jnp.maximum(entry - first, 0), last)
    return jnp.where(entry < 0, empty, base + inside)


FINE_BASE = [0, 44, 72]
FINE_EMPTY = 92


def fine_kernel(
    device,
    lists,
    anchors_hbm,
    moments_hbm,
    inner_hbm,
    outer_hbm,
    far_hbm,
    anchors,
    moments,
    inner,
    outer,
    far,
    held_anchors,
    held_moments,
    factors,
    weights,
    semaphores,
):
    me = device[0]
    loads = started(
        semaphores,
        (anchors_hbm, anchors),
        (moments_hbm, moments),
        (inner_hbm, inner),
        (outer_hbm, outer),
    )
    for copy in loads:
        copy.wait()
    odd = (me & 1) == 1
    start = 0
    for height in range(3):
        width = (LEAVES_DEV >> height) * RANK
        wide = REACH * RANK
        rim = slice(RIM[height], RIM[height] + wide)
        own = slice(COLUMN[height], COLUMN[height] + width)
        far_end = start + wide + width
        for held, whole, row in (
            (held_anchors, anchors, slice(0, DIM)),
            (held_moments, moments, slice(DIM, 2 * DIM)),
        ):
            held[:, start + wide : far_end] = whole[:, own]
            inner_at = pl.multiple_of(jnp.where(odd, start, far_end), 128)
            outer_at = pl.multiple_of(jnp.where(odd, far_end, start), 128)
            held[:, pl.ds(inner_at, wide)] = inner[row, rim]
            held[:, pl.ds(outer_at, wide)] = outer[row, rim]
        start = far_end + wide
    held_anchors[:, start:] = jnp.zeros((DIM, 48 * 128 - start), f32)
    held_moments[:, start:] = jnp.zeros((DIM, 48 * 128 - start), f32)
    prepare_factors(held_anchors, factors, 12)
    prepare_weights(held_moments, weights, 12)

    for height in range(3):
        number = LEAVES_DEV >> height

        def one_pair(q, carry, height=height, number=number):
            first = me * number - REACH
            located = []
            for cluster in range(2):
                for j in range(8):
                    entry = lists[j, 2 * LEAVES_DEV - 2 * number + 2 * q + cluster]
                    located.append(
                        locate(entry, first, number + 2 * REACH - 1, FINE_BASE[height], FINE_EMPTY)
                    )
            columns = pl.ds(pl.multiple_of(COLUMN[height] + q * 128, 128), 128)
            far[:, columns] = two_clusters(anchors[:, columns], factors, weights, located)
            return carry

        lax.fori_loop(0, number // 2, one_pair, 0, unroll=True)
    for copy in started(semaphores, (far, far_hbm)):
        copy.wait()


def fine_call(*arguments):
    return pl.pallas_call(
        fine_kernel,
        out_shape=jax.ShapeDtypeStruct((RHS, 56 * RANK), f32),
        in_specs=[SMEM, SMEM] + [HBM] * 4,
        out_specs=HBM,
        scratch_shapes=[
            pltpu.VMEM((DIM, 4096), f32),
            pltpu.VMEM((RHS, 4096), f32),
            pltpu.VMEM((32, RIM_WIDTH), f32),
            pltpu.VMEM((32, 2048), f32),
            pltpu.VMEM((RHS, 56 * RANK), f32),
            pltpu.VMEM((DIM, 48 * 128), f32),
            pltpu.VMEM((RHS, 48 * 128), f32),
            pltpu.VMEM((96, 64, 128), bf16),
            pltpu.VMEM((4, 12, 2, 64, 128), bf16),
            pltpu.SemaphoreType.DMA((4,)),
        ],
        compiler_params=pltpu.CompilerParams(vmem_limit_bytes=VMEM_LIMIT),
        cost_estimate=pl.CostEstimate(flops=5 * 10**9, bytes_accessed=2**22, transcendentals=0),
        name="fine",
    )(*arguments)


COARSE_EMPTY = 30


def coarse_kernel(
    device,
    lists,
    top_lists,
    tables_hbm,
    anchors_hbm,
    moments_hbm,
    inner_hbm,
    outer_hbm,
    beyond_hbm,
    third_hbm,
    summit,
    top_hbm,
    incoming_hbm,
    matrices_hbm,
    far_hbm,
    basis_hbm,
    near_hbm,
    out_hbm,
    tables,
    anchors,
    moments,
    inner,
    outer,
    beyond,
    third,
    top_anchors,
    incoming,
    matrices,
    far,
    basis,
    near,
    out,
    held_anchors,
    held_moments,
    factors,
    weights,
    expansion,
    staged,
    formed,
    semaphores,
):
    me = device[0]
    loads = started(
        semaphores,
        (anchors_hbm, anchors),
        (moments_hbm, moments),
        (inner_hbm.at[:, 1152:], inner),
        (outer_hbm.at[:, 1152:], outer),
        (beyond_hbm, beyond),
        (third_hbm, third),
        (top_hbm, top_anchors),
        (tables_hbm.at[me], tables),
        (incoming_hbm, incoming),
        (matrices_hbm, matrices),
        (far_hbm, far),
        (basis_hbm, basis),
        (near_hbm, near),
    )
    for copy in loads[:6]:
        copy.wait()
    odd = (me & 1) == 1

    def at(column):
        return slice(column, column + 128)

    def place(on_inner, source, column, low_place, high_place):
        below = odd if on_inner else jnp.logical_not(odd)
        target = pl.multiple_of(jnp.where(below, low_place, high_place) * 128, 128)
        held_anchors[:, pl.ds(target, 128)] = source[:DIM, column]
        held_moments[:, pl.ds(target, 128)] = source[DIM:, column]

    def nearest(on_inner, column):
        below = odd if on_inner else jnp.logical_not(odd)
        return pl.ds(pl.multiple_of(column + jnp.where(below, 128, 0), 128), 128)

    for on_inner, source in ((True, inner), (False, outer)):
        place(on_inner, source, at(0), 1, 5)
        place(on_inner, source, at(128), 2, 6)
        place(on_inner, source, at(256), 10, 12)
    place(False, outer, nearest(False, 512), 0, 7)
    place(False, outer, at(768), 9, 13)
    place(False, third, at(0), 8, 14)
    place(True, beyond, nearest(True, 0), 0, 7)
    place(True, beyond, at(256), 9, 13)
    place(True, beyond, at(768), 8, 14)
    for index, column in ((3, 3584), (4, 3712), (11, 3840)):
        held_anchors[:, at(128 * index)] = anchors[:, at(column)]
        held_moments[:, at(128 * index)] = moments[:, at(column)]
    held_anchors[:, at(128 * 15)] = jnp.zeros((DIM, 128), f32)
    held_moments[:, at(128 * 15)] = jnp.zeros((RHS, 128), f32)
    prepare_factors(held_anchors, factors, 4)
    prepare_weights(held_moments, weights, 4)

    def local_pair(height, q, base):
        number = LEAVES_DEV >> height
        located = []
        for cluster in range(2):
            for j in range(8):
                entry = lists[j, 2 * LEAVES_DEV - 2 * number + 2 * q + cluster]
                located.append(
                    locate(entry, me * number - REACH, number + 2 * REACH - 1, base, COARSE_EMPTY)
                )
        return two_clusters(
            anchors[:, at(COLUMN[height] + 128 * q)], factors, weights, located
        )

    far_third = [local_pair(3, q, 0) for q in range(2)]
    far_fourth = local_pair(4, 0, 16)

    loads[8].wait()
    loads[9].wait()
    loads[7].wait()

    lane = lax.broadcasted_iota(jnp.int32, (8, 128), 1)

    def two_blocks(first, second):
        return rows(
            jnp.where(lane < RANK, first, pltpu.roll(second, RANK, 1)),
            jnp.where(lane < RANK, pltpu.roll(first, RANK, 1), second),
        )

    sixth = [summit[0], summit[1]]
    seventh = lifted(two_blocks(*sixth), matrices[RANK * (LOCAL + 7) : RANK * (LOCAL + 9), :])
    seventh = as_block(seventh)

    def held(kind, other):
        slot = tables[SLOTS + kind, other]
        place = jnp.minimum(slot, SLOTS - 1)
        return slot, incoming[other, pl.ds(pl.multiple_of(place * 8, 8), 8), :]

    for index, shift in enumerate(FORMED):
        other = jnp.minimum(jnp.maximum(me + shift, 0), DEVICES - 1)
        value = two_blocks(held(1, other)[1], jnp.zeros((8, 128), f32))[:, :RANK]
        start = RANK * (LOCAL + 9 + index)
        formed[index] = as_block(lifted(value, matrices[start : start + RANK, :]))

    entries = [[lists[j, 62] for j in range(8)]]
    for level in range(1, TOP + 1):
        row = DEVICES - (DEVICES >> (level - 1)) + (me >> level)
        entries.append([top_lists[j, row] for j in range(8)])

    def block(level, entry):
        if level == TOP:
            return jnp.where(entry == 0, seventh, 0.0)
        if level == SHARED:
            return jnp.where(entry == 0, sixth[0], jnp.where(entry == 1, sixth[1], 0.0))
        first = jnp.maximum(entry, 0) << level

        def add(i, total):
            for step in range(min(8, 1 << level)):
                slot, value = held(level, first + min(8, 1 << level) * i + step)
                if level == 2:
                    value = jnp.where(slot < SLOTS, value, formed[slot & 3])
                total = total + value
            return total

        nothing = jnp.zeros((8, 128), f32)
        if level <= 3:
            return jnp.where(entry < 0, nothing, add(0, nothing))
        return lax.fori_loop(0, jnp.where(entry < 0, 0, 1 << (level - 3)), add, nothing)

    wanted = [0] + [DEVICES - (DEVICES >> (level - 1)) + (me >> level) for level in range(1, TOP + 1)]
    for level in range(1, TOP + 1):
        first = DEVICES - (DEVICES >> (level - 1))
        wanted += [first + jnp.maximum(entry, 0) for entry in entries[level]]
    columns = []
    loads[6].wait()
    for group in range(8):
        part = wanted[8 * group : 8 * group + 8]
        regrouped(lambda c: top_anchors[pl.ds(part[c], 1), :], staged.at[group % 2], 8, 8)
        columns += eight_anchors([tile(staged.at[group % 2], c, 8) for c in range(8)])

    far_chain = []
    for unit in range(4):
        pairs = []
        for level in (2 * unit, 2 * unit + 1):
            sums = [block(level, entry) for entry in entries[level]]
            pairs += [two_blocks(sums[2 * j], sums[2 * j + 1]) for j in range(4)]
        weight = []
        for h in range(2):
            parts = []
            for slot in range(4):
                high = pairs[2 * slot + h].astype(bf16).astype(f32)
                parts += [high, pairs[2 * slot + h] - high]
            weight.append(rows(*parts).T.astype(bf16))
        own = columns[unit]
        sources = []
        for level in (2 * unit, 2 * unit + 1):
            for h in range(2):
                if level == 0:
                    found = [
                        held(SHARED, jnp.maximum(entry, 0))[1] for entry in entries[0][4 * h : 4 * h + 4]
                    ]
                    pair = lanes(two_blocks(found[0], found[1]), two_blocks(found[2], found[3]))
                else:
                    pair = lanes(*columns[4 * level + 2 * h : 4 * level + 2 * h + 2])
                sources.append(source_side(pair).astype(bf16))
        if unit == 0:
            own = halves(anchors[:, at(COLUMN[5])], own)
        result = cluster_sums(interact(two_targets(own), rows(*sources), rows(*weight)))
        far_chain += [result[:, :RANK], result[:, RANK:]]

    def pushed(value, matrix):
        high, low = split(matrix)
        return folded(dot_nt(narrow(value), lanes(high, low)))

    value = far_chain[TOP]
    for level in range(TOP - 1, -1, -1):
        value = far_chain[level] + pushed(value, matrices[RANK * (LOCAL + level) : RANK * (LOCAL + level + 1), :])

    def children(parent, height, q):
        start = (ROW[height] + 2 * q) * RANK
        return pushed(parent, matrices[start : start + 128, :])

    loads[10].wait()
    upper = [far_fourth + children(value, 4, 0)]
    for height in (3, 2, 1, 0):
        lower = []
        for q, slab in enumerate(upper):
            for side in range(2):
                parent = slab[:, RANK * side : RANK * (side + 1)]
                index = 2 * q + side
                if height == 3:
                    own = far_third[index]
                else:
                    own = far[:, at(COLUMN[height] + 128 * index)]
                lower.append(own + children(parent, height, index))
        upper = lower
    for q, slab in enumerate(upper):
        expansion[:, at(128 * q)] = slab

    def two_leaves(q, carry):
        slab = expansion[:, pl.ds(pl.multiple_of(q * 128, 128), 128)]
        for leaf in range(2):
            columns = pl.ds(pl.multiple_of(q * 256 + leaf * 128, 128), 128)
            high, low = split(basis[:, columns])
            own = slab[:, RANK * leaf : RANK * (leaf + 1)]
            out[:, columns] = near[:, columns] + folded(dot(narrow(own), rows(high, low)))
        return carry

    loads[11].wait()
    loads[12].wait()
    stores = []
    for part in range(2):
        lax.fori_loop(8 * part, 8 * part + 8, two_leaves, 0, unroll=8)
        own = slice(2048 * part, 2048 * part + 2048)
        stores += started(semaphores.at[13 + part :], (out.at[:, own], out_hbm.at[:, own]))
    for copy in stores:
        copy.wait()


def coarse_call(*arguments):
    return pl.pallas_call(
        coarse_kernel,
        out_shape=jax.ShapeDtypeStruct((RHS, LEAVES_DEV * LEAF), f32),
        in_specs=[SMEM] * 3 + [HBM] * 7 + [VMEM] + [HBM] * 6,
        out_specs=HBM,
        scratch_shapes=[
            pltpu.SMEM((TABLE, 128), jnp.int32),
            pltpu.VMEM((DIM, 4096), f32),
            pltpu.VMEM((RHS, 4096), f32),
            pltpu.VMEM((32, 512), f32),
            pltpu.VMEM((32, 896), f32),
            pltpu.VMEM((32, 896), f32),
            pltpu.VMEM((32, 128), f32),
            pltpu.VMEM((127, RANK * DIM), f32),
            pltpu.VMEM((DEVICES, 8 * SLOTS, 128), f32),
            pltpu.VMEM((MATRICES * RANK, RANK), f32),
            pltpu.VMEM((RHS, 56 * RANK), f32),
            pltpu.VMEM((RANK, 4096), f32),
            pltpu.VMEM((RHS, 4096), f32),
            pltpu.VMEM((RHS, 4096), f32),
            pltpu.VMEM((DIM, 16 * 128), f32),
            pltpu.VMEM((RHS, 16 * 128), f32),
            pltpu.VMEM((32, 64, 128), bf16),
            pltpu.VMEM((4, 4, 2, 64, 128), bf16),
            pltpu.VMEM((RHS, 2048), f32),
            pltpu.VMEM((2, 64, 128), f32),
            pltpu.VMEM((4, 8, 128), f32),
            pltpu.SemaphoreType.DMA((15,)),
        ],
        compiler_params=pltpu.CompilerParams(vmem_limit_bytes=VMEM_LIMIT),
        cost_estimate=pl.CostEstimate(flops=10**9, bytes_accessed=2**23, transcendentals=0),
        name="coarse",
    )(*arguments)


def exchanged(value, mate):
    pairs = []
    for device in range(DEVICES):
        other = mate(device)
        pairs.append((device, other if 0 <= other < DEVICES else device))
    return lax.ppermute(value, "leaf", pairs)


def inner_mate(device):
    return device + 1 if device % 2 == 0 else device - 1


def outer_mate(device):
    return device - 1 if device % 2 == 0 else device + 1


def third_mate(device):
    return device - 3 if device % 2 == 0 else device + 3


def on_device(
    points,
    charges,
    leaf_basis,
    local_transfer,
    local_anchors,
    local_lists,
    near_blocks,
    top_transfer,
    top_anchors,
    top_lists,
):
    index = lax.axis_index("leaf")
    device = index.reshape(1)
    half = NREACH * LEAF
    lower = (index & 1) * half

    def edge(start):
        return jnp.concatenate(
            [lax.dynamic_slice_in_dim(array, start, half, 1) for array in (points, charges)], axis=0
        )

    inner_edge, outer_edge, device = lax.optimization_barrier(
        (edge(half - lower), edge(lower), device)
    )
    inner_leaves = exchanged(inner_edge, inner_mate)
    outer_leaves = exchanged(outer_edge, outer_mate)

    tables = jnp.asarray(slot_tables())
    moments, anchors, inner_rim, outer_rim, third, summit, outgoing, matrices = moments_call(
        device, tables, leaf_basis, charges, local_transfer, local_anchors, top_transfer
    )
    outgoing, inner_leaves, outer_leaves = lax.optimization_barrier(
        (outgoing, inner_leaves, outer_leaves)
    )
    inner = exchanged(inner_rim, inner_mate)
    incoming = lax.all_to_all(outgoing, "leaf", 0, 0)
    summit = lax.cond(
        jnp.any(top_lists[SUMMIT_ROW:] >= 0),
        lambda value: lax.psum(value, "leaf"),
        lambda value: jnp.zeros_like(value),
        summit,
    )
    outer = exchanged(
        jnp.concatenate([outer_rim, inner[:, RIM[3] : RIM[5]]], axis=1), outer_mate
    )
    near = near_call(device, near_blocks.T, points, charges, inner_leaves, outer_leaves)
    near, third = lax.optimization_barrier((near, third))
    third = exchanged(third, third_mate)
    near, outer = lax.optimization_barrier((near, outer))
    beyond = exchanged(outer[:, RIM[3] :], inner_mate)
    local_lists = local_lists.T
    far = fine_call(device, local_lists, anchors, moments, inner, outer)
    return coarse_call(
        device,
        local_lists,
        top_lists.T,
        tables,
        anchors,
        moments,
        inner,
        outer,
        beyond,
        third,
        summit,
        top_anchors,
        incoming,
        matrices,
        far,
        leaf_basis,
        near,
    )


def solution(mesh):
    in_specs = (
        P(None, "leaf"),
        P(None, "leaf"),
        P(None, "leaf"),
        P("leaf", None),
        P("leaf", None),
        P("leaf", None),
        P("leaf", None),
        P(),
        P(),
        P(),
    )
    out_specs = P(None, "leaf")
    return jax.shard_map(
        on_device, mesh=mesh, in_specs=in_specs, out_specs=out_specs, check_vma=False
    )
```

```python
import math

import jax
import jax.numpy as jnp
import numpy as np
from jax import lax
from jax.experimental import pallas as pl
from jax.experimental.pallas import tpu as pltpu
from jax.sharding import PartitionSpec as P

DIM = 16
RHS = 16
LEAF = 128
RANK = 64
LEAVES_DEV = 32
NREACH = 16
REACH = 6
DEVICES = 128
TOP = 7
SHARED = 6
SLOTS = 3
SUMMIT_ROW = 124
NOTHING = 7
ANCHORS = 8
FORMED = (-6, -5, 5, 6)
LOCAL = 62
MATRICES = LOCAL + 13

bf16 = jnp.bfloat16
f32 = jnp.float32
SCALE = math.log2(math.e) / math.sqrt(3.0)
LN2 = math.log(2.0)
TINY = 1e-30

COLUMN = [0, 2048, 3072, 3584, 3840, 3968]
ROW = [0, 32, 48, 56, 60]
RIM = [0, 384, 768, 1152, 1408, 1536]
RIM_WIDTH = 1664
LOW_PIECES = [(0, 384), (2048, 2432), (3072, 3456), (3584, 4096)]
HIGH_PIECES = [(1664, 2048), (2688, 3072), (3200, 4096)]
VMEM_LIMIT = 60 * 2**20
VMEM = pl.BlockSpec(memory_space=pltpu.VMEM)
SMEM = pl.BlockSpec(memory_space=pltpu.SMEM)
HBM = pl.BlockSpec(memory_space=pltpu.HBM)


def relevant(first, second, level):
    return 2 <= abs((first >> level) - (second >> level)) <= REACH


def slot_tables():
    sent = np.full((DEVICES, SLOTS, DEVICES), NOTHING, np.int32)
    held = np.zeros((DEVICES, SHARED + 1, DEVICES), np.int32)
    for first in range(DEVICES):
        for second in range(DEVICES):
            levels = [level for level in range(SHARED) if relevant(first, second, level)]
            if levels and levels[0] == 0:
                if len(levels) == 3:
                    levels.pop()
                    held[first, 2, second] = 4 + FORMED.index(second - first)
                levels.append(ANCHORS)
            for slot, level in enumerate(levels):
                sent[first, slot, second] = level
                held[first, SHARED if level == ANCHORS else level, second] = slot
    return np.concatenate([sent, held], axis=1)


TABLE = SLOTS + SHARED + 1


def started(semaphores, *pairs):
    copies = []
    for index, (source, target) in enumerate(pairs):
        copy = pltpu.make_async_copy(source, target, semaphores.at[index])
        copy.start()
        copies.append(copy)
    return copies


def split(x):
    high = x.astype(bf16)
    return high, (x - high.astype(f32)).astype(bf16)


def lanes(*parts):
    return jnp.concatenate(parts, axis=1)


def rows(*parts):
    return jnp.concatenate(parts, axis=0)


def dot(a, b):
    return jnp.dot(a, b, preferred_element_type=f32)


def dot_nt(a, b):
    return lax.dot_general(a, b, (((1,), (1,)), ((), ())), preferred_element_type=f32)


def narrow(x):
    high, low = split(x)
    return rows(lanes(high, high), lanes(low, low))


def folded(x):
    return x[:16] + x[16:]


def sides(x):
    x = x * SCALE
    high = x.astype(bf16).astype(f32)
    low = (x - high).astype(bf16).astype(f32)
    norm = jnp.sum(high * (high + 2.0 * low), axis=0, keepdims=True)
    norm_high = norm.astype(bf16).astype(f32)
    norm_middle = (norm - norm_high).astype(bf16).astype(f32)
    norm_low = norm - norm_high - norm_middle
    row = lax.broadcasted_iota(jnp.int32, x.shape, 0)
    parts = jnp.where(row % 3 == 0, norm_high, jnp.where(row % 3 == 1, norm_middle, norm_low))
    return high, low, parts, row


def source_side(x):
    high, low, parts, row = sides(x)
    tail = jnp.where(row < 3, 1.0, jnp.where(row < 6, parts, 0.0))
    return rows(high, high, low, tail)


def target_sides(x):
    high, low, parts, row = sides(x)
    tail = jnp.where(row < 3, parts, jnp.where(row < 6, 1.0, 0.0))
    factors = rows(-2.0 * high, -2.0 * low, -2.0 * high, tail)
    first = rows(factors, jnp.zeros_like(factors)).T
    return first.astype(bf16), pltpu.roll(first, RANK, 1).astype(bf16)


def matern(squared):
    squared = jnp.maximum(squared, TINY)
    distance = squared * lax.rsqrt(squared)
    return (1.0 + LN2 * distance) * jnp.exp2(-distance)


def pick(parts):
    lane = lax.broadcasted_iota(jnp.int32, parts[0].shape, 1)
    result = parts[3]
    for j in (2, 1, 0):
        result = jnp.where(lane < 32 * (j + 1), parts[j], result)
    return result


def interact(targets, sources, weights):
    kernel = matern(dot(targets, sources))
    high, low = split(kernel)
    size = kernel.shape[0]
    result = dot(rows(high, low), weights)
    quarter = size // 4
    return pick(
        [
            result[quarter * j : quarter * (j + 1)]
            + result[size + quarter * j : size + quarter * (j + 1)]
            for j in range(4)
        ]
    )


def weight_turns(slabs):
    parts = []
    for slab in slabs:
        high = slab.astype(bf16).astype(f32)
        parts += [high, slab - high]
    columns = rows(*parts).T
    return [
        (columns if turn == 0 else pltpu.roll(columns, 32 * turn, 1)).astype(bf16)
        for turn in range(4)
    ]


def halves(first, second):
    lane = lax.broadcasted_iota(jnp.int32, first.shape, 1)
    return jnp.where(lane < RANK, first, second)


def regrouped(load, staged, count, width):
    for c in range(count):
        value = load(c)
        for i in range(width):
            staged[8 * i + c : 8 * i + c + 1, :] = value[:, 128 * i : 128 * (i + 1)]


def tile(staged, c, width):
    return staged[pl.ds(c, width, stride=8), :]


def store_matrix(staged, c, matrices, index):
    value = tile(staged, c, 32)
    matrices[pl.ds(RANK * index, 32, stride=2), :] = value[:, :RANK]
    matrices[pl.ds(RANK * index + 1, 32, stride=2), :] = value[:, RANK:]


def eight_anchors(tiles):
    group = lax.broadcasted_iota(jnp.int32, (8, 128), 1) // 16
    for bit in (1, 2, 4):
        turned = list(tiles)
        for p in range(8):
            if p & bit == 0:
                first, second = tiles[p], tiles[p | bit]
                turned[p] = jnp.where(group & bit == 0, first, pltpu.roll(second, 16 * bit, 1))
                turned[p | bit] = jnp.where(
                    group & bit == 0, pltpu.roll(first, 128 - 16 * bit, 1), second
                )
        tiles = turned
    held = rows(*tiles).T
    slabs = [lanes(held[32 * q : 32 * q + 16], held[32 * q + 16 : 32 * q + 32]) for q in range(4)]
    value = rows(*slabs)
    high = value.astype(bf16)
    rest = value - high.astype(f32)
    middle = rest.astype(bf16)
    low = (rest - middle.astype(f32)).astype(bf16)
    row = lax.broadcasted_iota(jnp.int32, (128, 128), 0)
    column = lax.broadcasted_iota(jnp.int32, (128, 128), 1)
    order = (row & RANK) + 8 * (row & 7) + ((row & 63) >> 3)
    order = jnp.where(order == column, 1.0, 0.0).astype(bf16)
    value = dot(rows(high, middle, low), order)
    value = value[:64] + (value[64:128] + value[128:])
    return [value[16 * q : 16 * (q + 1)] for q in range(4)]


def lifted(slab, matrices):
    high, low = split(matrices)
    return folded(dot(narrow(slab), rows(high, low)))


def as_block(value):
    return lanes(value[:8], value[8:])


def moments_kernel(
    device,
    tables_hbm,
    basis_hbm,
    charges_hbm,
    transfer_hbm,
    anchors_hbm,
    top_hbm,
    moments_out,
    anchors_out,
    inner_out,
    outer_out,
    third,
    summit,
    outgoing_out,
    matrices_out,
    tables,
    basis,
    charges,
    transfer,
    anchor_rows,
    top_transfer,
    moments,
    anchors,
    inner,
    outer,
    outgoing,
    matrices,
    blocks,
    staged,
    staged_anchors,
    semaphores,
):
    me = device[0]
    quarters = [slice(1024 * i, 1024 * (i + 1)) for i in range(4)]
    loads = started(
        semaphores,
        (charges_hbm, charges),
        *[(basis_hbm.at[:, part], basis.at[:, part]) for part in quarters],
        (transfer_hbm, transfer),
        (anchors_hbm, anchor_rows),
        (tables_hbm.at[me], tables),
    )
    chain = [2 * DEVICES - (2 * DEVICES >> level) + (me >> level) for level in range(TOP)]
    chain += [252, 253]
    for shift in FORMED:
        other = jnp.minimum(jnp.maximum(me + shift, 0), DEVICES - 1)
        chain.append(DEVICES + (other >> 1))
    chain_loads = started(
        semaphores.at[18:],
        *[
            (top_hbm.at[pl.ds(row, 1), :], top_transfer.at[pl.ds(index, 1), :])
            for index, row in enumerate(chain)
        ],
    )
    loads[0].wait()

    def two_leaves(q, carry):
        parts = []
        for leaf in range(2):
            columns = pl.ds(pl.multiple_of(q * 256 + leaf * 128, 128), 128)
            high, low = split(basis[:, columns])
            parts.append(folded(dot_nt(narrow(charges[:, columns]), lanes(high, low))))
        moments[:, pl.ds(pl.multiple_of(q * 128, 128), 128)] = lanes(*parts)
        return carry

    for part in range(4):
        loads[1 + part].wait()
        lax.fori_loop(4 * part, 4 * part + 4, two_leaves, 0, unroll=4)

    loads[5].wait()
    for group in range(8):
        count = min(8, LOCAL - 8 * group)
        for i in range(32):
            staged[group % 2, 8 * i : 8 * i + count, :] = transfer[
                8 * group : 8 * group + count, 128 * i : 128 * (i + 1)
            ]
        for c in range(count):
            store_matrix(staged.at[group % 2], c, matrices, 8 * group + c)
    for copy in chain_loads:
        copy.wait()
    for group in range(2):
        count = min(8, 13 - 8 * group)
        for i in range(32):
            staged[group, 8 * i : 8 * i + count, :] = top_transfer[
                8 * group : 8 * group + count, 128 * i : 128 * (i + 1)
            ]
        for c in range(count):
            store_matrix(staged.at[group], c, matrices, LOCAL + 8 * group + c)
    stores = started(semaphores.at[9:], (matrices, matrices_out))

    loads[6].wait()
    for group in range(8):
        count = min(8, 63 - 8 * group)
        for i in range(8):
            staged_anchors[group % 2, 8 * i : 8 * i + count, :] = anchor_rows[
                8 * group : 8 * group + count, 128 * i : 128 * (i + 1)
            ]
        tiles = [tile(staged_anchors.at[group % 2], c, 8) for c in range(count)]
        tiles += [jnp.zeros((8, 128), f32)] * (8 - count)
        for q, slab in enumerate(eight_anchors(tiles)):
            anchors[:, 512 * group + 128 * q : 512 * group + 128 * (q + 1)] = slab

    for height in range(5):
        number = LEAVES_DEV >> height
        parents = []
        for q in range(number // 2):
            start = (ROW[height] + 2 * q) * RANK
            slab = moments[:, COLUMN[height] + 128 * q : COLUMN[height] + 128 * (q + 1)]
            parents.append(lifted(slab, matrices[start : start + 128, :]))
        if height == 4:
            parents.append(jnp.zeros((16, RANK), f32))
        for q in range(len(parents) // 2):
            start = COLUMN[height + 1] + 128 * q
            moments[:, start : start + 128] = lanes(parents[2 * q], parents[2 * q + 1])

    even = (me & 1) == 0

    def fill(low_rim, high_rim):
        for row, value in ((slice(0, DIM), anchors), (slice(DIM, 2 * DIM), moments)):
            for rim, parts in ((low_rim, LOW_PIECES), (high_rim, HIGH_PIECES)):
                start = 0
                for first, last in parts:
                    rim[row, start : start + last - first] = value[:, first:last]
                    start += last - first

    @pl.when(even)
    def _():
        fill(outer, inner)

    @pl.when(jnp.logical_not(even))
    def _():
        fill(inner, outer)

    third[:DIM, :] = anchors[:, 3840:3968]
    third[DIM:, :] = moments[:, 3840:3968]
    stores += started(
        semaphores.at[10:],
        (inner, inner_out),
        (outer, outer_out),
        (moments, moments_out),
        (anchors, anchors_out),
    )

    value = moments[:, COLUMN[5] : COLUMN[5] + RANK]
    for level in range(SHARED + 1):
        blocks[level] = as_block(value)
        if level < SHARED:
            start = RANK * (LOCAL + level)
            value = lifted(value, matrices[start : start + RANK, :])
    blocks[NOTHING] = jnp.zeros((8, 128), f32)
    for half in range(2):
        summit[half] = jnp.where(me >> SHARED == half, blocks[SHARED], 0.0)
    blocks[ANCHORS] = as_block(anchors[:, COLUMN[5] : COLUMN[5] + RANK])

    def one_device(other, carry):
        for slot in range(SLOTS):
            outgoing[other, 8 * slot : 8 * (slot + 1), :] = blocks[tables[slot, other]]
        return carry

    loads[7].wait()
    for part in range(4):
        lax.fori_loop(32 * part, 32 * part + 32, one_device, 0, unroll=8)
        own = slice(32 * part, 32 * part + 32)
        stores += started(semaphores.at[14 + part :], (outgoing.at[own], outgoing_out.at[own]))
    for copy in stores:
        copy.wait()


def moments_call(*arguments):
    shape = jax.ShapeDtypeStruct
    return pl.pallas_call(
        moments_kernel,
        out_shape=(
            shape((16, 4096), f32),
            shape((16, 4096), f32),
            shape((32, RIM_WIDTH), f32),
            shape((32, RIM_WIDTH), f32),
            shape((32, 128), f32),
            shape((2, 8, 128), f32),
            shape((DEVICES, 8 * SLOTS, 128), f32),
            shape((MATRICES * RANK, RANK), f32),
        ),
        in_specs=[SMEM] + [HBM] * 6,
        out_specs=(HBM, HBM, HBM, HBM, VMEM, VMEM, HBM, HBM),
        scratch_shapes=[
            pltpu.SMEM((TABLE, 128), jnp.int32),
            pltpu.VMEM((RANK, 4096), f32),
            pltpu.VMEM((RHS, 4096), f32),
            pltpu.VMEM((LOCAL, RANK * RANK), f32),
            pltpu.VMEM((63, RANK * DIM), f32),
            pltpu.VMEM((16, RANK * RANK), f32),
            pltpu.VMEM((RHS, 4096), f32),
            pltpu.VMEM((DIM, 4096), f32),
            pltpu.VMEM((32, RIM_WIDTH), f32),
            pltpu.VMEM((32, RIM_WIDTH), f32),
            pltpu.VMEM((DEVICES, 8 * SLOTS, 128), f32),
            pltpu.VMEM((MATRICES * RANK, RANK), f32),
            pltpu.VMEM((9, 8, 128), f32),
            pltpu.VMEM((2, 256, 128), f32),
            pltpu.VMEM((2, 64, 128), f32),
            pltpu.SemaphoreType.DMA((31,)),
        ],
        compiler_params=pltpu.CompilerParams(vmem_limit_bytes=VMEM_LIMIT),
        cost_estimate=pl.CostEstimate(flops=10**9, bytes_accessed=2**22, transcendentals=0),
        name="moments",
    )(*arguments)


def near_kernel(
    device,
    near_blocks,
    points_hbm,
    charges_hbm,
    inner_hbm,
    outer_hbm,
    out_hbm,
    points,
    charges,
    inner,
    outer,
    out,
    factors,
    weights,
    semaphores,
):
    me = device[0]
    loads = started(
        semaphores,
        (points_hbm, points),
        (charges_hbm, charges),
        (inner_hbm, inner),
        (outer_hbm, outer),
    )

    def prepare(point_ref, charge_ref, charge_row, first):
        def four_leaves(i, carry):
            columns = pl.ds(pl.multiple_of(i * 512, 512), 512)
            side = source_side(point_ref[:DIM, columns]).astype(bf16)
            charge = charge_ref[charge_row : charge_row + RHS, columns]
            slabs = []
            for m in range(4):
                factors[(first + i) * 4 + m] = side[:, 128 * m : 128 * (m + 1)]
                slabs.append(charge[:, 128 * m : 128 * (m + 1)])
            for turn, value in enumerate(weight_turns(slabs)):
                weights[turn, first + i] = value
            return carry

        return four_leaves

    loads[0].wait()
    loads[1].wait()
    lax.fori_loop(0, 8, prepare(points, charges, 0, 4), 0, unroll=8)
    side = (me & 1) * 12
    loads[2].wait()
    lax.fori_loop(0, 4, prepare(inner, inner, DIM, 12 - side), 0, unroll=4)
    loads[3].wait()
    lax.fori_loop(0, 4, prepare(outer, outer, DIM, side), 0, unroll=4)
    factors[64] = jnp.zeros((64, 128), bf16)
    for turn in range(4):
        weights[turn, 16] = jnp.zeros((128, 128), bf16)
    first_leaf = me * LEAVES_DEV - NREACH

    def one_leaf(t, carry):
        columns = pl.ds(pl.multiple_of(t * 128, 128), 128)
        front, back = target_sides(points[:, columns])
        empty = jnp.zeros_like(front)
        targets = rows(
            lanes(front, empty), lanes(back, empty), lanes(empty, front), lanes(empty, back)
        )
        located = []
        for j in range(8):
            block = near_blocks[j, t]
            inside = jnp.minimum(jnp.maximum(block - first_leaf, 0), 63)
            located.append(jnp.where(block < 0, 64, inside))
        sources = rows(
            *[lanes(factors[located[2 * j]], factors[located[2 * j + 1]]) for j in range(4)]
        )
        weight = rows(
            *[
                pick([weights[(j - located[2 * j + h]) & 3, located[2 * j + h] >> 2] for j in range(4)])
                for h in range(2)
            ]
        )
        total = interact(targets, sources, weight).T
        out[:, columns] = sum(total[16 * g : 16 * (g + 1)] for g in range(8))
        return carry

    stores = []
    for part in range(2):
        lax.fori_loop(16 * part, 16 * part + 16, one_leaf, 0, unroll=16)
        own = slice(2048 * part, 2048 * part + 2048)
        stores += started(semaphores.at[4 + part :], (out.at[:, own], out_hbm.at[:, own]))
    for copy in stores:
        copy.wait()


def near_call(*arguments):
    return pl.pallas_call(
        near_kernel,
        out_shape=jax.ShapeDtypeStruct((RHS, LEAVES_DEV * LEAF), f32),
        in_specs=[SMEM, SMEM] + [HBM] * 4,
        out_specs=HBM,
        scratch_shapes=[
            pltpu.VMEM((DIM, LEAVES_DEV * LEAF), f32),
            pltpu.VMEM((RHS, LEAVES_DEV * LEAF), f32),
            pltpu.VMEM((DIM + RHS, NREACH * LEAF), f32),
            pltpu.VMEM((DIM + RHS, NREACH * LEAF), f32),
            pltpu.VMEM((RHS, LEAVES_DEV * LEAF), f32),
            pltpu.VMEM((65, 64, 128), bf16),
            pltpu.VMEM((4, 17, 128, 128), bf16),
            pltpu.SemaphoreType.DMA((6,)),
        ],
        compiler_params=pltpu.CompilerParams(vmem_limit_bytes=VMEM_LIMIT),
        cost_estimate=pl.CostEstimate(flops=10**10, bytes_accessed=2**22, transcendentals=0),
        name="near",
    )(*arguments)


def prepare_factors(anchors, factors, groups):
    def four_slabs(i, carry):
        side = source_side(anchors[:, pl.ds(pl.multiple_of(i * 512, 512), 512)])
        for m in range(4):
            slab = side[:, 128 * m : 128 * (m + 1)]
            turned = pltpu.roll(slab, RANK, 1)
            factors[(i * 4 + m) * 2] = halves(slab, turned).astype(bf16)
            factors[(i * 4 + m) * 2 + 1] = halves(turned, slab).astype(bf16)
        return carry

    lax.fori_loop(0, groups, four_slabs, 0, unroll=True)


def prepare_weights(moments, weights, groups):
    def four_slabs(i, carry):
        value = moments[:, pl.ds(pl.multiple_of(i * 512, 512), 512)]
        turns = weight_turns([value[:, 128 * m : 128 * (m + 1)] for m in range(4)])
        for turn in range(4):
            weights[turn, i, 0] = turns[turn][:RANK]
            weights[turn, i, 1] = turns[turn][RANK:]
        return carry

    lax.fori_loop(0, groups, four_slabs, 0, unroll=True)


def two_targets(anchors):
    front, back = target_sides(anchors)
    empty = jnp.zeros((RANK, 128), bf16)
    return rows(
        lanes(front[:RANK], empty),
        lanes(back[:RANK], empty),
        lanes(empty, front[RANK:]),
        lanes(empty, back[RANK:]),
    )


def four_sources(factors, located):
    return lanes(
        halves(factors[located[0]], factors[located[1]]),
        halves(factors[located[2]], factors[located[3]]),
    )


def placed(weights, index, slot):
    pair = index >> 1
    return weights[(slot - pair) & 3, pair >> 2, index & 1]


def two_clusters(anchors, factors, weights, located):
    sources = rows(*[four_sources(factors, located[4 * slot : 4 * slot + 4]) for slot in range(4)])
    weight = rows(
        *[pick([placed(weights, located[4 * slot + m], slot) for slot in range(4)]) for m in range(4)]
    )
    return cluster_sums(interact(two_targets(anchors), sources, weight))


def cluster_sums(total):
    total = total.T
    return lanes(
        total[:16] + total[16:32] + total[32:48] + total[48:64],
        total[64:80] + total[80:96] + total[96:112] + total[112:],
    )


def locate(entry, first, last, base, empty):
    inside = jnp.minimum(jnp.maximum(entry - first, 0), last)
    return jnp.where(entry < 0, empty, base + inside)


FINE_BASE = [0, 44, 72]
FINE_EMPTY = 92


def fine_kernel(
    device,
    lists,
    anchors_hbm,
    moments_hbm,
    inner_hbm,
    outer_hbm,
    far_hbm,
    anchors,
    moments,
    inner,
    outer,
    far,
    held_anchors,
    held_moments,
    factors,
    weights,
    semaphores,
):
    me = device[0]
    loads = started(
        semaphores,
        (anchors_hbm, anchors),
        (moments_hbm, moments),
        (inner_hbm, inner),
        (outer_hbm, outer),
    )
    for copy in loads:
        copy.wait()
    odd = (me & 1) == 1
    start = 0
    for height in range(3):
        width = (LEAVES_DEV >> height) * RANK
        wide = REACH * RANK
        rim = slice(RIM[height], RIM[height] + wide)
        own = slice(COLUMN[height], COLUMN[height] + width)
        far_end = start + wide + width
        for held, whole, row in (
            (held_anchors, anchors, slice(0, DIM)),
            (held_moments, moments, slice(DIM, 2 * DIM)),
        ):
            held[:, start + wide : far_end] = whole[:, own]
            inner_at = pl.multiple_of(jnp.where(odd, start, far_end), 128)
            outer_at = pl.multiple_of(jnp.where(odd, far_end, start), 128)
            held[:, pl.ds(inner_at, wide)] = inner[row, rim]
            held[:, pl.ds(outer_at, wide)] = outer[row, rim]
        start = far_end + wide
    held_anchors[:, start:] = jnp.zeros((DIM, 48 * 128 - start), f32)
    held_moments[:, start:] = jnp.zeros((DIM, 48 * 128 - start), f32)
    prepare_factors(held_anchors, factors, 12)
    prepare_weights(held_moments, weights, 12)

    for height in range(3):
        number = LEAVES_DEV >> height

        def one_pair(q, carry, height=height, number=number):
            first = me * number - REACH
            located = []
            for cluster in range(2):
                for j in range(8):
                    entry = lists[j, 2 * LEAVES_DEV - 2 * number + 2 * q + cluster]
                    located.append(
                        locate(entry, first, number + 2 * REACH - 1, FINE_BASE[height], FINE_EMPTY)
                    )
            columns = pl.ds(pl.multiple_of(COLUMN[height] + q * 128, 128), 128)
            far[:, columns] = two_clusters(anchors[:, columns], factors, weights, located)
            return carry

        lax.fori_loop(0, number // 2, one_pair, 0, unroll=True)
    for copy in started(semaphores, (far, far_hbm)):
        copy.wait()


def fine_call(*arguments):
    return pl.pallas_call(
        fine_kernel,
        out_shape=jax.ShapeDtypeStruct((RHS, 56 * RANK), f32),
        in_specs=[SMEM, SMEM] + [HBM] * 4,
        out_specs=HBM,
        scratch_shapes=[
            pltpu.VMEM((DIM, 4096), f32),
            pltpu.VMEM((RHS, 4096), f32),
            pltpu.VMEM((32, RIM_WIDTH), f32),
            pltpu.VMEM((32, 2048), f32),
            pltpu.VMEM((RHS, 56 * RANK), f32),
            pltpu.VMEM((DIM, 48 * 128), f32),
            pltpu.VMEM((RHS, 48 * 128), f32),
            pltpu.VMEM((96, 64, 128), bf16),
            pltpu.VMEM((4, 12, 2, 64, 128), bf16),
            pltpu.SemaphoreType.DMA((4,)),
        ],
        compiler_params=pltpu.CompilerParams(vmem_limit_bytes=VMEM_LIMIT),
        cost_estimate=pl.CostEstimate(flops=5 * 10**9, bytes_accessed=2**22, transcendentals=0),
        name="fine",
    )(*arguments)


COARSE_EMPTY = 30


def coarse_kernel(
    device,
    lists,
    top_lists,
    tables_hbm,
    anchors_hbm,
    moments_hbm,
    inner_hbm,
    outer_hbm,
    beyond_hbm,
    third_hbm,
    summit,
    top_hbm,
    incoming_hbm,
    matrices_hbm,
    far_hbm,
    basis_hbm,
    near_hbm,
    out_hbm,
    tables,
    anchors,
    moments,
    inner,
    outer,
    beyond,
    third,
    top_anchors,
    incoming,
    matrices,
    far,
    basis,
    near,
    out,
    held_anchors,
    held_moments,
    factors,
    weights,
    expansion,
    staged,
    formed,
    semaphores,
):
    me = device[0]
    loads = started(
        semaphores,
        (anchors_hbm, anchors),
        (moments_hbm, moments),
        (inner_hbm.at[:, 1152:], inner),
        (outer_hbm.at[:, 1152:], outer),
        (beyond_hbm, beyond),
        (third_hbm, third),
        (top_hbm, top_anchors),
        (tables_hbm.at[me], tables),
        (incoming_hbm, incoming),
        (matrices_hbm, matrices),
        (far_hbm, far),
        (basis_hbm, basis),
        (near_hbm, near),
    )
    for copy in loads[:6]:
        copy.wait()
    odd = (me & 1) == 1

    def at(column):
        return slice(column, column + 128)

    def place(on_inner, source, column, low_place, high_place):
        below = odd if on_inner else jnp.logical_not(odd)
        target = pl.multiple_of(jnp.where(below, low_place, high_place) * 128, 128)
        held_anchors[:, pl.ds(target, 128)] = source[:DIM, column]
        held_moments[:, pl.ds(target, 128)] = source[DIM:, column]

    def nearest(on_inner, column):
        below = odd if on_inner else jnp.logical_not(odd)
        return pl.ds(pl.multiple_of(column + jnp.where(below, 128, 0), 128), 128)

    for on_inner, source in ((True, inner), (False, outer)):
        place(on_inner, source, at(0), 1, 5)
        place(on_inner, source, at(128), 2, 6)
        place(on_inner, source, at(256), 10, 12)
    place(False, outer, nearest(False, 512), 0, 7)
    place(False, outer, at(768), 9, 13)
    place(False, third, at(0), 8, 14)
    place(True, beyond, nearest(True, 0), 0, 7)
    place(True, beyond, at(256), 9, 13)
    place(True, beyond, at(768), 8, 14)
    for index, column in ((3, 3584), (4, 3712), (11, 3840)):
        held_anchors[:, at(128 * index)] = anchors[:, at(column)]
        held_moments[:, at(128 * index)] = moments[:, at(column)]
    held_anchors[:, at(128 * 15)] = jnp.zeros((DIM, 128), f32)
    held_moments[:, at(128 * 15)] = jnp.zeros((RHS, 128), f32)
    prepare_factors(held_anchors, factors, 4)
    prepare_weights(held_moments, weights, 4)

    def local_pair(height, q, base):
        number = LEAVES_DEV >> height
        located = []
        for cluster in range(2):
            for j in range(8):
                entry = lists[j, 2 * LEAVES_DEV - 2 * number + 2 * q + cluster]
                located.append(
                    locate(entry, me * number - REACH, number + 2 * REACH - 1, base, COARSE_EMPTY)
                )
        return two_clusters(
            anchors[:, at(COLUMN[height] + 128 * q)], factors, weights, located
        )

    far_third = [local_pair(3, q, 0) for q in range(2)]
    far_fourth = local_pair(4, 0, 16)

    entries = [[lists[j, 62] for j in range(8)]]
    for level in range(1, TOP + 1):
        row = DEVICES - (DEVICES >> (level - 1)) + (me >> level)
        entries.append([top_lists[j, row] for j in range(8)])

    wanted = [0] + [DEVICES - (DEVICES >> (level - 1)) + (me >> level) for level in range(1, TOP + 1)]
    for level in range(1, TOP + 1):
        first = DEVICES - (DEVICES >> (level - 1))
        wanted += [first + jnp.maximum(entry, 0) for entry in entries[level]]
    columns = []
    loads[6].wait()
    for group in range(8):
        part = wanted[8 * group : 8 * group + 8]
        regrouped(lambda c: top_anchors[pl.ds(part[c], 1), :], staged.at[group % 2], 8, 8)
        columns += eight_anchors([tile(staged.at[group % 2], c, 8) for c in range(8)])

    loads[8].wait()
    loads[9].wait()
    loads[7].wait()

    lane = lax.broadcasted_iota(jnp.int32, (8, 128), 1)

    def two_blocks(first, second):
        return rows(
            jnp.where(lane < RANK, first, pltpu.roll(second, RANK, 1)),
            jnp.where(lane < RANK, pltpu.roll(first, RANK, 1), second),
        )

    sixth = [summit[0], summit[1]]
    seventh = lifted(two_blocks(*sixth), matrices[RANK * (LOCAL + 7) : RANK * (LOCAL + 9), :])
    seventh = as_block(seventh)

    def held(kind, other):
        slot = tables[SLOTS + kind, other]
        place = jnp.minimum(slot, SLOTS - 1)
        return slot, incoming[other, pl.ds(pl.multiple_of(place * 8, 8), 8), :]

    for index, shift in enumerate(FORMED):
        other = jnp.minimum(jnp.maximum(me + shift, 0), DEVICES - 1)
        value = two_blocks(held(1, other)[1], jnp.zeros((8, 128), f32))[:, :RANK]
        start = RANK * (LOCAL + 9 + index)
        formed[index] = as_block(lifted(value, matrices[start : start + RANK, :]))

    def block(level, entry):
        if level == TOP:
            return jnp.where(entry == 0, seventh, 0.0)
        if level == SHARED:
            return jnp.where(entry == 0, sixth[0], jnp.where(entry == 1, sixth[1], 0.0))
        first = jnp.maximum(entry, 0) << level

        def add(i, total):
            for step in range(min(8, 1 << level)):
                slot, value = held(level, first + min(8, 1 << level) * i + step)
                if level == 2:
                    value = jnp.where(slot < SLOTS, value, formed[slot & 3])
                total = total + value
            return total

        nothing = jnp.zeros((8, 128), f32)
        if level <= 4:
            total = nothing
            for i in range(max(1, (1 << level) // 8)):
                total = add(i, total)
            return jnp.where(entry < 0, nothing, total)
        return lax.fori_loop(0, jnp.where(entry < 0, 0, 1 << (level - 3)), add, nothing)

    found_pairs = []
    for level in range(TOP + 1):
        sums = [block(level, entry) for entry in entries[level]]
        found_pairs += [two_blocks(sums[2 * j], sums[2 * j + 1]) for j in range(4)]

    far_chain = []
    for unit in range(4):
        pairs = found_pairs[8 * unit : 8 * unit + 8]
        weight = []
        for h in range(2):
            parts = []
            for slot in range(4):
                high = pairs[2 * slot + h].astype(bf16).astype(f32)
                parts += [high, pairs[2 * slot + h] - high]
            weight.append(rows(*parts).T.astype(bf16))
        own = columns[unit]
        sources = []
        for level in (2 * unit, 2 * unit + 1):
            for h in range(2):
                if level == 0:
                    found = [
                        held(SHARED, jnp.maximum(entry, 0))[1] for entry in entries[0][4 * h : 4 * h + 4]
                    ]
                    pair = lanes(two_blocks(found[0], found[1]), two_blocks(found[2], found[3]))
                else:
                    pair = lanes(*columns[4 * level + 2 * h : 4 * level + 2 * h + 2])
                sources.append(source_side(pair).astype(bf16))
        if unit == 0:
            own = halves(anchors[:, at(COLUMN[5])], own)
        result = cluster_sums(interact(two_targets(own), rows(*sources), rows(*weight)))
        far_chain += [result[:, :RANK], result[:, RANK:]]

    def pushed(value, matrix):
        high, low = split(matrix)
        return folded(dot_nt(narrow(value), lanes(high, low)))

    value = far_chain[TOP]
    for level in range(TOP - 1, -1, -1):
        value = far_chain[level] + pushed(value, matrices[RANK * (LOCAL + level) : RANK * (LOCAL + level + 1), :])

    def children(parent, height, q):
        start = (ROW[height] + 2 * q) * RANK
        return pushed(parent, matrices[start : start + 128, :])

    loads[10].wait()
    upper = [far_fourth + children(value, 4, 0)]
    for height in (3, 2, 1, 0):
        lower = []
        for q, slab in enumerate(upper):
            for side in range(2):
                parent = slab[:, RANK * side : RANK * (side + 1)]
                index = 2 * q + side
                if height == 3:
                    own = far_third[index]
                else:
                    own = far[:, at(COLUMN[height] + 128 * index)]
                lower.append(own + children(parent, height, index))
        upper = lower
    for q, slab in enumerate(upper):
        expansion[:, at(128 * q)] = slab

    def two_leaves(q, carry):
        slab = expansion[:, pl.ds(pl.multiple_of(q * 128, 128), 128)]
        for leaf in range(2):
            columns = pl.ds(pl.multiple_of(q * 256 + leaf * 128, 128), 128)
            high, low = split(basis[:, columns])
            own = slab[:, RANK * leaf : RANK * (leaf + 1)]
            out[:, columns] = near[:, columns] + folded(dot(narrow(own), rows(high, low)))
        return carry

    loads[11].wait()
    loads[12].wait()
    stores = []
    for part in range(2):
        lax.fori_loop(8 * part, 8 * part + 8, two_leaves, 0, unroll=8)
        own = slice(2048 * part, 2048 * part + 2048)
        stores += started(semaphores.at[13 + part :], (out.at[:, own], out_hbm.at[:, own]))
    for copy in stores:
        copy.wait()


def coarse_call(*arguments):
    return pl.pallas_call(
        coarse_kernel,
        out_shape=jax.ShapeDtypeStruct((RHS, LEAVES_DEV * LEAF), f32),
        in_specs=[SMEM] * 3 + [HBM] * 7 + [VMEM] + [HBM] * 6,
        out_specs=HBM,
        scratch_shapes=[
            pltpu.SMEM((TABLE, 128), jnp.int32),
            pltpu.VMEM((DIM, 4096), f32),
            pltpu.VMEM((RHS, 4096), f32),
            pltpu.VMEM((32, 512), f32),
            pltpu.VMEM((32, 896), f32),
            pltpu.VMEM((32, 896), f32),
            pltpu.VMEM((32, 128), f32),
            pltpu.VMEM((127, RANK * DIM), f32),
            pltpu.VMEM((DEVICES, 8 * SLOTS, 128), f32),
            pltpu.VMEM((MATRICES * RANK, RANK), f32),
            pltpu.VMEM((RHS, 56 * RANK), f32),
            pltpu.VMEM((RANK, 4096), f32),
            pltpu.VMEM((RHS, 4096), f32),
            pltpu.VMEM((RHS, 4096), f32),
            pltpu.VMEM((DIM, 16 * 128), f32),
            pltpu.VMEM((RHS, 16 * 128), f32),
            pltpu.VMEM((32, 64, 128), bf16),
            pltpu.VMEM((4, 4, 2, 64, 128), bf16),
            pltpu.VMEM((RHS, 2048), f32),
            pltpu.VMEM((2, 64, 128), f32),
            pltpu.VMEM((4, 8, 128), f32),
            pltpu.SemaphoreType.DMA((15,)),
        ],
        compiler_params=pltpu.CompilerParams(vmem_limit_bytes=VMEM_LIMIT),
        cost_estimate=pl.CostEstimate(flops=10**9, bytes_accessed=2**23, transcendentals=0),
        name="coarse",
    )(*arguments)


def exchanged(value, mate):
    pairs = []
    for device in range(DEVICES):
        other = mate(device)
        pairs.append((device, other if 0 <= other < DEVICES else device))
    return lax.ppermute(value, "leaf", pairs)


def inner_mate(device):
    return device + 1 if device % 2 == 0 else device - 1


def outer_mate(device):
    return device - 1 if device % 2 == 0 else device + 1


def third_mate(device):
    return device - 3 if device % 2 == 0 else device + 3


def on_device(
    points,
    charges,
    leaf_basis,
    local_transfer,
    local_anchors,
    local_lists,
    near_blocks,
    top_transfer,
    top_anchors,
    top_lists,
):
    index = lax.axis_index("leaf")
    device = index.reshape(1)
    half = NREACH * LEAF
    lower = (index & 1) * half

    def edge(start):
        return jnp.concatenate(
            [lax.dynamic_slice_in_dim(array, start, half, 1) for array in (points, charges)], axis=0
        )

    inner_edge, outer_edge, device = lax.optimization_barrier(
        (edge(half - lower), edge(lower), device)
    )
    inner_leaves = exchanged(inner_edge, inner_mate)
    outer_leaves = exchanged(outer_edge, outer_mate)

    tables = jnp.asarray(slot_tables())
    moments, anchors, inner_rim, outer_rim, third, summit, outgoing, matrices = moments_call(
        device, tables, leaf_basis, charges, local_transfer, local_anchors, top_transfer
    )
    outgoing, inner_leaves, outer_leaves = lax.optimization_barrier(
        (outgoing, inner_leaves, outer_leaves)
    )
    inner = exchanged(inner_rim, inner_mate)
    incoming = lax.all_to_all(outgoing, "leaf", 0, 0)
    summit = lax.cond(
        jnp.any(top_lists[SUMMIT_ROW:] >= 0),
        lambda value: lax.psum(value, "leaf"),
        lambda value: jnp.zeros_like(value),
        summit,
    )
    outer = exchanged(
        jnp.concatenate([outer_rim, inner[:, RIM[3] : RIM[5]]], axis=1), outer_mate
    )
    near = near_call(device, near_blocks.T, points, charges, inner_leaves, outer_leaves)
    near, third = lax.optimization_barrier((near, third))
    third = exchanged(third, third_mate)
    near, outer = lax.optimization_barrier((near, outer))
    beyond = exchanged(outer[:, RIM[3] :], inner_mate)
    local_lists = local_lists.T
    far = fine_call(device, local_lists, anchors, moments, inner, outer)
    return coarse_call(
        device,
        local_lists,
        top_lists.T,
        tables,
        anchors,
        moments,
        inner,
        outer,
        beyond,
        third,
        summit,
        top_anchors,
        incoming,
        matrices,
        far,
        leaf_basis,
        near,
    )


def solution(mesh):
    in_specs = (
        P(None, "leaf"),
        P(None, "leaf"),
        P(None, "leaf"),
        P("leaf", None),
        P("leaf", None),
        P("leaf", None),
        P("leaf", None),
        P(),
        P(),
        P(),
    )
    out_specs = P(None, "leaf")
    return jax.shard_map(
        on_device, mesh=mesh, in_specs=in_specs, out_specs=out_specs, check_vma=False
    )
```

```python
import math

import jax
import jax.numpy as jnp
import numpy as np
from jax import lax
from jax.experimental import pallas as pl
from jax.experimental.pallas import tpu as pltpu
from jax.sharding import PartitionSpec as P

DIM = 16
RHS = 16
LEAF = 128
RANK = 64
LEAVES_DEV = 32
NREACH = 16
REACH = 6
DEVICES = 128
TOP = 7
SHARED = 6
SLOTS = 3
SUMMIT_ROW = 124
NOTHING = 7
ANCHORS = 8
FORMED = (-6, -5, 5, 6)
LOCAL = 62
MATRICES = LOCAL + 13

bf16 = jnp.bfloat16
f32 = jnp.float32
SCALE = math.log2(math.e) / math.sqrt(3.0)
LN2 = math.log(2.0)
TINY = 1e-30

COLUMN = [0, 2048, 3072, 3584, 3840, 3968]
ROW = [0, 32, 48, 56, 60]
RIM = [0, 384, 768, 1152, 1408, 1536]
RIM_WIDTH = 1664
LOW_PIECES = [(0, 384), (2048, 2432), (3072, 3456), (3584, 4096)]
HIGH_PIECES = [(1664, 2048), (2688, 3072), (3200, 4096)]
VMEM_LIMIT = 60 * 2**20
VMEM = pl.BlockSpec(memory_space=pltpu.VMEM)
SMEM = pl.BlockSpec(memory_space=pltpu.SMEM)
HBM = pl.BlockSpec(memory_space=pltpu.HBM)


def relevant(first, second, level):
    return 2 <= abs((first >> level) - (second >> level)) <= REACH


def slot_tables():
    sent = np.full((DEVICES, SLOTS, DEVICES), NOTHING, np.int32)
    held = np.zeros((DEVICES, SHARED + 1, DEVICES), np.int32)
    for first in range(DEVICES):
        for second in range(DEVICES):
            levels = [level for level in range(SHARED) if relevant(first, second, level)]
            if levels and levels[0] == 0:
                if len(levels) == 3:
                    levels.pop()
                    held[first, 2, second] = 4 + FORMED.index(second - first)
                levels.append(ANCHORS)
            for slot, level in enumerate(levels):
                sent[first, slot, second] = level
                held[first, SHARED if level == ANCHORS else level, second] = slot
    return np.concatenate([sent, held], axis=1)


TABLE = SLOTS + SHARED + 1


def started(semaphores, *pairs):
    copies = []
    for index, (source, target) in enumerate(pairs):
        copy = pltpu.make_async_copy(source, target, semaphores.at[index])
        copy.start()
        copies.append(copy)
    return copies


def split(x):
    high = x.astype(bf16)
    return high, (x - high.astype(f32)).astype(bf16)


def lanes(*parts):
    return jnp.concatenate(parts, axis=1)


def rows(*parts):
    return jnp.concatenate(parts, axis=0)


def dot(a, b):
    return jnp.dot(a, b, preferred_element_type=f32)


def dot_nt(a, b):
    return lax.dot_general(a, b, (((1,), (1,)), ((), ())), preferred_element_type=f32)


def narrow(x):
    high, low = split(x)
    return rows(lanes(high, high), lanes(low, low))


def folded(x):
    return x[:16] + x[16:]


def sides(x):
    x = x * SCALE
    high = x.astype(bf16).astype(f32)
    low = (x - high).astype(bf16).astype(f32)
    norm = jnp.sum(high * (high + 2.0 * low), axis=0, keepdims=True)
    norm_high = norm.astype(bf16).astype(f32)
    norm_middle = (norm - norm_high).astype(bf16).astype(f32)
    norm_low = norm - norm_high - norm_middle
    row = lax.broadcasted_iota(jnp.int32, x.shape, 0)
    parts = jnp.where(row % 3 == 0, norm_high, jnp.where(row % 3 == 1, norm_middle, norm_low))
    return high, low, parts, row


def source_side(x):
    high, low, parts, row = sides(x)
    tail = jnp.where(row < 3, 1.0, jnp.where(row < 6, parts, 0.0))
    return rows(high, high, low, tail)


def target_sides(x):
    high, low, parts, row = sides(x)
    tail = jnp.where(row < 3, parts, jnp.where(row < 6, 1.0, 0.0))
    factors = rows(-2.0 * high, -2.0 * low, -2.0 * high, tail)
    first = rows(factors, jnp.zeros_like(factors)).T
    return first.astype(bf16), pltpu.roll(first, RANK, 1).astype(bf16)


def matern(squared):
    squared = jnp.maximum(squared, TINY)
    distance = squared * lax.rsqrt(squared)
    return (1.0 + LN2 * distance) * jnp.exp2(-distance)


def pick(parts):
    lane = lax.broadcasted_iota(jnp.int32, parts[0].shape, 1)
    result = parts[3]
    for j in (2, 1, 0):
        result = jnp.where(lane < 32 * (j + 1), parts[j], result)
    return result


def interact(targets, sources, weights):
    kernel = matern(dot(targets, sources))
    high, low = split(kernel)
    size = kernel.shape[0]
    result = dot(rows(high, low), weights)
    quarter = size // 4
    return pick(
        [
            result[quarter * j : quarter * (j + 1)]
            + result[size + quarter * j : size + quarter * (j + 1)]
            for j in range(4)
        ]
    )


def weight_turns(slabs):
    parts = []
    for slab in slabs:
        high = slab.astype(bf16).astype(f32)
        parts += [high, slab - high]
    columns = rows(*parts).T
    return [
        (columns if turn == 0 else pltpu.roll(columns, 32 * turn, 1)).astype(bf16)
        for turn in range(4)
    ]


def halves(first, second):
    lane = lax.broadcasted_iota(jnp.int32, first.shape, 1)
    return jnp.where(lane < RANK, first, second)


def regrouped(load, staged, count, width):
    for c in range(count):
        value = load(c)
        for i in range(width):
            staged[8 * i + c : 8 * i + c + 1, :] = value[:, 128 * i : 128 * (i + 1)]


def tile(staged, c, width):
    return staged[pl.ds(c, width, stride=8), :]


def store_matrix(staged, c, matrices, index):
    value = tile(staged, c, 32)
    matrices[pl.ds(RANK * index, 32, stride=2), :] = value[:, :RANK]
    matrices[pl.ds(RANK * index + 1, 32, stride=2), :] = value[:, RANK:]


def eight_anchors(tiles):
    group = lax.broadcasted_iota(jnp.int32, (8, 128), 1) // 16
    for bit in (1, 2, 4):
        turned = list(tiles)
        for p in range(8):
            if p & bit == 0:
                first, second = tiles[p], tiles[p | bit]
                turned[p] = jnp.where(group & bit == 0, first, pltpu.roll(second, 16 * bit, 1))
                turned[p | bit] = jnp.where(
                    group & bit == 0, pltpu.roll(first, 128 - 16 * bit, 1), second
                )
        tiles = turned
    held = rows(*tiles).T
    slabs = [lanes(held[32 * q : 32 * q + 16], held[32 * q + 16 : 32 * q + 32]) for q in range(4)]
    value = rows(*slabs)
    high = value.astype(bf16)
    rest = value - high.astype(f32)
    middle = rest.astype(bf16)
    low = (rest - middle.astype(f32)).astype(bf16)
    row = lax.broadcasted_iota(jnp.int32, (128, 128), 0)
    column = lax.broadcasted_iota(jnp.int32, (128, 128), 1)
    order = (row & RANK) + 8 * (row & 7) + ((row & 63) >> 3)
    order = jnp.where(order == column, 1.0, 0.0).astype(bf16)
    value = dot(rows(high, middle, low), order)
    value = value[:64] + (value[64:128] + value[128:])
    return [value[16 * q : 16 * (q + 1)] for q in range(4)]


def lifted(slab, matrices):
    high, low = split(matrices)
    return folded(dot(narrow(slab), rows(high, low)))


def as_block(value):
    return lanes(value[:8], value[8:])


def moments_kernel(
    device,
    tables_hbm,
    basis_hbm,
    charges_hbm,
    transfer_hbm,
    anchors_hbm,
    top_hbm,
    moments_out,
    anchors_out,
    inner_out,
    outer_out,
    third,
    summit,
    outgoing_out,
    matrices_out,
    tables,
    basis,
    charges,
    transfer,
    anchor_rows,
    top_transfer,
    moments,
    anchors,
    inner,
    outer,
    outgoing,
    matrices,
    blocks,
    staged,
    staged_anchors,
    semaphores,
):
    me = device[0]
    quarters = [slice(1024 * i, 1024 * (i + 1)) for i in range(4)]
    loads = started(
        semaphores,
        (charges_hbm, charges),
        *[(basis_hbm.at[:, part], basis.at[:, part]) for part in quarters],
        (transfer_hbm, transfer),
        (anchors_hbm, anchor_rows),
        (tables_hbm.at[me], tables),
    )
    chain = [2 * DEVICES - (2 * DEVICES >> level) + (me >> level) for level in range(TOP)]
    chain += [252, 253]
    for shift in FORMED:
        other = jnp.minimum(jnp.maximum(me + shift, 0), DEVICES - 1)
        chain.append(DEVICES + (other >> 1))
    chain_loads = started(
        semaphores.at[18:],
        *[
            (top_hbm.at[pl.ds(row, 1), :], top_transfer.at[pl.ds(index, 1), :])
            for index, row in enumerate(chain)
        ],
    )
    loads[0].wait()

    def two_leaves(q, carry):
        parts = []
        for leaf in range(2):
            columns = pl.ds(pl.multiple_of(q * 256 + leaf * 128, 128), 128)
            high, low = split(basis[:, columns])
            parts.append(folded(dot_nt(narrow(charges[:, columns]), lanes(high, low))))
        moments[:, pl.ds(pl.multiple_of(q * 128, 128), 128)] = lanes(*parts)
        return carry

    for part in range(4):
        loads[1 + part].wait()
    lax.fori_loop(0, LEAVES_DEV // 2, two_leaves, 0, unroll=16)

    loads[5].wait()
    for group in range(8):
        count = min(8, LOCAL - 8 * group)
        for i in range(32):
            staged[group % 2, 8 * i : 8 * i + count, :] = transfer[
                8 * group : 8 * group + count, 128 * i : 128 * (i + 1)
            ]
        for c in range(count):
            store_matrix(staged.at[group % 2], c, matrices, 8 * group + c)
    for copy in chain_loads:
        copy.wait()
    for group in range(2):
        count = min(8, 13 - 8 * group)
        for i in range(32):
            staged[group, 8 * i : 8 * i + count, :] = top_transfer[
                8 * group : 8 * group + count, 128 * i : 128 * (i + 1)
            ]
        for c in range(count):
            store_matrix(staged.at[group], c, matrices, LOCAL + 8 * group + c)
    stores = started(semaphores.at[9:], (matrices, matrices_out))

    loads[6].wait()
    for group in range(8):
        count = min(8, 63 - 8 * group)
        for i in range(8):
            staged_anchors[group % 2, 8 * i : 8 * i + count, :] = anchor_rows[
                8 * group : 8 * group + count, 128 * i : 128 * (i + 1)
            ]
        tiles = [tile(staged_anchors.at[group % 2], c, 8) for c in range(count)]
        tiles += [jnp.zeros((8, 128), f32)] * (8 - count)
        for q, slab in enumerate(eight_anchors(tiles)):
            anchors[:, 512 * group + 128 * q : 512 * group + 128 * (q + 1)] = slab

    for height in range(5):
        number = LEAVES_DEV >> height
        parents = []
        for q in range(number // 2):
            start = (ROW[height] + 2 * q) * RANK
            slab = moments[:, COLUMN[height] + 128 * q : COLUMN[height] + 128 * (q + 1)]
            parents.append(lifted(slab, matrices[start : start + 128, :]))
        if height == 4:
            parents.append(jnp.zeros((16, RANK), f32))
        for q in range(len(parents) // 2):
            start = COLUMN[height + 1] + 128 * q
            moments[:, start : start + 128] = lanes(parents[2 * q], parents[2 * q + 1])

    even = (me & 1) == 0

    def fill(low_rim, high_rim):
        for row, value in ((slice(0, DIM), anchors), (slice(DIM, 2 * DIM), moments)):
            for rim, parts in ((low_rim, LOW_PIECES), (high_rim, HIGH_PIECES)):
                start = 0
                for first, last in parts:
                    rim[row, start : start + last - first] = value[:, first:last]
                    start += last - first

    @pl.when(even)
    def _():
        fill(outer, inner)

    @pl.when(jnp.logical_not(even))
    def _():
        fill(inner, outer)

    third[:DIM, :] = anchors[:, 3840:3968]
    third[DIM:, :] = moments[:, 3840:3968]
    stores += started(
        semaphores.at[10:],
        (inner, inner_out),
        (outer, outer_out),
        (moments, moments_out),
        (anchors, anchors_out),
    )

    value = moments[:, COLUMN[5] : COLUMN[5] + RANK]
    for level in range(SHARED + 1):
        blocks[level] = as_block(value)
        if level < SHARED:
            start = RANK * (LOCAL + level)
            value = lifted(value, matrices[start : start + RANK, :])
    blocks[NOTHING] = jnp.zeros((8, 128), f32)
    for half in range(2):
        summit[half] = jnp.where(me >> SHARED == half, blocks[SHARED], 0.0)
    blocks[ANCHORS] = as_block(anchors[:, COLUMN[5] : COLUMN[5] + RANK])

    def one_device(other, carry):
        for slot in range(SLOTS):
            outgoing[other, 8 * slot : 8 * (slot + 1), :] = blocks[tables[slot, other]]
        return carry

    loads[7].wait()
    for part in range(4):
        lax.fori_loop(32 * part, 32 * part + 32, one_device, 0, unroll=32)
        own = slice(32 * part, 32 * part + 32)
        stores += started(semaphores.at[14 + part :], (outgoing.at[own], outgoing_out.at[own]))
    for copy in stores:
        copy.wait()


def moments_call(*arguments):
    shape = jax.ShapeDtypeStruct
    return pl.pallas_call(
        moments_kernel,
        out_shape=(
            shape((16, 4096), f32),
            shape((16, 4096), f32),
            shape((32, RIM_WIDTH), f32),
            shape((32, RIM_WIDTH), f32),
            shape((32, 128), f32),
            shape((2, 8, 128), f32),
            shape((DEVICES, 8 * SLOTS, 128), f32),
            shape((MATRICES * RANK, RANK), f32),
        ),
        in_specs=[SMEM] + [HBM] * 6,
        out_specs=(HBM, HBM, HBM, HBM, VMEM, VMEM, HBM, HBM),
        scratch_shapes=[
            pltpu.SMEM((TABLE, 128), jnp.int32),
            pltpu.VMEM((RANK, 4096), f32),
            pltpu.VMEM((RHS, 4096), f32),
            pltpu.VMEM((LOCAL, RANK * RANK), f32),
            pltpu.VMEM((63, RANK * DIM), f32),
            pltpu.VMEM((16, RANK * RANK), f32),
            pltpu.VMEM((RHS, 4096), f32),
            pltpu.VMEM((DIM, 4096), f32),
            pltpu.VMEM((32, RIM_WIDTH), f32),
            pltpu.VMEM((32, RIM_WIDTH), f32),
            pltpu.VMEM((DEVICES, 8 * SLOTS, 128), f32),
            pltpu.VMEM((MATRICES * RANK, RANK), f32),
            pltpu.VMEM((9, 8, 128), f32),
            pltpu.VMEM((2, 256, 128), f32),
            pltpu.VMEM((2, 64, 128), f32),
            pltpu.SemaphoreType.DMA((31,)),
        ],
        compiler_params=pltpu.CompilerParams(vmem_limit_bytes=VMEM_LIMIT),
        cost_estimate=pl.CostEstimate(flops=10**9, bytes_accessed=2**22, transcendentals=0),
        name="moments",
    )(*arguments)


def near_kernel(
    device,
    near_blocks,
    points_hbm,
    charges_hbm,
    inner_hbm,
    outer_hbm,
    out_hbm,
    points,
    charges,
    inner,
    outer,
    out,
    factors,
    weights,
    semaphores,
):
    me = device[0]
    loads = started(
        semaphores,
        (points_hbm, points),
        (charges_hbm, charges),
        (inner_hbm, inner),
        (outer_hbm, outer),
    )

    def prepare(point_ref, charge_ref, charge_row, first):
        def four_leaves(i, carry):
            columns = pl.ds(pl.multiple_of(i * 512, 512), 512)
            side = source_side(point_ref[:DIM, columns]).astype(bf16)
            charge = charge_ref[charge_row : charge_row + RHS, columns]
            slabs = []
            for m in range(4):
                factors[(first + i) * 4 + m] = side[:, 128 * m : 128 * (m + 1)]
                slabs.append(charge[:, 128 * m : 128 * (m + 1)])
            for turn, value in enumerate(weight_turns(slabs)):
                weights[turn, first + i] = value
            return carry

        return four_leaves

    loads[0].wait()
    loads[1].wait()
    lax.fori_loop(0, 8, prepare(points, charges, 0, 4), 0, unroll=8)
    side = (me & 1) * 12
    loads[2].wait()
    lax.fori_loop(0, 4, prepare(inner, inner, DIM, 12 - side), 0, unroll=4)
    loads[3].wait()
    lax.fori_loop(0, 4, prepare(outer, outer, DIM, side), 0, unroll=4)
    factors[64] = jnp.zeros((64, 128), bf16)
    for turn in range(4):
        weights[turn, 16] = jnp.zeros((128, 128), bf16)
    first_leaf = me * LEAVES_DEV - NREACH

    def one_leaf(t, carry):
        columns = pl.ds(pl.multiple_of(t * 128, 128), 128)
        front, back = target_sides(points[:, columns])
        empty = jnp.zeros_like(front)
        targets = rows(
            lanes(front, empty), lanes(back, empty), lanes(empty, front), lanes(empty, back)
        )
        located = []
        for j in range(8):
            block = near_blocks[j, t]
            inside = jnp.minimum(jnp.maximum(block - first_leaf, 0), 63)
            located.append(jnp.where(block < 0, 64, inside))
        sources = rows(
            *[lanes(factors[located[2 * j]], factors[located[2 * j + 1]]) for j in range(4)]
        )
        weight = rows(
            *[
                pick([weights[(j - located[2 * j + h]) & 3, located[2 * j + h] >> 2] for j in range(4)])
                for h in range(2)
            ]
        )
        total = interact(targets, sources, weight).T
        out[:, columns] = sum(total[16 * g : 16 * (g + 1)] for g in range(8))
        return carry

    stores = []
    for part in range(2):
        lax.fori_loop(16 * part, 16 * part + 16, one_leaf, 0, unroll=16)
        own = slice(2048 * part, 2048 * part + 2048)
        stores += started(semaphores.at[4 + part :], (out.at[:, own], out_hbm.at[:, own]))
    for copy in stores:
        copy.wait()


def near_call(*arguments):
    return pl.pallas_call(
        near_kernel,
        out_shape=jax.ShapeDtypeStruct((RHS, LEAVES_DEV * LEAF), f32),
        in_specs=[SMEM, SMEM] + [HBM] * 4,
        out_specs=HBM,
        scratch_shapes=[
            pltpu.VMEM((DIM, LEAVES_DEV * LEAF), f32),
            pltpu.VMEM((RHS, LEAVES_DEV * LEAF), f32),
            pltpu.VMEM((DIM + RHS, NREACH * LEAF), f32),
            pltpu.VMEM((DIM + RHS, NREACH * LEAF), f32),
            pltpu.VMEM((RHS, LEAVES_DEV * LEAF), f32),
            pltpu.VMEM((65, 64, 128), bf16),
            pltpu.VMEM((4, 17, 128, 128), bf16),
            pltpu.SemaphoreType.DMA((6,)),
        ],
        compiler_params=pltpu.CompilerParams(vmem_limit_bytes=VMEM_LIMIT),
        cost_estimate=pl.CostEstimate(flops=10**10, bytes_accessed=2**22, transcendentals=0),
        name="near",
    )(*arguments)


def prepare_factors(anchors, factors, groups):
    def four_slabs(i, carry):
        side = source_side(anchors[:, pl.ds(pl.multiple_of(i * 512, 512), 512)])
        for m in range(4):
            slab = side[:, 128 * m : 128 * (m + 1)]
            turned = pltpu.roll(slab, RANK, 1)
            factors[(i * 4 + m) * 2] = halves(slab, turned).astype(bf16)
            factors[(i * 4 + m) * 2 + 1] = halves(turned, slab).astype(bf16)
        return carry

    lax.fori_loop(0, groups, four_slabs, 0, unroll=True)


def prepare_weights(moments, weights, groups):
    def four_slabs(i, carry):
        value = moments[:, pl.ds(pl.multiple_of(i * 512, 512), 512)]
        turns = weight_turns([value[:, 128 * m : 128 * (m + 1)] for m in range(4)])
        for turn in range(4):
            weights[turn, i, 0] = turns[turn][:RANK]
            weights[turn, i, 1] = turns[turn][RANK:]
        return carry

    lax.fori_loop(0, groups, four_slabs, 0, unroll=True)


def two_targets(anchors):
    front, back = target_sides(anchors)
    empty = jnp.zeros((RANK, 128), bf16)
    return rows(
        lanes(front[:RANK], empty),
        lanes(back[:RANK], empty),
        lanes(empty, front[RANK:]),
        lanes(empty, back[RANK:]),
    )


def four_sources(factors, located):
    return lanes(
        halves(factors[located[0]], factors[located[1]]),
        halves(factors[located[2]], factors[located[3]]),
    )


def placed(weights, index, slot):
    pair = index >> 1
    return weights[(slot - pair) & 3, pair >> 2, index & 1]


def two_clusters(anchors, factors, weights, located):
    sources = rows(*[four_sources(factors, located[4 * slot : 4 * slot + 4]) for slot in range(4)])
    weight = rows(
        *[pick([placed(weights, located[4 * slot + m], slot) for slot in range(4)]) for m in range(4)]
    )
    return cluster_sums(interact(two_targets(anchors), sources, weight))


def cluster_sums(total):
    total = total.T
    return lanes(
        total[:16] + total[16:32] + total[32:48] + total[48:64],
        total[64:80] + total[80:96] + total[96:112] + total[112:],
    )


def locate(entry, first, last, base, empty):
    inside = jnp.minimum(jnp.maximum(entry - first, 0), last)
    return jnp.where(entry < 0, empty, base + inside)


FINE_BASE = [0, 44, 72]
FINE_EMPTY = 92


def fine_kernel(
    device,
    lists,
    anchors_hbm,
    moments_hbm,
    inner_hbm,
    outer_hbm,
    far_hbm,
    anchors,
    moments,
    inner,
    outer,
    far,
    held_anchors,
    held_moments,
    factors,
    weights,
    semaphores,
):
    me = device[0]
    loads = started(
        semaphores,
        (anchors_hbm, anchors),
        (moments_hbm, moments),
        (inner_hbm, inner),
        (outer_hbm, outer),
    )
    for copy in loads:
        copy.wait()
    odd = (me & 1) == 1
    start = 0
    for height in range(3):
        width = (LEAVES_DEV >> height) * RANK
        wide = REACH * RANK
        rim = slice(RIM[height], RIM[height] + wide)
        own = slice(COLUMN[height], COLUMN[height] + width)
        far_end = start + wide + width
        for held, whole, row in (
            (held_anchors, anchors, slice(0, DIM)),
            (held_moments, moments, slice(DIM, 2 * DIM)),
        ):
            held[:, start + wide : far_end] = whole[:, own]
            inner_at = pl.multiple_of(jnp.where(odd, start, far_end), 128)
            outer_at = pl.multiple_of(jnp.where(odd, far_end, start), 128)
            held[:, pl.ds(inner_at, wide)] = inner[row, rim]
            held[:, pl.ds(outer_at, wide)] = outer[row, rim]
        start = far_end + wide
    held_anchors[:, start:] = jnp.zeros((DIM, 48 * 128 - start), f32)
    held_moments[:, start:] = jnp.zeros((DIM, 48 * 128 - start), f32)
    prepare_factors(held_anchors, factors, 12)
    prepare_weights(held_moments, weights, 12)

    for height in range(3):
        number = LEAVES_DEV >> height

        def one_pair(q, carry, height=height, number=number):
            first = me * number - REACH
            located = []
            for cluster in range(2):
                for j in range(8):
                    entry = lists[j, 2 * LEAVES_DEV - 2 * number + 2 * q + cluster]
                    located.append(
                        locate(entry, first, number + 2 * REACH - 1, FINE_BASE[height], FINE_EMPTY)
                    )
            columns = pl.ds(pl.multiple_of(COLUMN[height] + q * 128, 128), 128)
            far[:, columns] = two_clusters(anchors[:, columns], factors, weights, located)
            return carry

        lax.fori_loop(0, number // 2, one_pair, 0, unroll=True)
    for copy in started(semaphores, (far, far_hbm)):
        copy.wait()


def fine_call(*arguments):
    return pl.pallas_call(
        fine_kernel,
        out_shape=jax.ShapeDtypeStruct((RHS, 56 * RANK), f32),
        in_specs=[SMEM, SMEM] + [HBM] * 4,
        out_specs=HBM,
        scratch_shapes=[
            pltpu.VMEM((DIM, 4096), f32),
            pltpu.VMEM((RHS, 4096), f32),
            pltpu.VMEM((32, RIM_WIDTH), f32),
            pltpu.VMEM((32, 2048), f32),
            pltpu.VMEM((RHS, 56 * RANK), f32),
            pltpu.VMEM((DIM, 48 * 128), f32),
            pltpu.VMEM((RHS, 48 * 128), f32),
            pltpu.VMEM((96, 64, 128), bf16),
            pltpu.VMEM((4, 12, 2, 64, 128), bf16),
            pltpu.SemaphoreType.DMA((4,)),
        ],
        compiler_params=pltpu.CompilerParams(vmem_limit_bytes=VMEM_LIMIT),
        cost_estimate=pl.CostEstimate(flops=5 * 10**9, bytes_accessed=2**22, transcendentals=0),
        name="fine",
    )(*arguments)


COARSE_EMPTY = 30


def coarse_kernel(
    device,
    lists,
    top_lists,
    tables_hbm,
    anchors_hbm,
    moments_hbm,
    inner_hbm,
    outer_hbm,
    beyond_hbm,
    third_hbm,
    summit,
    top_hbm,
    incoming_hbm,
    matrices_hbm,
    far_hbm,
    basis_hbm,
    near_hbm,
    out_hbm,
    tables,
    anchors,
    moments,
    inner,
    outer,
    beyond,
    third,
    top_anchors,
    incoming,
    matrices,
    far,
    basis,
    near,
    out,
    held_anchors,
    held_moments,
    factors,
    weights,
    expansion,
    staged,
    formed,
    semaphores,
):
    me = device[0]
    loads = started(
        semaphores,
        (anchors_hbm, anchors),
        (moments_hbm, moments),
        (inner_hbm.at[:, 1152:], inner),
        (outer_hbm.at[:, 1152:], outer),
        (beyond_hbm, beyond),
        (third_hbm, third),
        (top_hbm, top_anchors),
        (tables_hbm.at[me], tables),
        (incoming_hbm, incoming),
        (matrices_hbm, matrices),
        (far_hbm, far),
        (basis_hbm, basis),
        (near_hbm, near),
    )
    for copy in loads[:6]:
        copy.wait()
    odd = (me & 1) == 1

    def at(column):
        return slice(column, column + 128)

    def place(on_inner, source, column, low_place, high_place):
        below = odd if on_inner else jnp.logical_not(odd)
        target = pl.multiple_of(jnp.where(below, low_place, high_place) * 128, 128)
        held_anchors[:, pl.ds(target, 128)] = source[:DIM, column]
        held_moments[:, pl.ds(target, 128)] = source[DIM:, column]

    def nearest(on_inner, column):
        below = odd if on_inner else jnp.logical_not(odd)
        return pl.ds(pl.multiple_of(column + jnp.where(below, 128, 0), 128), 128)

    for on_inner, source in ((True, inner), (False, outer)):
        place(on_inner, source, at(0), 1, 5)
        place(on_inner, source, at(128), 2, 6)
        place(on_inner, source, at(256), 10, 12)
    place(False, outer, nearest(False, 512), 0, 7)
    place(False, outer, at(768), 9, 13)
    place(False, third, at(0), 8, 14)
    place(True, beyond, nearest(True, 0), 0, 7)
    place(True, beyond, at(256), 9, 13)
    place(True, beyond, at(768), 8, 14)
    for index, column in ((3, 3584), (4, 3712), (11, 3840)):
        held_anchors[:, at(128 * index)] = anchors[:, at(column)]
        held_moments[:, at(128 * index)] = moments[:, at(column)]
    held_anchors[:, at(128 * 15)] = jnp.zeros((DIM, 128), f32)
    held_moments[:, at(128 * 15)] = jnp.zeros((RHS, 128), f32)
    prepare_factors(held_anchors, factors, 4)
    prepare_weights(held_moments, weights, 4)

    def local_pair(height, q, base):
        number = LEAVES_DEV >> height
        located = []
        for cluster in range(2):
            for j in range(8):
                entry = lists[j, 2 * LEAVES_DEV - 2 * number + 2 * q + cluster]
                located.append(
                    locate(entry, me * number - REACH, number + 2 * REACH - 1, base, COARSE_EMPTY)
                )
        return two_clusters(
            anchors[:, at(COLUMN[height] + 128 * q)], factors, weights, located
        )

    far_third = [local_pair(3, q, 0) for q in range(2)]
    far_fourth = local_pair(4, 0, 16)

    entries = [[lists[j, 62] for j in range(8)]]
    for level in range(1, TOP + 1):
        row = DEVICES - (DEVICES >> (level - 1)) + (me >> level)
        entries.append([top_lists[j, row] for j in range(8)])

    wanted = [0] + [DEVICES - (DEVICES >> (level - 1)) + (me >> level) for level in range(1, TOP + 1)]
    for level in range(1, TOP + 1):
        first = DEVICES - (DEVICES >> (level - 1))
        wanted += [first + jnp.maximum(entry, 0) for entry in entries[level]]
    columns = []
    loads[6].wait()
    for group in range(8):
        part = wanted[8 * group : 8 * group + 8]
        regrouped(lambda c: top_anchors[pl.ds(part[c], 1), :], staged.at[group % 2], 8, 8)
        columns += eight_anchors([tile(staged.at[group % 2], c, 8) for c in range(8)])

    loads[8].wait()
    loads[9].wait()
    loads[7].wait()

    lane = lax.broadcasted_iota(jnp.int32, (8, 128), 1)

    def two_blocks(first, second):
        return rows(
            jnp.where(lane < RANK, first, pltpu.roll(second, RANK, 1)),
            jnp.where(lane < RANK, pltpu.roll(first, RANK, 1), second),
        )

    sixth = [summit[0], summit[1]]
    seventh = lifted(two_blocks(*sixth), matrices[RANK * (LOCAL + 7) : RANK * (LOCAL + 9), :])
    seventh = as_block(seventh)

    def held(kind, other):
        slot = tables[SLOTS + kind, other]
        place = jnp.minimum(slot, SLOTS - 1)
        return slot, incoming[other, pl.ds(pl.multiple_of(place * 8, 8), 8), :]

    for index, shift in enumerate(FORMED):
        other = jnp.minimum(jnp.maximum(me + shift, 0), DEVICES - 1)
        value = two_blocks(held(1, other)[1], jnp.zeros((8, 128), f32))[:, :RANK]
        start = RANK * (LOCAL + 9 + index)
        formed[index] = as_block(lifted(value, matrices[start : start + RANK, :]))

    def block(level, entry):
        if level == TOP:
            return jnp.where(entry == 0, seventh, 0.0)
        if level == SHARED:
            return jnp.where(entry == 0, sixth[0], jnp.where(entry == 1, sixth[1], 0.0))
        first = jnp.maximum(entry, 0) << level

        def add(i, total):
            for step in range(min(8, 1 << level)):
                slot, value = held(level, first + min(8, 1 << level) * i + step)
                if level == 2:
                    value = jnp.where(slot < SLOTS, value, formed[slot & 3])
                total = total + value
            return total

        nothing = jnp.zeros((8, 128), f32)
        if level <= 4:
            total = nothing
            for i in range(max(1, (1 << level) // 8)):
                total = add(i, total)
            return jnp.where(entry < 0, nothing, total)
        return lax.fori_loop(0, jnp.where(entry < 0, 0, 1 << (level - 3)), add, nothing)

    found_pairs = []
    for level in range(TOP + 1):
        sums = [block(level, entry) for entry in entries[level]]
        found_pairs += [two_blocks(sums[2 * j], sums[2 * j + 1]) for j in range(4)]

    far_chain = []
    for unit in range(4):
        pairs = found_pairs[8 * unit : 8 * unit + 8]
        weight = []
        for h in range(2):
            parts = []
            for slot in range(4):
                high = pairs[2 * slot + h].astype(bf16).astype(f32)
                parts += [high, pairs[2 * slot + h] - high]
            weight.append(rows(*parts).T.astype(bf16))
        own = columns[unit]
        sources = []
        for level in (2 * unit, 2 * unit + 1):
            for h in range(2):
                if level == 0:
                    found = [
                        held(SHARED, jnp.maximum(entry, 0))[1] for entry in entries[0][4 * h : 4 * h + 4]
                    ]
                    pair = lanes(two_blocks(found[0], found[1]), two_blocks(found[2], found[3]))
                else:
                    pair = lanes(*columns[4 * level + 2 * h : 4 * level + 2 * h + 2])
                sources.append(source_side(pair).astype(bf16))
        if unit == 0:
            own = halves(anchors[:, at(COLUMN[5])], own)
        result = cluster_sums(interact(two_targets(own), rows(*sources), rows(*weight)))
        far_chain += [result[:, :RANK], result[:, RANK:]]

    def pushed(value, matrix):
        high, low = split(matrix)
        return folded(dot_nt(narrow(value), lanes(high, low)))

    value = far_chain[TOP]
    for level in range(TOP - 1, -1, -1):
        value = far_chain[level] + pushed(value, matrices[RANK * (LOCAL + level) : RANK * (LOCAL + level + 1), :])

    def children(parent, height, q):
        start = (ROW[height] + 2 * q) * RANK
        return pushed(parent, matrices[start : start + 128, :])

    loads[10].wait()
    upper = [far_fourth + children(value, 4, 0)]
    for height in (3, 2, 1, 0):
        lower = []
        for q, slab in enumerate(upper):
            for side in range(2):
                parent = slab[:, RANK * side : RANK * (side + 1)]
                index = 2 * q + side
                if height == 3:
                    own = far_third[index]
                else:
                    own = far[:, at(COLUMN[height] + 128 * index)]
                lower.append(own + children(parent, height, index))
        upper = lower
    for q, slab in enumerate(upper):
        expansion[:, at(128 * q)] = slab

    def two_leaves(q, carry):
        slab = expansion[:, pl.ds(pl.multiple_of(q * 128, 128), 128)]
        for leaf in range(2):
            columns = pl.ds(pl.multiple_of(q * 256 + leaf * 128, 128), 128)
            high, low = split(basis[:, columns])
            own = slab[:, RANK * leaf : RANK * (leaf + 1)]
            out[:, columns] = near[:, columns] + folded(dot(narrow(own), rows(high, low)))
        return carry

    loads[11].wait()
    loads[12].wait()
    stores = []
    for part in range(2):
        lax.fori_loop(8 * part, 8 * part + 8, two_leaves, 0, unroll=8)
        own = slice(2048 * part, 2048 * part + 2048)
        stores += started(semaphores.at[13 + part :], (out.at[:, own], out_hbm.at[:, own]))
    for copy in stores:
        copy.wait()


def coarse_call(*arguments):
    return pl.pallas_call(
        coarse_kernel,
        out_shape=jax.ShapeDtypeStruct((RHS, LEAVES_DEV * LEAF), f32),
        in_specs=[SMEM] * 3 + [HBM] * 7 + [VMEM] + [HBM] * 6,
        out_specs=HBM,
        scratch_shapes=[
            pltpu.SMEM((TABLE, 128), jnp.int32),
            pltpu.VMEM((DIM, 4096), f32),
            pltpu.VMEM((RHS, 4096), f32),
            pltpu.VMEM((32, 512), f32),
            pltpu.VMEM((32, 896), f32),
            pltpu.VMEM((32, 896), f32),
            pltpu.VMEM((32, 128), f32),
            pltpu.VMEM((127, RANK * DIM), f32),
            pltpu.VMEM((DEVICES, 8 * SLOTS, 128), f32),
            pltpu.VMEM((MATRICES * RANK, RANK), f32),
            pltpu.VMEM((RHS, 56 * RANK), f32),
            pltpu.VMEM((RANK, 4096), f32),
            pltpu.VMEM((RHS, 4096), f32),
            pltpu.VMEM((RHS, 4096), f32),
            pltpu.VMEM((DIM, 16 * 128), f32),
            pltpu.VMEM((RHS, 16 * 128), f32),
            pltpu.VMEM((32, 64, 128), bf16),
            pltpu.VMEM((4, 4, 2, 64, 128), bf16),
            pltpu.VMEM((RHS, 2048), f32),
            pltpu.VMEM((2, 64, 128), f32),
            pltpu.VMEM((4, 8, 128), f32),
            pltpu.SemaphoreType.DMA((15,)),
        ],
        compiler_params=pltpu.CompilerParams(vmem_limit_bytes=VMEM_LIMIT),
        cost_estimate=pl.CostEstimate(flops=10**9, bytes_accessed=2**23, transcendentals=0),
        name="coarse",
    )(*arguments)


def exchanged(value, mate):
    pairs = []
    for device in range(DEVICES):
        other = mate(device)
        pairs.append((device, other if 0 <= other < DEVICES else device))
    return lax.ppermute(value, "leaf", pairs)


def inner_mate(device):
    return device + 1 if device % 2 == 0 else device - 1


def outer_mate(device):
    return device - 1 if device % 2 == 0 else device + 1


def third_mate(device):
    return device - 3 if device % 2 == 0 else device + 3


def on_device(
    points,
    charges,
    leaf_basis,
    local_transfer,
    local_anchors,
    local_lists,
    near_blocks,
    top_transfer,
    top_anchors,
    top_lists,
):
    index = lax.axis_index("leaf")
    device = index.reshape(1)
    half = NREACH * LEAF
    lower = (index & 1) * half

    def edge(start):
        return jnp.concatenate(
            [lax.dynamic_slice_in_dim(array, start, half, 1) for array in (points, charges)], axis=0
        )

    inner_edge, outer_edge, device = lax.optimization_barrier(
        (edge(half - lower), edge(lower), device)
    )
    inner_leaves = exchanged(inner_edge, inner_mate)
    outer_leaves = exchanged(outer_edge, outer_mate)

    tables = jnp.asarray(slot_tables())
    moments, anchors, inner_rim, outer_rim, third, summit, outgoing, matrices = moments_call(
        device, tables, leaf_basis, charges, local_transfer, local_anchors, top_transfer
    )
    outgoing, inner_leaves, outer_leaves = lax.optimization_barrier(
        (outgoing, inner_leaves, outer_leaves)
    )
    inner = exchanged(inner_rim, inner_mate)
    incoming = lax.all_to_all(outgoing, "leaf", 0, 0)
    summit = lax.cond(
        jnp.any(top_lists[SUMMIT_ROW:] >= 0),
        lambda value: lax.psum(value, "leaf"),
        lambda value: jnp.zeros_like(value),
        summit,
    )
    outer = exchanged(
        jnp.concatenate([outer_rim, inner[:, RIM[3] : RIM[5]]], axis=1), outer_mate
    )
    near = near_call(device, near_blocks.T, points, charges, inner_leaves, outer_leaves)
    near, third = lax.optimization_barrier((near, third))
    third = exchanged(third, third_mate)
    near, outer = lax.optimization_barrier((near, outer))
    beyond = exchanged(outer[:, RIM[3] :], inner_mate)
    local_lists = local_lists.T
    far = fine_call(device, local_lists, anchors, moments, inner, outer)
    return coarse_call(
        device,
        local_lists,
        top_lists.T,
        tables,
        anchors,
        moments,
        inner,
        outer,
        beyond,
        third,
        summit,
        top_anchors,
        incoming,
        matrices,
        far,
        leaf_basis,
        near,
    )


def solution(mesh):
    in_specs = (
        P(None, "leaf"),
        P(None, "leaf"),
        P(None, "leaf"),
        P("leaf", None),
        P("leaf", None),
        P("leaf", None),
        P("leaf", None),
        P(),
        P(),
        P(),
    )
    out_specs = P(None, "leaf")
    return jax.shard_map(
        on_device, mesh=mesh, in_specs=in_specs, out_specs=out_specs, check_vma=False
    )
```
